512 devices in a mesh: seq: 32 (over z, core), tensor: 4 (over x), dp: 4 (over y).
Axes of the slice: x: 4, y: 4, z: 16, core: 2. Of those that a mesh axis runs over, the one named last changes fastest.
Arguments:
- prefix: bfloat16 [4, 16384, 2048], P('dp', 'seq'), may hold values from -6 to 6
- key_weight: bfloat16 [2048, 2048], P('seq', 'tensor'), may hold values from -0.125 to 0.125
- value_weight: bfloat16 [2048, 2048], P('seq', 'tensor'), may hold values from -0.125 to 0.125
- query_weight: bfloat16 [2048, 2048], P('seq', 'tensor'), may hold values from -0.125 to 0.125
- queries: bfloat16 [4, 1024, 2048], P('dp', 'seq', 'tensor'), may hold values from -6 to 6
- out_grad: bfloat16 [4, 1024, 2048], P('dp', 'seq', 'tensor'), may hold values from -6 to 6
- attn_out: bfloat16 [4, 1024, 2048], P('dp', 'seq', 'tensor'), may hold values from -6 to 6
- shifted_lse: float32 [4, 1024, 16], P('dp', 'seq', 'tensor'), may hold values from 0 to 1
- latent_in: bfloat16 [4, 1024, 2048], P('dp', None, 'seq'), may hold values from -6 to 6
Outputs:
- key_grad: bfloat16 [4, 16384, 2048], P('dp', 'seq', 'tensor')
- value_grad: bfloat16 [4, 16384, 2048], P('dp', 'seq', 'tensor')
- latent_grad: bfloat16 [4, 1024, 2048], P('dp', 'tensor', 'seq')
- query_weight_grad: float32 [2048, 2048], P('seq', 'tensor')
The draws below stay inside these ranges and needn't reach their ends.
All inputs are finite; a program needn't handle non-finite values.
Results may differ from the reference program's by a relative error of at most 0.015.
The reference program's roundings to bfloat16 on the way count: a program that leaves them out, or rounds other values in their place, can miss the bound.
Values may be sent and summed in bfloat16 or wider, within the bound.
No kernel may reach another device: no remote copies, remote signals or barrier semaphores. Data moves between devices by JAX's collectives and lax.ppermute only.
A program may use at most 64 MiB of HBM per device.

```python
import math
import jax
import jax.numpy as jnp
from jax import lax

D = 2048
HEADS = 16
HEAD = 128
LATENTS = 1024
PREFIX = 16384
BATCH = 4


def block_scale(stream_key, extent, cuts, least, high):
    def one(axis_at, shards_of):
        steps = jax.random.uniform(jax.random.fold_in(jax.random.fold_in(stream_key, 6), axis_at), (shards_of,), jnp.float32, least / len(cuts), high / len(cuts))
        return jnp.repeat(jnp.exp(steps), extent[axis_at] // shards_of).reshape((-1,) + (1,) * (len(extent) - axis_at - 1))

    loudness = one(*cuts[0])
    for cut in cuts[1:]:
        loudness = loudness * one(*cut)
    return loudness


def bell_draw(key, extent, width, reach, cuts=(), kind=jnp.bfloat16):
    array = jax.random.normal(key, extent, jnp.float32) * width
    if len(cuts) > 0:
        array = block_scale(key, extent, cuts, -0.22, 0.18) * array
    return jnp.clip(array, min=-reach, max=reach).astype(kind)


def setup_inputs(seed: int = 0) -> dict:
    seeds = jax.random.split(jax.random.key(seed), 10)
    prefix = bell_draw(seeds[0], (BATCH, PREFIX, D), 1.0, 6.0, ((0, 4), (1, 32)))
    key_weight = bell_draw(seeds[1], (D, D), D ** -0.5, 0.125, ((0, 32), (1, 4)))
    value_weight = bell_draw(seeds[2], (D, D), D ** -0.5, 0.125, ((0, 32), (1, 4)))
    query_weight = bell_draw(seeds[3], (D, D), D ** -0.5, 0.125, ((0, 32), (1, 4)))
    queries = bell_draw(seeds[4], (BATCH, LATENTS, D), 1.0, 6.0, ((0, 4), (1, 32), (2, 4)))
    out_grad = bell_draw(seeds[5], (BATCH, LATENTS, D), 1.0, 6.0, ((0, 4), (1, 32), (2, 4)))
    attn_out = bell_draw(seeds[6], (BATCH, LATENTS, D), 1.0, 6.0, ((0, 4), (1, 32), (2, 4)))
    shifted_lse = jnp.clip(1.0 * jax.random.uniform(seeds[7], (BATCH, LATENTS, HEADS), jnp.float32) ** block_scale(seeds[7], (BATCH, LATENTS, HEADS), ((0, 4), (1, 32), (2, 4)), -0.2, 0.2), 0.0, 1.0)
    latent_in = bell_draw(seeds[8], (BATCH, LATENTS, D), 1.0, 6.0, ((0, 4), (2, 32)))
    return {"prefix": prefix, "key_weight": key_weight, "value_weight": value_weight, "query_weight": query_weight, "queries": queries, "out_grad": out_grad, "attn_out": attn_out, "shifted_lse": shifted_lse, "latent_in": latent_in}


def single_sequence(tokens_in, query_rows, grad_rows, output_rows, lse_rows, key_weight, value_weight):
    scaling = 1.0 / math.sqrt(HEAD)
    latent_factor = 1.0 / math.sqrt(LATENTS)
    prefix_factor = 1.0 / math.sqrt(PREFIX)
    key_rows = jnp.dot(tokens_in, key_weight, preferred_element_type=jnp.float32).astype(jnp.bfloat16)
    value_rows = jnp.dot(tokens_in, value_weight, preferred_element_type=jnp.float32).astype(jnp.bfloat16)

    def single_head(head_index):
        first = head_index * HEAD

        def column_slice(matrix):
            return lax.dynamic_slice_in_dim(matrix, first, HEAD, 1)
        query_head = column_slice(query_rows)
        grad_head = column_slice(grad_rows)
        key_head = column_slice(key_rows)
        value_head = column_slice(value_rows)
        row_delta = lax.optimization_barrier(jnp.sum(grad_head.astype(jnp.float32) * column_slice(output_rows).astype(jnp.float32), axis=1))
        lse_head = lax.dynamic_slice_in_dim(lse_rows, head_index, 1, 1)[:, 0]
        scores = jnp.dot(query_head, key_head.T, preferred_element_type=jnp.float32) * scaling
        weights = jnp.exp(scores - lse_head[:, None])
        grad_probs = jnp.dot(grad_head, value_head.T, preferred_element_type=jnp.float32)
        score_grad = weights * (grad_probs - row_delta[:, None])
        weight_bf = weights.astype(jnp.bfloat16)
        score_bf = score_grad.astype(jnp.bfloat16)
        value_grad = (jnp.dot(weight_bf.T, grad_head, preferred_element_type=jnp.float32) * latent_factor).astype(jnp.bfloat16)
        key_grad = (jnp.dot(score_bf.T, query_head, preferred_element_type=jnp.float32) * (scaling * latent_factor)).astype(jnp.bfloat16)
        query_grad = jnp.dot(score_bf, key_head, preferred_element_type=jnp.float32) * (scaling * prefix_factor)
        return (key_grad, value_grad, query_grad)
    key_grad, value_grad, query_grad = lax.map(single_head, jnp.arange(HEADS, dtype=jnp.int32))
    key_grad = jnp.transpose(key_grad, (1, 0, 2)).reshape(PREFIX, D)
    value_grad = jnp.transpose(value_grad, (1, 0, 2)).reshape(PREFIX, D)
    query_grad = jnp.transpose(query_grad, (1, 0, 2)).reshape(LATENTS, D)
    return (key_grad, value_grad, query_grad)

def reference(prefix, key_weight, value_weight, query_weight, queries, out_grad, attn_out, shifted_lse, latent_in):

    def per_sequence(packed):
        return single_sequence(packed[0], packed[1], packed[2], packed[3], packed[4], key_weight, value_weight)
    key_grad, value_grad, query_grad = lax.map(per_sequence, (prefix, queries, out_grad, attn_out, shifted_lse))
    query_bf = query_grad.astype(jnp.bfloat16)
    latent_grad = jnp.einsum('bik,ck->bic', query_bf.astype(jnp.float32), query_weight.astype(jnp.float32)).astype(jnp.bfloat16)
    weight_factor = 1.0 / math.sqrt(LATENTS * BATCH)
    weight_grad = jnp.dot(latent_in.reshape(BATCH * LATENTS, D).T, query_bf.reshape(BATCH * LATENTS, D), preferred_element_type=jnp.float32) * weight_factor
    return (key_grad, value_grad, latent_grad, weight_grad)
```

```python
import math

import jax
import jax.numpy as jnp
from jax import lax
from jax.experimental import pallas as pl
from jax.experimental.pallas import tpu as pltpu
from jax.sharding import Mesh, PartitionSpec as P

BF = jnp.bfloat16
F32 = jnp.float32
SEQ = ("zh", "zl", "core")
SWAP = [(0, 1), (1, 0)]


def dot(a, b):
    return jnp.dot(a, b, preferred_element_type=F32)


def dot_nt(a, b):
    return lax.dot_general(a, b, (((1,), (1,)), ((), ())), preferred_element_type=F32)


def project_kernel(own_ref, other_ref, weight_ref, out_ref):
    step = pl.program_id(0)
    half = pl.num_programs(0) // 2
    size = weight_ref.shape[2]

    def run(rows):
        for pair in range(2):
            weight = jnp.concatenate([weight_ref[2 * pair], weight_ref[2 * pair + 1]], axis=1)
            out_ref[:, 2 * pair * size : 2 * (pair + 1) * size] = dot(rows, weight).astype(BF)

    @pl.when(step < half)
    def _():
        run(own_ref[...])

    @pl.when(step >= half)
    def _():
        run(other_ref[...])


def project(own, other, weight):
    rows, width = own.shape
    slabs, _, size = weight.shape
    block = 256
    half = rows // block
    return pl.pallas_call(
        project_kernel,
        grid=(2 * half,),
        in_specs=[
            pl.BlockSpec((block, width), lambda t: (jnp.minimum(t, half - 1), 0)),
            pl.BlockSpec((block, width), lambda t: (jnp.maximum(t - half, 0), 0)),
            pl.BlockSpec((slabs, width, size), lambda t: (0, 0, 0)),
        ],
        out_specs=pl.BlockSpec((block, slabs * size), lambda t: (t, 0)),
        out_shape=jax.ShapeDtypeStruct((2 * rows, slabs * size), BF),
        compiler_params=pltpu.CompilerParams(vmem_limit_bytes=40 * 2**20),
        cost_estimate=pl.CostEstimate(
            flops=4 * rows * width * slabs * size, bytes_accessed=8 * 2**20, transcendentals=0
        ),
    )(own, other, weight)


def attend_kernel(
    core_ref, kv_ref, query_ref, grad_ref, stat_ref, own_ref, other_ref, part_ref, qt, gt, total,
    *, size, scaling, latent_factor, prefix_factor,
):
    step = pl.program_id(0)
    last = pl.num_programs(0) - 1
    half = pl.num_programs(0) // 2

    @pl.when(step == 0)
    def _():
        qt[...] = query_ref[...].T
        gt[...] = grad_ref[...].T
        total[...] = jnp.zeros_like(total)

    key_out, value_out = [], []
    for head in range(2):
        cols = slice(head * size, (head + 1) * size)
        keys = kv_ref[:, cols]
        values = kv_ref[:, (2 + head) * size : (3 + head) * size]
        scores = dot(keys, qt[cols, :]) * scaling
        weights = jnp.exp(scores - stat_ref[2 * head : 2 * head + 1, :])
        probs = dot(values, gt[cols, :])
        score_grad = (weights * (probs - stat_ref[2 * head + 1 : 2 * head + 2, :])).astype(BF)
        value_out.append(dot(weights.astype(BF), grad_ref[:, cols]) * latent_factor)
        key_out.append(dot(score_grad, query_ref[:, cols]) * (scaling * latent_factor))
        total[cols, :] += dot(keys.T, score_grad)
    result = jnp.concatenate(key_out + value_out, axis=1).astype(BF)

    @pl.when(step < half)
    def _():
        own_ref[...] = result

    @pl.when(step >= half)
    def _():
        other_ref[...] = result

    @pl.when(step == last)
    def _():
        count, _, width = part_ref.shape
        for i in range(count):
            part_ref[i] = (
                total[:, i * width : (i + 1) * width] * (scaling * prefix_factor)
            ).astype(BF)


def attend(core, kv, gathered, stats, groups, prefix_count):
    tokens, columns = kv.shape
    latents = gathered.shape[0]
    size = columns // 4
    block = 256
    half = tokens // block // 2
    kernel = lambda *refs: attend_kernel(
        *refs,
        size=size,
        scaling=1.0 / math.sqrt(size),
        latent_factor=1.0 / math.sqrt(latents),
        prefix_factor=1.0 / math.sqrt(prefix_count),
    )
    return pl.pallas_call(
        kernel,
        grid_spec=pltpu.PrefetchScalarGridSpec(
            num_scalar_prefetch=1,
            grid=(tokens // block,),
            in_specs=[
                pl.BlockSpec((block, columns), lambda t, c: (t, 0)),
                pl.BlockSpec((latents, 2 * size), lambda t, c: (0, c[0])),
                pl.BlockSpec((latents, 2 * size), lambda t, c: (0, c[0] + 2)),
                pl.BlockSpec(stats.shape, lambda t, c: (0, 0)),
            ],
            out_specs=[
                pl.BlockSpec((block, columns), lambda t, c: (jnp.minimum(t, half - 1), 0)),
                pl.BlockSpec((block, columns), lambda t, c: (jnp.maximum(t - half, 0), 0)),
                pl.BlockSpec((groups, 2 * size, latents // groups), lambda t, c: (0, 0, 0)),
            ],
            scratch_shapes=[
                pltpu.VMEM((2 * size, latents), BF),
                pltpu.VMEM((2 * size, latents), BF),
                pltpu.VMEM((2 * size, latents), F32),
            ],
        ),
        out_shape=[
            jax.ShapeDtypeStruct((tokens // 2, columns), BF),
            jax.ShapeDtypeStruct((tokens // 2, columns), BF),
            jax.ShapeDtypeStruct((groups, 2 * size, latents // groups), BF),
        ],
        compiler_params=pltpu.CompilerParams(vmem_limit_bytes=48 * 2**20),
        cost_estimate=pl.CostEstimate(
            flops=20 * tokens * latents * size,
            bytes_accessed=6 * 2**20,
            transcendentals=2 * tokens * latents,
        ),
    )(core, kv, gathered, gathered, stats)


def exchange(x, axes):
    return lax.all_to_all(x, axes, 0, 0, tiled=True)


def spread(x, axes):
    count = lax.axis_size(axes)
    return exchange(jnp.broadcast_to(x[None], (count,) + x.shape), axes)


def halves(x):
    return jnp.transpose(x.reshape(x.shape[0], 2, x.shape[1] // 2), (1, 0, 2))


def two_parts(x):
    high = lax.reduce_precision(x, 8, 7)
    return high.astype(BF), (x - high).astype(BF)


def local(
    prefix, key_weight, value_weight, query_weight, queries, out_grad, attn_out, shifted_lse, latent_in
):
    core = lax.axis_index("core")
    batch = lax.axis_index("dp")
    first = core == 0
    ranks = lax.axis_size(SEQ)
    batches = lax.axis_size("dp")
    tokens_in = prefix[0]
    token_count = tokens_in.shape[0]
    rows, columns = queries.shape[1:]
    heads = shifted_lse.shape[2]
    size = columns // heads
    latents = rows * ranks

    gathered = lax.all_gather(
        jnp.concatenate([queries[0], out_grad[0]], axis=1), SEQ, axis=0, tiled=True
    )
    other_tokens = lax.ppermute(tokens_in, "core", SWAP)
    latent_own = latent_in[0].T
    query_halves = halves(query_weight)
    query_mine = jnp.where(first, query_halves[0], query_halves[1])
    query_theirs = jnp.where(first, query_halves[1], query_halves[0])
    swapped = lax.ppermute(jnp.concatenate([latent_own, query_theirs], axis=1), "core", SWAP)
    latent_other, query_other = swapped[:, :latents], swapped[:, latents:]

    def in_order(own, other):
        return jnp.where(first, jnp.concatenate([own, other], 0), jnp.concatenate([other, own], 0))

    latent_both = in_order(latent_own, latent_other)
    query_both = in_order(query_mine, query_other)

    row_delta = jnp.sum(
        (out_grad[0].astype(F32) * attn_out[0].astype(F32)).reshape(rows, heads, size), axis=2
    )
    stats = jnp.stack([shifted_lse[0], row_delta]).reshape(2, rows, 2, heads // 2)
    high, low = two_parts(stats)
    packed = jnp.transpose(jnp.stack([high, low]), (3, 1, 0, 4, 2))
    packed = packed.reshape(2, 2, 2 * (heads // 2) * rows)
    packed = jnp.pad(packed, ((0, 0), (0, 14), (0, 0)))
    slabs = jnp.concatenate([halves(key_weight), halves(value_weight)], axis=2)
    slab = lax.dynamic_slice_in_dim(slabs, batch * size, size, 2)
    block = jnp.concatenate([slab, packed], axis=1)
    block = jnp.broadcast_to(block[None], (ranks // 2,) + block.shape).reshape((ranks,) + block.shape[1:])
    landed = exchange(block, SEQ)
    depth = key_weight.shape[0]
    weight = spread(landed[:, :depth].reshape(depth * ranks, size), "dp")
    stats_all = landed[:, depth : depth + 2].astype(F32).reshape(ranks, 2, 2, heads // 2, rows)
    stats_all = jnp.transpose(stats_all[:, :, 0] + stats_all[:, :, 1], (2, 1, 0, 3))
    stats_all = stats_all.reshape(heads, latents)

    kv = project(tokens_in, other_tokens, weight)
    groups = lax.axis_size("zl")
    own_grads, other_grads, part = attend(
        jnp.reshape(core, (1,)).astype(jnp.int32), kv, gathered, stats_all, groups, token_count * ranks
    )
    theirs = lax.ppermute(other_grads, "core", SWAP)
    half = columns // 2

    def whole(lo):
        mine, other = own_grads[:, lo : lo + half], theirs[:, lo : lo + half]
        return jnp.where(
            first, jnp.concatenate([mine, other], 1), jnp.concatenate([other, mine], 1)
        )[None]

    near = jnp.sum(exchange(part, "zl").astype(F32), axis=0).astype(BF)
    full = jnp.sum(spread(near, "zh").astype(F32), axis=0).astype(BF)
    every = lax.all_gather(full, "zl", axis=1, tiled=True)

    latent_part = dot(query_both, every).astype(BF)
    latent_part = latent_part.reshape(2, columns // 8, lax.axis_size("tensor"), -1)
    latent_part = jnp.transpose(latent_part, (0, 2, 1, 3)).reshape(-1, columns // 8, latents // 4)
    latent_sum = jnp.sum(exchange(latent_part, ("core", "tensor")).astype(F32), axis=0)
    latent_grad = latent_sum.astype(BF).T[None]

    weight_part = dot_nt(latent_both, every).astype(BF)
    weight_part = weight_part.reshape(2, 1, columns // 8, half)
    weight_part = jnp.broadcast_to(weight_part, (2, batches, columns // 8, half))
    weight_sum = exchange(weight_part.reshape(-1, columns // 8, half), ("core", "dp"))
    weight_sum = jnp.sum(weight_sum.reshape(2, batches, columns // 8, half).astype(F32), axis=1)
    weight_factor = 1.0 / math.sqrt(latents * batches)
    weight_grad = jnp.transpose(weight_sum, (1, 0, 2)).reshape(columns // 8, columns) * weight_factor
    return (whole(0), whole(half), latent_grad, weight_grad)


def solution(mesh):
    fine = Mesh(
        mesh.devices.reshape(4, 4, 2, *mesh.devices.shape[1:]), SEQ + tuple(mesh.axis_names[1:])
    )
    return jax.shard_map(
        local,
        mesh=fine,
        in_specs=(
            P("dp", SEQ, None),
            P(SEQ, "tensor"),
            P(SEQ, "tensor"),
            P(SEQ, "tensor"),
            P("dp", SEQ, "tensor"),
            P("dp", SEQ, "tensor"),
            P("dp", SEQ, "tensor"),
            P("dp", SEQ, "tensor"),
            P("dp", None, SEQ),
        ),
        out_specs=(
            P("dp", SEQ, "tensor"),
            P("dp", SEQ, "tensor"),
            P("dp", "tensor", SEQ),
            P(SEQ, "tensor"),
        ),
        check_vma=False,
    )
```

```python
import math

import jax
import jax.numpy as jnp
from jax import lax
from jax.experimental import pallas as pl
from jax.experimental.pallas import tpu as pltpu
from jax.sharding import Mesh, PartitionSpec as P

BF = jnp.bfloat16
F32 = jnp.float32
SEQ = ("zh", "zl", "core")
SWAP = [(0, 1), (1, 0)]


def dot(a, b):
    return jnp.dot(a, b, preferred_element_type=F32)


def dot_nt(a, b):
    return lax.dot_general(a, b, (((1,), (1,)), ((), ())), preferred_element_type=F32)


def project_kernel(batch_ref, own_ref, other_ref, *refs):
    slabs, out_ref, weight = refs[:-2], refs[-2], refs[-1]
    step = pl.program_id(0)
    half = pl.num_programs(0) // 2
    near, far, rows, size = slabs[0].shape

    @pl.when(step == 0)
    def _():
        for shift, slab in enumerate(slabs):
            source = lax.rem(batch_ref[0] + len(slabs) - shift, len(slabs))
            cols = pl.ds(pl.multiple_of(source * size, size), size)
            for zl in range(near):
                for zh in range(far):
                    first = (zh * near + zl) * rows
                    weight[first : first + rows, cols] = slab[zl, zh]

    @pl.when(step < half)
    def _():
        out_ref[...] = dot(own_ref[...], weight[...]).astype(BF)

    @pl.when(step >= half)
    def _():
        out_ref[...] = dot(other_ref[...], weight[...]).astype(BF)


def project(batch, own, other, slabs):
    rows, width = own.shape
    size = slabs[0].shape[-1]
    columns = len(slabs) * size
    block = 256
    half = rows // block
    whole = pl.BlockSpec(slabs[0].shape, lambda t, b: (0, 0, 0, 0))
    return pl.pallas_call(
        project_kernel,
        grid_spec=pltpu.PrefetchScalarGridSpec(
            num_scalar_prefetch=1,
            grid=(2 * half,),
            in_specs=[
                pl.BlockSpec((block, width), lambda t, b: (jnp.minimum(t, half - 1), 0)),
                pl.BlockSpec((block, width), lambda t, b: (jnp.maximum(t - half, 0), 0)),
            ]
            + [whole] * len(slabs),
            out_specs=pl.BlockSpec((block, columns), lambda t, b: (t, 0)),
            scratch_shapes=[pltpu.VMEM((width, columns), BF)],
        ),
        out_shape=jax.ShapeDtypeStruct((2 * rows, columns), BF),
        compiler_params=pltpu.CompilerParams(vmem_limit_bytes=56 * 2**20),
        cost_estimate=pl.CostEstimate(flops=0, bytes_accessed=2**20, transcendentals=0),
    )(batch, own, other, *slabs)


def attend_kernel(
    core_ref, kv_ref, query_ref, grad_ref, stat_ref, own_ref, other_ref, part_ref, qt, gt, total,
    *, size, scaling, latent_factor, prefix_factor,
):
    step = pl.program_id(0)
    last = pl.num_programs(0) - 1
    half = pl.num_programs(0) // 2

    @pl.when(step == 0)
    def _():
        qt[...] = query_ref[...].T
        gt[...] = grad_ref[...].T
        total[...] = jnp.zeros_like(total)

    key_out, value_out = [], []
    for head in range(2):
        cols = slice(head * size, (head + 1) * size)
        keys = kv_ref[:, cols]
        values = kv_ref[:, (2 + head) * size : (3 + head) * size]
        scores = dot(keys, qt[cols, :]) * scaling
        weights = jnp.exp(scores - stat_ref[2 * head : 2 * head + 1, :])
        probs = dot(values, gt[cols, :])
        score_grad = (weights * (probs - stat_ref[2 * head + 1 : 2 * head + 2, :])).astype(BF)
        value_out.append(dot(weights.astype(BF), grad_ref[:, cols]) * latent_factor)
        key_out.append(dot(score_grad, query_ref[:, cols]) * (scaling * latent_factor))
        total[cols, :] += dot(keys.T, score_grad)
    result = jnp.concatenate(key_out + value_out, axis=1).astype(BF)

    @pl.when(step < half)
    def _():
        own_ref[...] = result

    @pl.when(step >= half)
    def _():
        other_ref[...] = result

    @pl.when(step == last)
    def _():
        count, _, width = part_ref.shape
        for i in range(count):
            part_ref[i] = (
                total[:, i * width : (i + 1) * width] * (scaling * prefix_factor)
            ).astype(BF)


def attend(core, kv, gathered, stats, groups, prefix_count):
    tokens, columns = kv.shape
    latents = gathered.shape[0]
    size = columns // 4
    block = 256
    half = tokens // block // 2
    kernel = lambda *refs: attend_kernel(
        *refs,
        size=size,
        scaling=1.0 / math.sqrt(size),
        latent_factor=1.0 / math.sqrt(latents),
        prefix_factor=1.0 / math.sqrt(prefix_count),
    )
    return pl.pallas_call(
        kernel,
        grid_spec=pltpu.PrefetchScalarGridSpec(
            num_scalar_prefetch=1,
            grid=(tokens // block,),
            in_specs=[
                pl.BlockSpec((block, columns), lambda t, c: (t, 0)),
                pl.BlockSpec((latents, 2 * size), lambda t, c: (0, c[0])),
                pl.BlockSpec((latents, 2 * size), lambda t, c: (0, c[0] + 2)),
                pl.BlockSpec(stats.shape, lambda t, c: (0, 0)),
            ],
            out_specs=[
                pl.BlockSpec((block, columns), lambda t, c: (jnp.minimum(t, half - 1), 0)),
                pl.BlockSpec((block, columns), lambda t, c: (jnp.maximum(t - half, 0), 0)),
                pl.BlockSpec((groups, 2 * size, latents // groups), lambda t, c: (0, 0, 0)),
            ],
            scratch_shapes=[
                pltpu.VMEM((2 * size, latents), BF),
                pltpu.VMEM((2 * size, latents), BF),
                pltpu.VMEM((2 * size, latents), F32),
            ],
        ),
        out_shape=[
            jax.ShapeDtypeStruct((tokens // 2, columns), BF),
            jax.ShapeDtypeStruct((tokens // 2, columns), BF),
            jax.ShapeDtypeStruct((groups, 2 * size, latents // groups), BF),
        ],
        compiler_params=pltpu.CompilerParams(vmem_limit_bytes=56 * 2**20),
        cost_estimate=pl.CostEstimate(
            flops=20 * tokens * latents * size,
            bytes_accessed=6 * 2**20,
            transcendentals=2 * tokens * latents,
        ),
    )(core, kv, gathered, gathered, stats)


def exchange(x, axes):
    return lax.all_to_all(x, axes, 0, 0, tiled=True)


def spread(x, axes):
    count = lax.axis_size(axes)
    return exchange(jnp.broadcast_to(x[None], (count,) + x.shape), axes)


def halves(x):
    return jnp.transpose(x.reshape(x.shape[0], 2, x.shape[1] // 2), (1, 0, 2))


def two_parts(x):
    high = lax.reduce_precision(x, 8, 7)
    return high.astype(BF), (x - high).astype(BF)


def local(
    prefix, key_weight, value_weight, query_weight, queries, out_grad, attn_out, shifted_lse, latent_in
):
    core = lax.axis_index("core")
    batch = lax.axis_index("dp")
    first = core == 0
    ranks = lax.axis_size(SEQ)
    batches = lax.axis_size("dp")
    tokens_in = prefix[0]
    token_count = tokens_in.shape[0]
    rows, columns = queries.shape[1:]
    heads = shifted_lse.shape[2]
    size = columns // heads
    latents = rows * ranks

    gathered = lax.all_gather(
        jnp.concatenate([queries[0], out_grad[0]], axis=1), SEQ, axis=0, tiled=True
    )
    other_tokens = lax.ppermute(tokens_in, "core", SWAP)
    latent_own = latent_in[0].T
    query_halves = halves(query_weight)
    query_mine = jnp.where(first, query_halves[0], query_halves[1])
    query_theirs = jnp.where(first, query_halves[1], query_halves[0])
    swapped = lax.ppermute(jnp.concatenate([latent_own, query_theirs], axis=1), "core", SWAP)
    latent_other, query_other = swapped[:, :latents], swapped[:, latents:]

    def in_order(own, other):
        return jnp.where(first, jnp.concatenate([own, other], 0), jnp.concatenate([other, own], 0))

    latent_both = in_order(latent_own, latent_other)
    query_both = in_order(query_mine, query_other)

    row_delta = jnp.sum(
        (out_grad[0].astype(F32) * attn_out[0].astype(F32)).reshape(rows, heads, size), axis=2
    )
    stats = jnp.stack([shifted_lse[0], row_delta]).reshape(2, rows, 2, heads // 2)
    high, low = two_parts(stats)
    packed = jnp.transpose(jnp.stack([high, low]), (3, 1, 0, 4, 2))
    packed = packed.reshape(2, 2, 2 * (heads // 2) * rows)
    packed = jnp.pad(packed, ((0, 0), (0, 14), (0, 0)))
    source = jnp.where(batch < batches // 2, key_weight, value_weight)
    column = lax.rem(batch, batches // 2) * size
    slab = jnp.stack(
        [lax.dynamic_slice_in_dim(source, c * (columns // 2) + column, size, 1) for c in range(2)]
    )
    block = jnp.concatenate([slab, packed], axis=1)
    far = lax.axis_size("zh")
    near = lax.axis_size("zl")
    block = jnp.broadcast_to(block[None], (far,) + block.shape).reshape((-1,) + block.shape[1:])
    landed = lax.all_gather(exchange(block, ("zh", "core")), "zl", axis=0, tiled=True)
    depth = key_weight.shape[0]
    first_slab = landed[:, :depth].reshape(near, far, 2 * depth, size)
    arrived = [first_slab] + [
        lax.ppermute(first_slab, "dp", [(i, (i + d) % batches) for i in range(batches)])
        for d in range(1, batches)
    ]
    stats_all = landed[:, depth : depth + 2].astype(F32)
    stats_all = stats_all.reshape(near, far, 2, 2, 2, heads // 2, rows)
    stats_all = stats_all[:, :, :, :, 0] + stats_all[:, :, :, :, 1]
    stats_all = jnp.transpose(stats_all, (4, 3, 1, 0, 2, 5)).reshape(heads, latents)

    kv = project(batch.reshape(1).astype(jnp.int32), tokens_in, other_tokens, arrived)
    groups = lax.axis_size("zl")
    own_grads, other_grads, part = attend(
        jnp.reshape(core, (1,)).astype(jnp.int32), kv, gathered, stats_all, groups, token_count * ranks
    )
    theirs = lax.ppermute(other_grads, "core", SWAP)
    half = columns // 2

    def whole(lo):
        mine, other = own_grads[:, lo : lo + half], theirs[:, lo : lo + half]
        return jnp.where(
            first, jnp.concatenate([mine, other], 1), jnp.concatenate([other, mine], 1)
        )[None]

    near = jnp.sum(exchange(part, "zl").astype(F32), axis=0).astype(BF)
    full = jnp.sum(spread(near, "zh").astype(F32), axis=0).astype(BF)
    every = lax.all_gather(full, "zl", axis=1, tiled=True)

    latent_part = dot(query_both, every).astype(BF)
    latent_part = latent_part.reshape(2, columns // 8, lax.axis_size("tensor"), -1)
    latent_part = jnp.transpose(latent_part, (0, 2, 1, 3)).reshape(-1, columns // 8, latents // 4)
    latent_sum = jnp.sum(exchange(latent_part, ("core", "tensor")).astype(F32), axis=0)
    latent_grad = latent_sum.astype(BF).T[None]

    weight_part = dot_nt(latent_both, every).astype(BF)
    weight_part = weight_part.reshape(2, 1, columns // 8, half)
    weight_part = jnp.broadcast_to(weight_part, (2, batches, columns // 8, half))
    weight_sum = exchange(weight_part.reshape(-1, columns // 8, half), ("core", "dp"))
    weight_sum = jnp.sum(weight_sum.reshape(2, batches, columns // 8, half).astype(F32), axis=1)
    weight_factor = 1.0 / math.sqrt(latents * batches)
    weight_grad = jnp.transpose(weight_sum, (1, 0, 2)).reshape(columns // 8, columns) * weight_factor
    return (whole(0), whole(half), latent_grad, weight_grad)


def solution(mesh):
    fine = Mesh(
        mesh.devices.reshape(4, 4, 2, *mesh.devices.shape[1:]), SEQ + tuple(mesh.axis_names[1:])
    )
    return jax.shard_map(
        local,
        mesh=fine,
        in_specs=(
            P("dp", SEQ, None),
            P(SEQ, "tensor"),
            P(SEQ, "tensor"),
            P(SEQ, "tensor"),
            P("dp", SEQ, "tensor"),
            P("dp", SEQ, "tensor"),
            P("dp", SEQ, "tensor"),
            P("dp", SEQ, "tensor"),
            P("dp", None, SEQ),
        ),
        out_specs=(
            P("dp", SEQ, "tensor"),
            P("dp", SEQ, "tensor"),
            P("dp", "tensor", SEQ),
            P(SEQ, "tensor"),
        ),
        check_vma=False,
    )
```

```python
import math

import jax
import jax.numpy as jnp
from jax import lax
from jax.experimental import pallas as pl
from jax.experimental.pallas import tpu as pltpu
from jax.sharding import Mesh, PartitionSpec as P

BF = jnp.bfloat16
F32 = jnp.float32
SEQ = ("zh", "zl", "core")
SWAP = [(0, 1), (1, 0)]


def dot(a, b):
    return jnp.dot(a, b, preferred_element_type=F32)


def dot_nt(a, b):
    return lax.dot_general(a, b, (((1,), (1,)), ((), ())), preferred_element_type=F32)


def project_kernel(own_ref, other_ref, slab_ref, out_ref, weight):
    step = pl.program_id(0)
    half = pl.num_programs(0) // 2
    near, slabs, far, cores, _, size = slab_ref.shape
    rows = weight.shape[0] // (near * far * cores)

    @pl.when(step == 0)
    def _():
        for slab in range(slabs):
            for zl in range(near):
                for zh in range(far):
                    for core in range(cores):
                        first = ((zh * near + zl) * cores + core) * rows
                        weight[first : first + rows, slab * size : (slab + 1) * size] = slab_ref[
                            zl, slab, zh, core, :rows
                        ]

    @pl.when(step < half)
    def _():
        out_ref[...] = dot(own_ref[...], weight[...]).astype(BF)

    @pl.when(step >= half)
    def _():
        out_ref[...] = dot(other_ref[...], weight[...]).astype(BF)


def project(own, other, slabs):
    rows, width = own.shape
    columns = slabs.shape[1] * slabs.shape[5]
    block = 256
    half = rows // block
    return pl.pallas_call(
        project_kernel,
        grid=(2 * half,),
        in_specs=[
            pl.BlockSpec((block, width), lambda t: (jnp.minimum(t, half - 1), 0)),
            pl.BlockSpec((block, width), lambda t: (jnp.maximum(t - half, 0), 0)),
            pl.BlockSpec(slabs.shape, lambda t: (0, 0, 0, 0, 0, 0)),
        ],
        out_specs=pl.BlockSpec((block, columns), lambda t: (t, 0)),
        out_shape=jax.ShapeDtypeStruct((2 * rows, columns), BF),
        scratch_shapes=[pltpu.VMEM((width, columns), BF)],
        compiler_params=pltpu.CompilerParams(vmem_limit_bytes=32 * 2**20),
        cost_estimate=pl.CostEstimate(flops=0, bytes_accessed=2**20, transcendentals=0),
    )(own, other, slabs)


def attend_kernel(
    place_ref, kv_ref, query_ref, grad_ref, stat_ref, own_ref, other_ref, *refs,
    size, scaling, latent_factor, prefix_factor,
):
    part_refs, (qt, gt, total) = refs[:-3], refs[-3:]
    step = pl.program_id(0)
    last = pl.num_programs(0) - 1
    half = pl.num_programs(0) // 2

    @pl.when(step == 0)
    def _():
        qt[...] = query_ref[...].T
        gt[...] = grad_ref[...].T
        total[...] = jnp.zeros_like(total)

    key_out, value_out = [], []
    for head in range(2):
        cols = slice(head * size, (head + 1) * size)
        keys = kv_ref[:, cols]
        values = kv_ref[:, (2 + head) * size : (3 + head) * size]
        scores = dot(keys, qt[cols, :]) * scaling
        weights = jnp.exp(scores - stat_ref[2 * head : 2 * head + 1, :])
        probs = dot(values, gt[cols, :])
        score_grad = (weights * (probs - stat_ref[2 * head + 1 : 2 * head + 2, :])).astype(BF)
        value_out.append(dot(weights.astype(BF), grad_ref[:, cols]) * latent_factor)
        key_out.append(dot(score_grad, query_ref[:, cols]) * (scaling * latent_factor))
        total[cols, :] += dot(keys.T, score_grad)
    result = jnp.concatenate(key_out + value_out, axis=1).astype(BF)

    @pl.when(step < half)
    def _():
        own_ref[...] = result

    @pl.when(step >= half)
    def _():
        other_ref[...] = result

    @pl.when(step == last)
    def _():
        for ahead, part_ref in enumerate(part_refs):
            rows = part_ref.shape[0]
            block = lax.rem(place_ref[1] + ahead, len(part_refs))
            part = total[pl.ds(pl.multiple_of(block * rows, rows), rows), :]
            part_ref[...] = (part * (scaling * prefix_factor)).astype(BF)


def attend(place, kv, gathered, stats, near, prefix_count):
    tokens, columns = kv.shape
    latents = gathered.shape[0]
    size = columns // 4
    block = 256
    half = tokens // block // 2
    kernel = lambda *refs: attend_kernel(
        *refs,
        size=size,
        scaling=1.0 / math.sqrt(size),
        latent_factor=1.0 / math.sqrt(latents),
        prefix_factor=1.0 / math.sqrt(prefix_count),
    )
    return pl.pallas_call(
        kernel,
        grid_spec=pltpu.PrefetchScalarGridSpec(
            num_scalar_prefetch=1,
            grid=(tokens // block,),
            in_specs=[
                pl.BlockSpec((block, columns), lambda t, c: (t, 0)),
                pl.BlockSpec((latents, 2 * size), lambda t, c: (0, c[0])),
                pl.BlockSpec((latents, 2 * size), lambda t, c: (0, c[0] + 2)),
                pl.BlockSpec(stats.shape, lambda t, c: (0, 0)),
            ],
            out_specs=[
                pl.BlockSpec((block, columns), lambda t, c: (jnp.minimum(t, half - 1), 0)),
                pl.BlockSpec((block, columns), lambda t, c: (jnp.maximum(t - half, 0), 0)),
            ]
            + [pl.BlockSpec((2 * size // near, latents), lambda t, c: (0, 0))] * near,
            scratch_shapes=[
                pltpu.VMEM((2 * size, latents), BF),
                pltpu.VMEM((2 * size, latents), BF),
                pltpu.VMEM((2 * size, latents), F32),
            ],
        ),
        out_shape=[
            jax.ShapeDtypeStruct((tokens // 2, columns), BF),
            jax.ShapeDtypeStruct((tokens // 2, columns), BF),
        ]
        + [jax.ShapeDtypeStruct((2 * size // near, latents), BF)] * near,
        compiler_params=pltpu.CompilerParams(vmem_limit_bytes=32 * 2**20),
        cost_estimate=pl.CostEstimate(
            flops=20 * tokens * latents * size,
            bytes_accessed=6 * 2**20,
            transcendentals=2 * tokens * latents,
        ),
    )(place, kv, gathered, gathered, stats)


def tail_kernel(place_ref, query_ref, latent_ref, *refs):
    blocks, (latent_out, weight_out, every) = refs[:-3], refs[-3:]
    for ahead, block_ref in enumerate(blocks):
        rows = block_ref.shape[0]
        block = lax.rem(place_ref[1] + ahead, len(blocks))
        every[pl.ds(pl.multiple_of(block * rows, rows), rows), :] = block_ref[...]
    count, rows, width = latent_out.shape
    latent = dot(query_ref[...], every[...]).astype(BF)
    weight = dot_nt(latent_ref[...], every[...]).astype(BF)
    for i in range(count):
        core, group = divmod(i, count // 2)
        latent_out[i] = latent[core * rows : (core + 1) * rows, group * width : (group + 1) * width]
        weight_out[i] = weight[core * rows : (core + 1) * rows, :]


def tail(place, query, latent, blocks, tensors, batches):
    both, half = query.shape
    rows = both // 2
    latents = latent.shape[1]
    return pl.pallas_call(
        tail_kernel,
        in_specs=[pl.BlockSpec(memory_space=pltpu.SMEM)]
        + [pl.BlockSpec(memory_space=pltpu.VMEM)] * (2 + len(blocks)),
        out_specs=[pl.BlockSpec(memory_space=pltpu.VMEM)] * 2,
        out_shape=[
            jax.ShapeDtypeStruct((2 * tensors, rows, latents // tensors), BF),
            jax.ShapeDtypeStruct((2 * batches, rows, half), BF),
        ],
        scratch_shapes=[pltpu.VMEM((half, latents), BF)],
        compiler_params=pltpu.CompilerParams(vmem_limit_bytes=32 * 2**20),
        cost_estimate=pl.CostEstimate(flops=0, bytes_accessed=2**20, transcendentals=0),
    )(place, query, latent, *blocks)


def exchange(x, axes):
    return lax.all_to_all(x, axes, 0, 0, tiled=True)


def halves(x):
    return jnp.transpose(x.reshape(x.shape[0], 2, x.shape[1] // 2), (1, 0, 2))


def two_parts(x):
    high = lax.reduce_precision(x, 8, 7)
    return high.astype(BF), (x - high).astype(BF)


def local(
    prefix, key_weight, value_weight, query_weight, queries, out_grad, attn_out, shifted_lse, latent_in
):
    core = lax.axis_index("core")
    batch = lax.axis_index("dp")
    first = core == 0
    ranks = lax.axis_size(SEQ)
    batches = lax.axis_size("dp")
    tokens_in = prefix[0]
    token_count = tokens_in.shape[0]
    rows, columns = queries.shape[1:]
    heads = shifted_lse.shape[2]
    size = columns // heads
    latents = rows * ranks

    gathered = lax.all_gather(
        jnp.concatenate([queries[0], out_grad[0]], axis=1), SEQ, axis=0, tiled=True
    )
    other_tokens = lax.ppermute(tokens_in, "core", SWAP)
    latent_own = latent_in[0].T
    query_halves = halves(query_weight)
    query_mine = jnp.where(first, query_halves[0], query_halves[1])
    query_theirs = jnp.where(first, query_halves[1], query_halves[0])
    swapped = lax.ppermute(jnp.concatenate([latent_own, query_theirs], axis=1), "core", SWAP)
    latent_other, query_other = swapped[:, :latents], swapped[:, latents:]

    def in_order(own, other):
        return jnp.where(first, jnp.concatenate([own, other], 0), jnp.concatenate([other, own], 0))

    latent_both = in_order(latent_own, latent_other)
    query_both = in_order(query_mine, query_other)

    row_delta = jnp.sum(
        (out_grad[0].astype(F32) * attn_out[0].astype(F32)).reshape(rows, heads, size), axis=2
    )
    stats = jnp.stack([shifted_lse[0], row_delta]).reshape(2, rows, 2, heads // 2)
    high, low = two_parts(stats)
    packed = jnp.transpose(jnp.stack([high, low]), (3, 1, 0, 4, 2))
    packed = packed.reshape(2, 2, 2 * (heads // 2) * rows)
    packed = jnp.pad(packed, ((0, 0), (0, 14), (0, 0)))
    source = jnp.where(batch < batches // 2, key_weight, value_weight)
    column = lax.rem(batch, batches // 2) * size
    slab = jnp.stack(
        [lax.dynamic_slice_in_dim(source, c * (columns // 2) + column, size, 1) for c in range(2)]
    )
    block = jnp.concatenate([slab, packed], axis=1)
    far = lax.axis_size("zh")
    near = lax.axis_size("zl")
    block = jnp.broadcast_to(block[None], (far,) + block.shape).reshape((-1,) + block.shape[1:])
    depth = key_weight.shape[0]

    def gather_slabs(carried):
        landed = exchange(block, ("zh", "core"))
        wide = jnp.broadcast_to(landed, (near * batches,) + landed.shape)
        return carried[0] + 1, exchange(wide.reshape((-1,) + landed.shape[1:]), ("zl", "dp"))

    _, spread_out = lax.while_loop(
        lambda carried: carried[0] < 1,
        gather_slabs,
        (jnp.minimum(batch, 0), jnp.zeros((near * batches * block.shape[0],) + block.shape[1:], BF)),
    )
    spread_out = spread_out.reshape(near, batches, far, 2, depth + 16, size)
    stats_all = lax.dynamic_index_in_dim(spread_out, batch, 1, False)[:, :, :, depth : depth + 2]
    stats_all = stats_all.astype(F32).reshape(near, far, 2, 2, 2, heads // 2, rows)
    stats_all = stats_all[:, :, :, :, 0] + stats_all[:, :, :, :, 1]
    stats_all = jnp.transpose(stats_all, (4, 3, 1, 0, 2, 5)).reshape(heads, latents)

    kv = project(tokens_in, other_tokens, spread_out)
    place = jnp.stack([core, lax.axis_index("zl")]).astype(jnp.int32)
    own_grads, other_grads, *parts = attend(
        place, kv, gathered, stats_all, near, token_count * ranks
    )
    theirs = lax.ppermute(other_grads, "core", SWAP)
    half = columns // 2

    def whole(lo):
        mine, other = own_grads[:, lo : lo + half], theirs[:, lo : lo + half]
        return jnp.where(
            first, jnp.concatenate([mine, other], 1), jnp.concatenate([other, mine], 1)
        )[None]

    def move(x, distance):
        return lax.ppermute(x, ("zh", "zl"), [(i, (i + distance) % 16) for i in range(16)])

    def total(*terms):
        return sum(term.astype(F32) for term in terms).astype(BF)

    window = total(parts[0], move(parts[1], 1), move(parts[2], 2), move(parts[3], -1))
    full = total(window, move(window, 4), move(window, 8), move(window, -4))
    blocks = [full, move(full, -1), move(full, 2), move(full, 1)]
    latent_part, weight_part = tail(
        place, query_both, latent_both, blocks, lax.axis_size("tensor"), batches
    )

    latent_sum = jnp.sum(exchange(latent_part, ("core", "tensor")).astype(F32), axis=0)
    latent_grad = latent_sum.astype(BF).T[None]

    weight_sum = exchange(weight_part, ("core", "dp"))
    weight_sum = jnp.sum(weight_sum.reshape(2, batches, columns // 8, half).astype(F32), axis=1)
    weight_factor = 1.0 / math.sqrt(latents * batches)
    weight_grad = jnp.transpose(weight_sum, (1, 0, 2)).reshape(columns // 8, columns) * weight_factor
    return (whole(0), whole(half), latent_grad, weight_grad)


def solution(mesh):
    fine = Mesh(
        mesh.devices.reshape(4, 4, 2, *mesh.devices.shape[1:]), SEQ + tuple(mesh.axis_names[1:])
    )
    return jax.shard_map(
        local,
        mesh=fine,
        in_specs=(
            P("dp", SEQ, None),
            P(SEQ, "tensor"),
            P(SEQ, "tensor"),
            P(SEQ, "tensor"),
            P("dp", SEQ, "tensor"),
            P("dp", SEQ, "tensor"),
            P("dp", SEQ, "tensor"),
            P("dp", SEQ, "tensor"),
            P("dp", None, SEQ),
        ),
        out_specs=(
            P("dp", SEQ, "tensor"),
            P("dp", SEQ, "tensor"),
            P("dp", "tensor", SEQ),
            P(SEQ, "tensor"),
        ),
        check_vma=False,
    )
```

```python
import functools
import math

import jax
import jax.numpy as jnp
from jax import lax
from jax.experimental import pallas as pl
from jax.experimental.pallas import tpu as pltpu
from jax.sharding import Mesh, PartitionSpec as P

BF = jnp.bfloat16
F32 = jnp.float32
SEQ = ("zh", "zl", "core")
SWAP = [(0, 1), (1, 0)]


def dot(a, b):
    return jnp.dot(a, b, preferred_element_type=F32)


def dot_nt(a, b):
    return lax.dot_general(a, b, (((1,), (1,)), ((), ())), preferred_element_type=F32)


def pack_kernel(place_ref, key_ref, value_ref, query_ref, grad_ref, out_ref, lse_ref, block_ref):
    batch = place_ref[2]
    depth, columns = key_ref.shape
    rows = query_ref.shape[0]
    count, _, size = block_ref.shape
    heads = columns // size
    half = columns // 2
    product = grad_ref[...].astype(F32) * out_ref[...].astype(F32)
    lane = lax.broadcasted_iota(jnp.int32, (rows, size), 1)
    delta = jnp.zeros((rows, size), F32)
    for head in range(heads):
        one = jnp.sum(product[:, head * size : (head + 1) * size], axis=1, keepdims=True)
        delta = jnp.where(lane == head, one, delta)
    lse, delta = lse_ref[...], delta.T[:heads]
    zeros = jnp.zeros((16, size), BF)
    for core in range(2):
        column = pl.multiple_of(core * half + lax.rem(batch, 2) * size, size)
        mine = slice(core * heads // 2, (core + 1) * heads // 2)
        exact = jnp.concatenate([lse[mine], delta[mine]], axis=0)
        high = exact.astype(BF).astype(F32)
        stats = jnp.concatenate([high, exact - high], axis=0).astype(BF)
        for block in range(core, count, 2):

            @pl.when(batch < 2)
            def _():
                block_ref[block, :depth] = key_ref[:, pl.ds(column, size)]

            @pl.when(batch >= 2)
            def _():
                block_ref[block, :depth] = value_ref[:, pl.ds(column, size)]

            first = depth
            for ref in (query_ref, grad_ref):
                for lo in range(core * half, (core + 1) * half, size):
                    block_ref[block, first : first + rows] = ref[:, lo : lo + size]
                    first += rows
            block_ref[block, first:] = zeros
            block_ref[block, first : first + 2 * heads, :rows] = stats


def pack(place, key_weight, value_weight, query, grad, out, lse, count):
    depth, columns = key_weight.shape
    size = columns // lse.shape[0]
    return pl.pallas_call(
        pack_kernel,
        grid=(1,),
        in_specs=[pl.BlockSpec(memory_space=pltpu.SMEM)]
        + [
            pl.BlockSpec(x.shape, lambda i: (0, 0))
            for x in (key_weight, value_weight, query, grad, out, lse)
        ],
        out_specs=pl.BlockSpec((count, depth + 4 * query.shape[0] + 16, size), lambda i: (0, 0, 0)),
        out_shape=jax.ShapeDtypeStruct((count, depth + 4 * query.shape[0] + 16, size), BF),
        compiler_params=pltpu.CompilerParams(vmem_limit_bytes=32 * 2**20),
        cost_estimate=pl.CostEstimate(flops=0, bytes_accessed=2**19, transcendentals=0),
    )(place, key_weight, value_weight, query, grad, out, lse)


def project_kernel(place_ref, own_ref, other_ref, *refs):
    slabs, out_ref, weight = refs[:-2], refs[-2], refs[-1]
    step = pl.program_id(0)
    half = pl.num_programs(0) // 2
    near, far, rows, size = slabs[0].shape

    @pl.when(step == 0)
    def _():
        for shift, slab in enumerate(slabs):
            source = lax.rem(place_ref[2] + len(slabs) - shift, len(slabs))
            cols = pl.ds(pl.multiple_of(source * size, size), size)
            for zl in range(near):
                for zh in range(far):
                    first = (zh * near + zl) * rows
                    weight[first : first + rows, cols] = slab[zl, zh]

    @pl.when(step < half)
    def _():
        out_ref[...] = dot(own_ref[...], weight[...]).astype(BF)

    @pl.when(step >= half)
    def _():
        out_ref[...] = dot(other_ref[...], weight[...]).astype(BF)


def project(place, own, other, slabs):
    rows, width = own.shape
    size = slabs[0].shape[-1]
    columns = len(slabs) * size
    block = 256
    half = rows // block
    whole = pl.BlockSpec(slabs[0].shape, lambda t, b: (0, 0, 0, 0))
    return pl.pallas_call(
        project_kernel,
        grid_spec=pltpu.PrefetchScalarGridSpec(
            num_scalar_prefetch=1,
            grid=(2 * half,),
            in_specs=[
                pl.BlockSpec((block, width), lambda t, b: (jnp.minimum(t, half - 1), 0)),
                pl.BlockSpec((block, width), lambda t, b: (jnp.maximum(t - half, 0), 0)),
            ]
            + [whole] * len(slabs),
            out_specs=pl.BlockSpec((block, columns), lambda t, b: (t, 0)),
            scratch_shapes=[pltpu.VMEM((width, columns), BF)],
        ),
        out_shape=jax.ShapeDtypeStruct((2 * rows, columns), BF),
        compiler_params=pltpu.CompilerParams(vmem_limit_bytes=32 * 2**20),
        cost_estimate=pl.CostEstimate(flops=0, bytes_accessed=2**20, transcendentals=0),
    )(place, own, other, *slabs)


def attend_kernel(
    kv_ref, rows_ref, stat_ref, own_ref, other_ref, part_ref, query, grad, qt, gt, total,
    size, scaling, latent_factor, prefix_factor,
):
    step = pl.program_id(0)
    last = pl.num_programs(0) - 1
    half = pl.num_programs(0) // 2
    near, far, cores, _, _ = rows_ref.shape
    rows = query.shape[0] // (near * far * cores)

    @pl.when(step == 0)
    def _():
        for zl in range(near):
            for zh in range(far):
                for core in range(cores):
                    first = ((zh * near + zl) * cores + core) * rows
                    for part in range(4):
                        to = (query, grad)[part // 2]
                        lo = part % 2 * size
                        to[first : first + rows, lo : lo + size] = rows_ref[
                            zl, zh, core, part * rows : (part + 1) * rows
                        ]
        qt[...] = query[...].T
        gt[...] = grad[...].T
        total[...] = jnp.zeros_like(total)

    key_out, value_out = [], []
    for head in range(2):
        cols = slice(head * size, (head + 1) * size)
        keys = kv_ref[:, cols]
        values = kv_ref[:, (2 + head) * size : (3 + head) * size]
        scores = dot(keys, qt[cols, :]) * scaling
        weights = jnp.exp(scores - stat_ref[head : head + 1, :])
        probs = dot(values, gt[cols, :])
        score_grad = (weights * (probs - stat_ref[2 + head : 3 + head, :])).astype(BF)
        value_out.append(dot(weights.astype(BF), grad[:, cols]) * latent_factor)
        key_out.append(dot(score_grad, query[:, cols]) * (scaling * latent_factor))
        total[cols, :] += dot(keys.T, score_grad)
    result = jnp.concatenate(key_out + value_out, axis=1).astype(BF)

    @pl.when(step < half)
    def _():
        own_ref[...] = result

    @pl.when(step >= half)
    def _():
        other_ref[...] = result

    @pl.when(step == last)
    def _():
        part_ref[...] = (total[...] * (scaling * prefix_factor)).astype(BF)


def attend(kv, gathered, stats, prefix_count):
    tokens, columns = kv.shape
    latents = stats.shape[1]
    size = columns // 4
    block = 256
    half = tokens // block // 2
    kernel = functools.partial(
        attend_kernel,
        size=size,
        scaling=1.0 / math.sqrt(size),
        latent_factor=1.0 / math.sqrt(latents),
        prefix_factor=1.0 / math.sqrt(prefix_count),
    )
    return pl.pallas_call(
        kernel,
        grid=(tokens // block,),
        in_specs=[
            pl.BlockSpec((block, columns), lambda t: (t, 0)),
            pl.BlockSpec(gathered.shape, lambda t: (0, 0, 0, 0, 0)),
            pl.BlockSpec(stats.shape, lambda t: (0, 0)),
        ],
        out_specs=[
            pl.BlockSpec((block, columns), lambda t: (jnp.minimum(t, half - 1), 0)),
            pl.BlockSpec((block, columns), lambda t: (jnp.maximum(t - half, 0), 0)),
            pl.BlockSpec((2 * size, latents), lambda t: (0, 0)),
        ],
        out_shape=[
            jax.ShapeDtypeStruct((tokens // 2, columns), BF),
            jax.ShapeDtypeStruct((tokens // 2, columns), BF),
            jax.ShapeDtypeStruct((2 * size, latents), BF),
        ],
        scratch_shapes=[
            pltpu.VMEM((latents, 2 * size), BF),
            pltpu.VMEM((latents, 2 * size), BF),
            pltpu.VMEM((2 * size, latents), BF),
            pltpu.VMEM((2 * size, latents), BF),
            pltpu.VMEM((2 * size, latents), F32),
        ],
        compiler_params=pltpu.CompilerParams(vmem_limit_bytes=32 * 2**20),
        cost_estimate=pl.CostEstimate(
            flops=20 * tokens * latents * size,
            bytes_accessed=6 * 2**20,
            transcendentals=2 * tokens * latents,
        ),
    )(kv, gathered, stats)


def tail_kernel(query_ref, latent_ref, every_ref, latent_out, weight_out):
    count, rows, width = latent_out.shape
    latent = dot(query_ref[...], every_ref[...]).astype(BF)
    weight = dot_nt(latent_ref[...], every_ref[...]).astype(BF)
    for i in range(count):
        core, group = divmod(i, count // 2)
        latent_out[i] = latent[core * rows : (core + 1) * rows, group * width : (group + 1) * width]
        weight_out[i] = weight[core * rows : (core + 1) * rows, :]


def tail(query, latent, every, tensors, batches):
    both, half = query.shape
    rows = both // 2
    latents = latent.shape[1]
    return pl.pallas_call(
        tail_kernel,
        in_specs=[pl.BlockSpec(memory_space=pltpu.VMEM)] * 3,
        out_specs=[pl.BlockSpec(memory_space=pltpu.VMEM)] * 2,
        out_shape=[
            jax.ShapeDtypeStruct((2 * tensors, rows, latents // tensors), BF),
            jax.ShapeDtypeStruct((2 * batches, rows, half), BF),
        ],
        compiler_params=pltpu.CompilerParams(vmem_limit_bytes=32 * 2**20),
        cost_estimate=pl.CostEstimate(flops=0, bytes_accessed=2**20, transcendentals=0),
    )(query, latent, every)


def exchange(x, axes):
    return lax.all_to_all(x, axes, 0, 0, tiled=True)


def spread(x, axes):
    count = lax.axis_size(axes)
    return exchange(jnp.broadcast_to(x[None], (count,) + x.shape), axes)


def halves(x):
    return jnp.transpose(x.reshape(x.shape[0], 2, x.shape[1] // 2), (1, 0, 2))


def local(
    prefix, key_weight, value_weight, query_weight, queries, out_grad, attn_out, shifted_lse, latent_in
):
    core = lax.axis_index("core")
    batch = lax.axis_index("dp")
    first = core == 0
    ranks = lax.axis_size(SEQ)
    batches = lax.axis_size("dp")
    tokens_in = prefix[0]
    token_count = tokens_in.shape[0]
    rows, columns = queries.shape[1:]
    heads = shifted_lse.shape[2]
    size = columns // heads
    latents = rows * ranks

    other_tokens = lax.ppermute(tokens_in, "core", SWAP)
    latent_own = latent_in[0].T
    query_halves = halves(query_weight)
    query_mine = jnp.where(first, query_halves[0], query_halves[1])
    query_theirs = jnp.where(first, query_halves[1], query_halves[0])
    swapped = lax.ppermute(jnp.concatenate([latent_own, query_theirs], axis=1), "core", SWAP)
    latent_other, query_other = swapped[:, :latents], swapped[:, latents:]

    def in_order(own, other):
        return jnp.where(first, jnp.concatenate([own, other], 0), jnp.concatenate([other, own], 0))

    latent_both = in_order(latent_own, latent_other)
    query_both = in_order(query_mine, query_other)

    far = lax.axis_size("zh")
    near = lax.axis_size("zl")
    depth = key_weight.shape[0]
    place = jnp.stack([core, lax.axis_index("zl"), batch]).astype(jnp.int32)
    blocks = pack(
        place, key_weight, value_weight, queries[0], out_grad[0], attn_out[0], shifted_lse[0].T, 2 * far
    )
    landed = exchange(blocks, ("zh", "core"))
    slab = lax.all_gather(landed[:, :depth], "zl", axis=0, tiled=True)
    gathered = spread(landed[:, depth:], "zl").reshape(near, far, 2, -1, size)
    slab = slab.reshape(near, far, 2 * depth, size)
    slabs = [slab] + [
        lax.ppermute(slab, "dp", [(i, (i + d) % batches) for i in range(batches)])
        for d in range(1, batches)
    ]
    stats = gathered[:, :, :, 4 * rows : 4 * rows + 2 * heads, :rows].astype(F32)
    stats = stats[:, :, :, :heads] + stats[:, :, :, heads:]
    stats = jnp.transpose(stats, (3, 1, 0, 2, 4)).reshape(heads, latents)

    kv = project(place, tokens_in, other_tokens, slabs)
    own_grads, other_grads, part = attend(kv, gathered, stats, token_count * ranks)
    theirs = lax.ppermute(other_grads, "core", SWAP)
    half = columns // 2

    def whole(lo):
        mine, other = own_grads[:, lo : lo + half], theirs[:, lo : lo + half]
        return jnp.where(
            first, jnp.concatenate([mine, other], 1), jnp.concatenate([other, mine], 1)
        )[None]

    share = exchange(part.reshape(far * near, -1, latents), ("zh", "zl"))
    share = jnp.sum(share.astype(F32), axis=0).astype(BF)
    every = lax.all_gather(share, ("zh", "zl"), axis=0, tiled=True)
    latent_part, weight_part = tail(
        query_both, latent_both, every, lax.axis_size("tensor"), batches
    )

    latent_sum = jnp.sum(exchange(latent_part, ("core", "tensor")).astype(F32), axis=0)
    latent_grad = latent_sum.astype(BF).T[None]

    weight_sum = exchange(weight_part, ("core", "dp"))
    weight_sum = jnp.sum(weight_sum.reshape(2, batches, columns // 8, half).astype(F32), axis=1)
    weight_factor = 1.0 / math.sqrt(latents * batches)
    weight_grad = jnp.transpose(weight_sum, (1, 0, 2)).reshape(columns // 8, columns) * weight_factor
    return (whole(0), whole(half), latent_grad, weight_grad)


def solution(mesh):
    fine = Mesh(
        mesh.devices.reshape(4, 4, 2, *mesh.devices.shape[1:]), SEQ + tuple(mesh.axis_names[1:])
    )
    return jax.shard_map(
        local,
        mesh=fine,
        in_specs=(
            P("dp", SEQ, None),
            P(SEQ, "tensor"),
            P(SEQ, "tensor"),
            P(SEQ, "tensor"),
            P("dp", SEQ, "tensor"),
            P("dp", SEQ, "tensor"),
            P("dp", SEQ, "tensor"),
            P("dp", SEQ, "tensor"),
            P("dp", None, SEQ),
        ),
        out_specs=(
            P("dp", SEQ, "tensor"),
            P("dp", SEQ, "tensor"),
            P("dp", "tensor", SEQ),
            P(SEQ, "tensor"),
        ),
        check_vma=False,
    )
```

```python
import functools
import math

import jax
import jax.numpy as jnp
from jax import lax
from jax.experimental import pallas as pl
from jax.experimental.pallas import tpu as pltpu
from jax.sharding import Mesh, PartitionSpec as P

BF = jnp.bfloat16
F32 = jnp.float32
SEQ = ("zh", "zl", "core")
SWAP = [(0, 1), (1, 0)]


def dot(a, b):
    return jnp.dot(a, b, preferred_element_type=F32)


def dot_nt(a, b):
    return lax.dot_general(a, b, (((1,), (1,)), ((), ())), preferred_element_type=F32)


def pack_kernel(place_ref, *refs):
    sources, block_ref, landing, arrived = refs[:6], refs[6], refs[7:13], refs[13]
    copies = [
        pltpu.make_async_copy(source, target, arrived.at[i])
        for i, (source, target) in enumerate(zip(sources, landing))
    ]
    for copy in copies:
        copy.start()
    for copy in copies:
        copy.wait()
    key_ref, value_ref, query_ref, grad_ref, out_ref, lse_ref = landing
    batch = place_ref[2]
    depth, columns = key_ref.shape
    rows = query_ref.shape[0]
    count, _, size = block_ref.shape
    heads = columns // size
    half = columns // 2
    product = grad_ref[...].astype(F32) * out_ref[...].astype(F32)
    lane = lax.broadcasted_iota(jnp.int32, (rows, size), 1)
    delta = jnp.zeros((rows, size), F32)
    for head in range(heads):
        one = jnp.sum(product[:, head * size : (head + 1) * size], axis=1, keepdims=True)
        delta = jnp.where(lane == head, one, delta)
    lse, delta = lse_ref[...], delta.T[:heads]
    zeros = jnp.zeros((16, size), BF)
    for core in range(2):
        column = pl.multiple_of(core * half + lax.rem(batch, 2) * size, size)
        mine = slice(core * heads // 2, (core + 1) * heads // 2)
        exact = jnp.concatenate([lse[mine], delta[mine]], axis=0)
        high = exact.astype(BF).astype(F32)
        stats = jnp.concatenate([high, exact - high], axis=0).astype(BF)
        for block in range(core, count, 2):

            @pl.when(batch < 2)
            def _():
                block_ref[block, :depth] = key_ref[:, pl.ds(column, size)]

            @pl.when(batch >= 2)
            def _():
                block_ref[block, :depth] = value_ref[:, pl.ds(column, size)]

            first = depth
            for ref in (query_ref, grad_ref):
                for lo in range(core * half, (core + 1) * half, size):
                    block_ref[block, first : first + rows] = ref[:, lo : lo + size]
                    first += rows
            block_ref[block, first:] = zeros
            block_ref[block, first : first + 2 * heads, :rows] = stats


def pack(place, key_weight, value_weight, query, grad, out, lse, count):
    depth, columns = key_weight.shape
    size = columns // lse.shape[0]
    sources = (key_weight, value_weight, query, grad, out, lse)
    return pl.pallas_call(
        pack_kernel,
        in_specs=[pl.BlockSpec(memory_space=pltpu.SMEM)]
        + [pl.BlockSpec(memory_space=pltpu.HBM)] * len(sources),
        out_specs=pl.BlockSpec(memory_space=pltpu.VMEM),
        out_shape=jax.ShapeDtypeStruct((count, depth + 4 * query.shape[0] + 16, size), BF),
        scratch_shapes=[pltpu.VMEM(x.shape, x.dtype) for x in sources]
        + [pltpu.SemaphoreType.DMA((len(sources),))],
        compiler_params=pltpu.CompilerParams(vmem_limit_bytes=60 * 2**20),
        cost_estimate=pl.CostEstimate(flops=0, bytes_accessed=2**19, transcendentals=0),
    )(place, *sources)


def unpack_kernel(landed_ref, weight_ref, rows_ref):
    depth = weight_ref.shape[1]
    weight_ref[...] = landed_ref[:, :depth]
    for i in range(rows_ref.shape[0]):
        rows_ref[i] = landed_ref[:, depth:]


def unpack(landed, depth, copies):
    blocks, rows, size = landed.shape
    return pl.pallas_call(
        unpack_kernel,
        in_specs=[pl.BlockSpec(memory_space=pltpu.VMEM)],
        out_specs=[pl.BlockSpec(memory_space=pltpu.VMEM)] * 2,
        out_shape=[
            jax.ShapeDtypeStruct((blocks, depth, size), BF),
            jax.ShapeDtypeStruct((copies, blocks, rows - depth, size), BF),
        ],
        compiler_params=pltpu.CompilerParams(vmem_limit_bytes=60 * 2**20),
        cost_estimate=pl.CostEstimate(flops=0, bytes_accessed=2**20, transcendentals=0),
    )(landed)


def project_kernel(place_ref, own_ref, other_ref, *refs):
    slabs, out_ref, weight = refs[:-2], refs[-2], refs[-1]
    step = pl.program_id(0)
    half = pl.num_programs(0) // 2
    near, far, rows, size = slabs[0].shape

    @pl.when(step == 0)
    def _():
        for shift, slab in enumerate(slabs):
            source = lax.rem(place_ref[2] + len(slabs) - shift, len(slabs))
            cols = pl.ds(pl.multiple_of(source * size, size), size)
            for zl in range(near):
                for zh in range(far):
                    first = (zh * near + zl) * rows
                    weight[first : first + rows, cols] = slab[zl, zh]

    @pl.when(step < half)
    def _():
        out_ref[...] = dot(own_ref[...], weight[...]).astype(BF)

    @pl.when(step >= half)
    def _():
        out_ref[...] = dot(other_ref[...], weight[...]).astype(BF)


def project(place, own, other, slabs):
    rows, width = own.shape
    size = slabs[0].shape[-1]
    columns = len(slabs) * size
    block = 256
    half = rows // block
    whole = pl.BlockSpec(slabs[0].shape, lambda t, b: (0, 0, 0, 0))
    return pl.pallas_call(
        project_kernel,
        grid_spec=pltpu.PrefetchScalarGridSpec(
            num_scalar_prefetch=1,
            grid=(2 * half,),
            in_specs=[
                pl.BlockSpec((block, width), lambda t, b: (jnp.minimum(t, half - 1), 0)),
                pl.BlockSpec((block, width), lambda t, b: (jnp.maximum(t - half, 0), 0)),
            ]
            + [whole] * len(slabs),
            out_specs=pl.BlockSpec((block, columns), lambda t, b: (t, 0)),
            scratch_shapes=[pltpu.VMEM((width, columns), BF)],
        ),
        out_shape=jax.ShapeDtypeStruct((2 * rows, columns), BF),
        compiler_params=pltpu.CompilerParams(vmem_limit_bytes=60 * 2**20),
        cost_estimate=pl.CostEstimate(flops=0, bytes_accessed=2**20, transcendentals=0),
    )(place, own, other, *slabs)


def attend_kernel(
    kv_ref, rows_ref, stat_ref, own_ref, other_ref, part_ref, query, grad, qt, gt, total,
    size, scaling, latent_factor, prefix_factor,
):
    step = pl.program_id(0)
    last = pl.num_programs(0) - 1
    half = pl.num_programs(0) // 2
    near, far, cores, _, _ = rows_ref.shape
    rows = query.shape[0] // (near * far * cores)

    @pl.when(step == 0)
    def _():
        for zl in range(near):
            for zh in range(far):
                for core in range(cores):
                    first = ((zh * near + zl) * cores + core) * rows
                    for part in range(4):
                        to = (query, grad)[part // 2]
                        lo = part % 2 * size
                        to[first : first + rows, lo : lo + size] = rows_ref[
                            zl, zh, core, part * rows : (part + 1) * rows
                        ]
        qt[...] = query[...].T
        gt[...] = grad[...].T
        total[...] = jnp.zeros_like(total)

    key_out, value_out = [], []
    for head in range(2):
        cols = slice(head * size, (head + 1) * size)
        keys = kv_ref[:, cols]
        values = kv_ref[:, (2 + head) * size : (3 + head) * size]
        scores = dot(keys, qt[cols, :]) * scaling
        weights = jnp.exp(scores - stat_ref[head : head + 1, :])
        probs = dot(values, gt[cols, :])
        score_grad = (weights * (probs - stat_ref[2 + head : 3 + head, :])).astype(BF)
        value_out.append(dot(weights.astype(BF), grad[:, cols]) * latent_factor)
        key_out.append(dot(score_grad, query[:, cols]) * (scaling * latent_factor))
        total[cols, :] += dot(keys.T, score_grad)
    result = jnp.concatenate(key_out + value_out, axis=1).astype(BF)

    @pl.when(step < half)
    def _():
        own_ref[...] = result

    @pl.when(step >= half)
    def _():
        other_ref[...] = result

    @pl.when(step == last)
    def _():
        part_ref[...] = (total[...] * (scaling * prefix_factor)).astype(BF)


def attend(kv, gathered, stats, prefix_count):
    tokens, columns = kv.shape
    latents = stats.shape[1]
    size = columns // 4
    block = 256
    half = tokens // block // 2
    kernel = functools.partial(
        attend_kernel,
        size=size,
        scaling=1.0 / math.sqrt(size),
        latent_factor=1.0 / math.sqrt(latents),
        prefix_factor=1.0 / math.sqrt(prefix_count),
    )
    return pl.pallas_call(
        kernel,
        grid=(tokens // block,),
        in_specs=[
            pl.BlockSpec((block, columns), lambda t: (t, 0)),
            pl.BlockSpec(gathered.shape, lambda t: (0, 0, 0, 0, 0)),
            pl.BlockSpec(stats.shape, lambda t: (0, 0)),
        ],
        out_specs=[
            pl.BlockSpec((block, columns), lambda t: (jnp.minimum(t, half - 1), 0)),
            pl.BlockSpec((block, columns), lambda t: (jnp.maximum(t - half, 0), 0)),
            pl.BlockSpec((2 * size, latents), lambda t: (0, 0)),
        ],
        out_shape=[
            jax.ShapeDtypeStruct((tokens // 2, columns), BF),
            jax.ShapeDtypeStruct((tokens // 2, columns), BF),
            jax.ShapeDtypeStruct((2 * size, latents), BF),
        ],
        scratch_shapes=[
            pltpu.VMEM((latents, 2 * size), BF),
            pltpu.VMEM((latents, 2 * size), BF),
            pltpu.VMEM((2 * size, latents), BF),
            pltpu.VMEM((2 * size, latents), BF),
            pltpu.VMEM((2 * size, latents), F32),
        ],
        compiler_params=pltpu.CompilerParams(vmem_limit_bytes=56 * 2**20),
        cost_estimate=pl.CostEstimate(
            flops=20 * tokens * latents * size,
            bytes_accessed=6 * 2**20,
            transcendentals=2 * tokens * latents,
        ),
    )(kv, gathered, stats)


def tail_kernel(place_ref, query_ref, latent_ref, every_ref, latent_out, mine_out, theirs_out):
    core = place_ref[0]
    count, rows, width = latent_out.shape
    weight = dot_nt(latent_ref[...], every_ref[...]).astype(BF)
    for one, out in enumerate((mine_out, theirs_out)):

        @pl.when(core == 0)
        def _():
            out[...] = weight[one * rows : (one + 1) * rows]

        @pl.when(core == 1)
        def _():
            out[...] = weight[(1 - one) * rows : (2 - one) * rows]

    latent = dot(query_ref[...], every_ref[...]).astype(BF)
    for i in range(count):
        half, group = divmod(i, count // 2)
        latent_out[i] = latent[half * rows : (half + 1) * rows, group * width : (group + 1) * width]


def tail(place, query, latent, every, tensors):
    both, half = query.shape
    rows = both // 2
    latents = latent.shape[1]
    return pl.pallas_call(
        tail_kernel,
        in_specs=[pl.BlockSpec(memory_space=pltpu.SMEM)]
        + [pl.BlockSpec(memory_space=pltpu.VMEM)] * 3,
        out_specs=[pl.BlockSpec(memory_space=pltpu.VMEM)] * 3,
        out_shape=[
            jax.ShapeDtypeStruct((2 * tensors, rows, latents // tensors), BF),
            jax.ShapeDtypeStruct((rows, half), BF),
            jax.ShapeDtypeStruct((rows, half), BF),
        ],
        compiler_params=pltpu.CompilerParams(vmem_limit_bytes=32 * 2**20),
        cost_estimate=pl.CostEstimate(flops=0, bytes_accessed=2**20, transcendentals=0),
    )(place, query, latent, every)


def exchange(x, axes):
    return lax.all_to_all(x, axes, 0, 0, tiled=True)


def halves(x):
    return jnp.transpose(x.reshape(x.shape[0], 2, x.shape[1] // 2), (1, 0, 2))


def local(
    prefix, key_weight, value_weight, query_weight, queries, out_grad, attn_out, shifted_lse, latent_in
):
    core = lax.axis_index("core")
    batch = lax.axis_index("dp")
    first = core == 0
    ranks = lax.axis_size(SEQ)
    batches = lax.axis_size("dp")
    tokens_in = prefix[0]
    token_count = tokens_in.shape[0]
    rows, columns = queries.shape[1:]
    heads = shifted_lse.shape[2]
    size = columns // heads
    latents = rows * ranks

    other_tokens = lax.ppermute(tokens_in, "core", SWAP)
    latent_own = latent_in[0].T
    query_halves = halves(query_weight)
    query_mine = jnp.where(first, query_halves[0], query_halves[1])
    query_theirs = jnp.where(first, query_halves[1], query_halves[0])
    swapped = lax.ppermute(jnp.concatenate([latent_own, query_theirs], axis=1), "core", SWAP)
    latent_other, query_other = swapped[:, :latents], swapped[:, latents:]

    def in_order(own, other):
        return jnp.where(first, jnp.concatenate([own, other], 0), jnp.concatenate([other, own], 0))

    latent_both = in_order(latent_own, latent_other)
    query_both = in_order(query_mine, query_other)

    far = lax.axis_size("zh")
    near = lax.axis_size("zl")
    depth = key_weight.shape[0]
    place = jnp.stack([core, lax.axis_index("zl"), batch]).astype(jnp.int32)
    blocks = pack(
        place, key_weight, value_weight, queries[0], out_grad[0], attn_out[0], shifted_lse[0].T, 2 * far
    )
    landed = exchange(blocks, ("zh", "core"))
    weight_rows, other_rows = unpack(landed, depth, near)
    slab = lax.all_gather(weight_rows, "zl", axis=0, tiled=True)
    slab, other_rows = lax.optimization_barrier((slab, other_rows))
    gathered = exchange(other_rows, "zl").reshape(near, far, 2, -1, size)
    slab = slab.reshape(near, far, 2 * depth, size)
    slabs = [slab] + [
        lax.ppermute(slab, "dp", [(i, (i + d) % batches) for i in range(batches)])
        for d in range(1, batches)
    ]
    stats = gathered[:, :, :, 4 * rows : 4 * rows + 2 * heads, :rows].astype(F32)
    stats = stats[:, :, :, :heads] + stats[:, :, :, heads:]
    stats = jnp.transpose(stats, (3, 1, 0, 2, 4)).reshape(heads, latents)

    kv = project(place, tokens_in, other_tokens, slabs)
    own_grads, other_grads, part = attend(kv, gathered, stats, token_count * ranks)
    theirs = lax.ppermute(other_grads, "core", SWAP)
    half = columns // 2

    def whole(lo):
        mine, other = own_grads[:, lo : lo + half], theirs[:, lo : lo + half]
        return jnp.where(
            first, jnp.concatenate([mine, other], 1), jnp.concatenate([other, mine], 1)
        )[None]

    share = exchange(part.reshape(far * near, -1, latents), ("zh", "zl"))
    share = jnp.sum(share.astype(F32), axis=0).astype(BF)
    every = lax.all_gather(share, ("zh", "zl"), axis=0, tiled=True)
    latent_part, weight_mine, weight_theirs = tail(
        place, query_both, latent_both, every, lax.axis_size("tensor")
    )

    latent_sum = jnp.sum(exchange(latent_part, ("core", "tensor")).astype(F32), axis=0)
    latent_grad = latent_sum.astype(BF).T[None]

    weight_other = lax.ppermute(weight_theirs, "core", SWAP)
    weight_rows = jnp.where(
        first,
        jnp.concatenate([weight_mine, weight_other], 1),
        jnp.concatenate([weight_other, weight_mine], 1),
    )
    weight_sum = jnp.sum(lax.all_gather(weight_rows, "dp").astype(F32), axis=0)
    weight_grad = weight_sum * (1.0 / math.sqrt(latents * batches))
    return (whole(0), whole(half), latent_grad, weight_grad)


def solution(mesh):
    fine = Mesh(
        mesh.devices.reshape(4, 4, 2, *mesh.devices.shape[1:]), SEQ + tuple(mesh.axis_names[1:])
    )
    return jax.shard_map(
        local,
        mesh=fine,
        in_specs=(
            P("dp", SEQ, None),
            P(SEQ, "tensor"),
            P(SEQ, "tensor"),
            P(SEQ, "tensor"),
            P("dp", SEQ, "tensor"),
            P("dp", SEQ, "tensor"),
            P("dp", SEQ, "tensor"),
            P("dp", SEQ, "tensor"),
            P("dp", None, SEQ),
        ),
        out_specs=(
            P("dp", SEQ, "tensor"),
            P("dp", SEQ, "tensor"),
            P("dp", "tensor", SEQ),
            P(SEQ, "tensor"),
        ),
        check_vma=False,
    )
```

```python
import functools
import math

import jax
import jax.numpy as jnp
from jax import lax
from jax.experimental import pallas as pl
from jax.experimental.pallas import tpu as pltpu
from jax.sharding import Mesh, PartitionSpec as P

BF = jnp.bfloat16
F32 = jnp.float32
SEQ = ("zh", "zl", "core")
Z = ("zh", "zl")
SWAP = [(0, 1), (1, 0)]


def dot(a, b):
    return jnp.dot(a, b, preferred_element_type=F32)


def dot_nt(a, b):
    return lax.dot_general(a, b, (((1,), (1,)), ((), ())), preferred_element_type=F32)


def pack_kernel(place_ref, *refs):
    sources, block_ref, landing, arrived = refs[:6], refs[6], refs[7:13], refs[13]
    copies = [
        pltpu.make_async_copy(source, target, arrived.at[i])
        for i, (source, target) in enumerate(zip(sources, landing))
    ]
    for copy in copies:
        copy.start()
    for copy in copies:
        copy.wait()
    key_ref, value_ref, query_ref, grad_ref, out_ref, lse_ref = landing
    batch = place_ref[2]
    depth, columns = key_ref.shape
    rows = query_ref.shape[0]
    size = block_ref.shape[2]
    heads = columns // size
    half = columns // 2
    product = grad_ref[...].astype(F32) * out_ref[...].astype(F32)
    lane = lax.broadcasted_iota(jnp.int32, (rows, size), 1)
    delta = jnp.zeros((rows, size), F32)
    for head in range(heads):
        one = jnp.sum(product[:, head * size : (head + 1) * size], axis=1, keepdims=True)
        delta = jnp.where(lane == head, one, delta)
    lse, delta = lse_ref[...], delta.T[:heads]
    for core in range(2):
        column = pl.multiple_of(core * half + lax.rem(batch, 2) * size, size)
        mine = slice(core * heads // 2, (core + 1) * heads // 2)
        exact = jnp.concatenate([lse[mine], delta[mine]], axis=0)
        high = exact.astype(BF).astype(F32)
        stats = jnp.concatenate([high, exact - high], axis=0).astype(BF)

        @pl.when(batch < 2)
        def _():
            block_ref[core, :depth] = key_ref[:, pl.ds(column, size)]

        @pl.when(batch >= 2)
        def _():
            block_ref[core, :depth] = value_ref[:, pl.ds(column, size)]

        first = depth
        for ref in (query_ref, grad_ref):
            for lo in range(core * half, (core + 1) * half, size):
                block_ref[core, first : first + rows] = ref[:, lo : lo + size]
                first += rows
                if first == depth + rows:
                    block_ref[core, first : first + 16] = jnp.zeros((16, size), BF)
                    block_ref[core, first : first + 2 * heads, :rows] = stats
                    first += 16


def pack(place, key_weight, value_weight, query, grad, out, lse):
    depth, columns = key_weight.shape
    size = columns // lse.shape[0]
    sources = (key_weight, value_weight, query, grad, out, lse)
    return pl.pallas_call(
        pack_kernel,
        in_specs=[pl.BlockSpec(memory_space=pltpu.SMEM)]
        + [pl.BlockSpec(memory_space=pltpu.HBM)] * len(sources),
        out_specs=pl.BlockSpec(memory_space=pltpu.VMEM),
        out_shape=jax.ShapeDtypeStruct((2, depth + 16 + 4 * query.shape[0], size), BF),
        scratch_shapes=[pltpu.VMEM(x.shape, x.dtype) for x in sources]
        + [pltpu.SemaphoreType.DMA((len(sources),))],
        compiler_params=pltpu.CompilerParams(vmem_limit_bytes=60 * 2**20),
        cost_estimate=pl.CostEstimate(flops=0, bytes_accessed=2**19, transcendentals=0),
    )(place, *sources)


def project_kernel(own_ref, other_ref, slab_ref, out_ref, weight):
    step = pl.program_id(0)
    half = pl.num_programs(0) // 2
    slabs, _, size = slab_ref.shape

    @pl.when(step == 0)
    def _():
        for slab in range(slabs):
            weight[:, slab * size : (slab + 1) * size] = slab_ref[slab]

    @pl.when(step < half)
    def _():
        out_ref[...] = dot(own_ref[...], weight[...]).astype(BF)

    @pl.when(step >= half)
    def _():
        out_ref[...] = dot(other_ref[...], weight[...]).astype(BF)


def project(own, other, slabs):
    rows, width = own.shape
    columns = slabs.shape[0] * slabs.shape[2]
    block = 256
    half = rows // block
    return pl.pallas_call(
        project_kernel,
        grid=(2 * half,),
        in_specs=[
            pl.BlockSpec((block, width), lambda t: (jnp.minimum(t, half - 1), 0)),
            pl.BlockSpec((block, width), lambda t: (jnp.maximum(t - half, 0), 0)),
            pl.BlockSpec(slabs.shape, lambda t: (0, 0, 0)),
        ],
        out_specs=pl.BlockSpec((block, columns), lambda t: (t, 0)),
        out_shape=jax.ShapeDtypeStruct((2 * rows, columns), BF),
        scratch_shapes=[pltpu.VMEM((width, columns), BF)],
        compiler_params=pltpu.CompilerParams(vmem_limit_bytes=32 * 2**20),
        cost_estimate=pl.CostEstimate(flops=0, bytes_accessed=2**20, transcendentals=0),
    )(own, other, slabs)


def attend_kernel(
    kv_ref, head_ref, stat_ref, rest_ref, own_ref, other_ref, part_ref, query, grad, qt, gt, pieces, stats, total,
    size, scaling, latent_factor, prefix_factor,
):
    step = pl.program_id(0)
    last = pl.num_programs(0) - 1
    half = pl.num_programs(0) // 2
    ranks = head_ref.shape[0]
    rows = query.shape[0] // ranks

    @pl.when(step == 0)
    def _():
        for rank in range(ranks):
            here = slice(rank * rows, (rank + 1) * rows)
            query[here, :size] = head_ref[rank]
            query[here, size:] = rest_ref[rank, :rows]
            grad[here, :size] = rest_ref[rank, rows : 2 * rows]
            grad[here, size:] = rest_ref[rank, 2 * rows :]
            pieces[:, here] = stat_ref[rank].astype(F32)[:8, :rows]
        stats[...] = pieces[:4] + pieces[4:]
        qt[...] = query[...].T
        gt[...] = grad[...].T
        total[...] = jnp.zeros_like(total)

    key_out, value_out = [], []
    for head in range(2):
        cols = slice(head * size, (head + 1) * size)
        keys = kv_ref[:, cols]
        values = kv_ref[:, (2 + head) * size : (3 + head) * size]
        scores = dot(keys, qt[cols, :]) * scaling
        weights = jnp.exp(scores - stats[head : head + 1, :])
        probs = dot(values, gt[cols, :])
        score_grad = (weights * (probs - stats[2 + head : 3 + head, :])).astype(BF)
        value_out.append(dot(weights.astype(BF), grad[:, cols]) * latent_factor)
        key_out.append(dot(score_grad, query[:, cols]) * (scaling * latent_factor))
        total[cols, :] += dot(keys.T, score_grad)
    result = jnp.concatenate(key_out + value_out, axis=1).astype(BF)

    @pl.when(step < half)
    def _():
        own_ref[...] = result

    @pl.when(step >= half)
    def _():
        other_ref[...] = result

    @pl.when(step == last)
    def _():
        part_ref[...] = (total[...] * (scaling * prefix_factor)).astype(BF)


def attend(kv, first_rows, last_rows, latents, prefix_count):
    tokens, columns = kv.shape
    ranks = first_rows.shape[0]
    rows = latents // ranks
    depth = first_rows.shape[1] - 16 - rows
    size = columns // 4
    block = 256
    half = tokens // block // 2
    kernel = functools.partial(
        attend_kernel,
        size=size,
        scaling=1.0 / math.sqrt(size),
        latent_factor=1.0 / math.sqrt(latents),
        prefix_factor=1.0 / math.sqrt(prefix_count),
    )
    return pl.pallas_call(
        kernel,
        grid=(tokens // block,),
        in_specs=[
            pl.BlockSpec((block, columns), lambda t: (t, 0)),
            pl.BlockSpec((ranks, rows, size), lambda t: (0, depth // rows, 0)),
            pl.BlockSpec((ranks, 16, size), lambda t: (0, (depth + rows) // 16, 0)),
            pl.BlockSpec(last_rows.shape, lambda t: (0, 0, 0)),
        ],
        out_specs=[
            pl.BlockSpec((block, columns), lambda t: (jnp.minimum(t, half - 1), 0)),
            pl.BlockSpec((block, columns), lambda t: (jnp.maximum(t - half, 0), 0)),
            pl.BlockSpec((2 * size, latents), lambda t: (0, 0)),
        ],
        out_shape=[
            jax.ShapeDtypeStruct((tokens // 2, columns), BF),
            jax.ShapeDtypeStruct((tokens // 2, columns), BF),
            jax.ShapeDtypeStruct((2 * size, latents), BF),
        ],
        scratch_shapes=[
            pltpu.VMEM((latents, 2 * size), BF),
            pltpu.VMEM((latents, 2 * size), BF),
            pltpu.VMEM((2 * size, latents), BF),
            pltpu.VMEM((2 * size, latents), BF),
            pltpu.VMEM((8, latents), F32),
            pltpu.VMEM((4, latents), F32),
            pltpu.VMEM((2 * size, latents), F32),
        ],
        compiler_params=pltpu.CompilerParams(vmem_limit_bytes=56 * 2**20),
        cost_estimate=pl.CostEstimate(
            flops=20 * tokens * latents * size,
            bytes_accessed=6 * 2**20,
            transcendentals=2 * tokens * latents,
        ),
    )(kv, first_rows, first_rows, last_rows)


def tail_kernel(query_ref, latent_ref, every_ref, latent_out, weight_out):
    count, rows, width = latent_out.shape
    weight_out[...] = dot_nt(latent_ref[...], every_ref[...]).astype(BF)
    latent = dot(query_ref[...], every_ref[...]).astype(BF)
    for i in range(count):
        half, group = divmod(i, count // 2)
        latent_out[i] = latent[half * rows : (half + 1) * rows, group * width : (group + 1) * width]


def tail(query, latent, every, tensors):
    both, half = query.shape
    latents = latent.shape[1]
    return pl.pallas_call(
        tail_kernel,
        in_specs=[pl.BlockSpec(memory_space=pltpu.VMEM)] * 3,
        out_specs=[pl.BlockSpec(memory_space=pltpu.VMEM)] * 2,
        out_shape=[
            jax.ShapeDtypeStruct((2 * tensors, both // 2, latents // tensors), BF),
            jax.ShapeDtypeStruct((both, half), BF),
        ],
        compiler_params=pltpu.CompilerParams(vmem_limit_bytes=32 * 2**20),
        cost_estimate=pl.CostEstimate(flops=0, bytes_accessed=2**20, transcendentals=0),
    )(query, latent, every)


def total_kernel(place_ref, part_ref, out_ref, *, factor):
    rows = out_ref.shape[0]
    here = pl.ds(pl.multiple_of(place_ref[0] * rows, rows), rows)
    count, _, width = part_ref.shape
    for half in range(2):
        parts = [part_ref[i, here, :].astype(F32) for i in range(half * count // 2, (half + 1) * count // 2)]
        out_ref[:, half * width : (half + 1) * width] = sum(parts[1:], parts[0]) * factor


def total(place, parts, factor):
    _, rows, width = parts.shape
    return pl.pallas_call(
        functools.partial(total_kernel, factor=factor),
        in_specs=[pl.BlockSpec(memory_space=pltpu.SMEM), pl.BlockSpec(memory_space=pltpu.VMEM)],
        out_specs=pl.BlockSpec(memory_space=pltpu.VMEM),
        out_shape=jax.ShapeDtypeStruct((rows // 2, 2 * width), F32),
        compiler_params=pltpu.CompilerParams(vmem_limit_bytes=32 * 2**20),
        cost_estimate=pl.CostEstimate(flops=0, bytes_accessed=2**10, transcendentals=0),
    )(place, parts)


def exchange(x, axes):
    return lax.all_to_all(x, axes, 0, 0, tiled=True)


def halves(x):
    return jnp.transpose(x.reshape(x.shape[0], 2, x.shape[1] // 2), (1, 0, 2))


def local(
    prefix, key_weight, value_weight, query_weight, queries, out_grad, attn_out, shifted_lse, latent_in
):
    core = lax.axis_index("core")
    batch = lax.axis_index("dp")
    first = core == 0
    ranks = lax.axis_size(SEQ)
    batches = lax.axis_size("dp")
    tokens_in = prefix[0]
    token_count = tokens_in.shape[0]
    rows, columns = queries.shape[1:]
    heads = shifted_lse.shape[2]
    size = columns // heads
    latents = rows * ranks

    other_tokens = lax.ppermute(tokens_in, "core", SWAP)
    latent_own = latent_in[0].T
    query_halves = halves(query_weight)
    query_mine = jnp.where(first, query_halves[0], query_halves[1])
    query_theirs = jnp.where(first, query_halves[1], query_halves[0])
    swapped = lax.ppermute(jnp.concatenate([latent_own, query_theirs], axis=1), "core", SWAP)
    latent_other, query_other = swapped[:, :latents], swapped[:, latents:]

    def in_order(own, other):
        return jnp.where(first, jnp.concatenate([own, other], 0), jnp.concatenate([other, own], 0))

    latent_both = in_order(latent_own, latent_other)
    query_both = in_order(query_mine, query_other)

    depth = key_weight.shape[0]
    place = jnp.stack([core, lax.axis_index("zl"), batch]).astype(jnp.int32)
    blocks = exchange(
        pack(place, key_weight, value_weight, queries[0], out_grad[0], attn_out[0], shifted_lse[0].T), "core"
    )
    cut = depth + 16 + rows
    first_rows = lax.all_gather(blocks[:, :cut], Z, axis=0, tiled=True)
    slab = first_rows[:, :depth].reshape(-1, size)
    slabs = jnp.broadcast_to(slab[None], (batches,) + slab.shape)
    slabs, rest = lax.optimization_barrier((slabs, blocks[:, cut:]))
    slabs = exchange(slabs, "dp")
    last_rows = lax.all_gather(rest, Z, axis=0, tiled=True)

    kv = project(tokens_in, other_tokens, slabs)
    own_grads, other_grads, part = attend(kv, first_rows, last_rows, latents, token_count * ranks)
    theirs = lax.ppermute(other_grads, "core", SWAP)
    half = columns // 2

    def whole(lo):
        mine, other = own_grads[:, lo : lo + half], theirs[:, lo : lo + half]
        return jnp.where(
            first, jnp.concatenate([mine, other], 1), jnp.concatenate([other, mine], 1)
        )[None]

    share = exchange(part.reshape(lax.axis_size(Z), -1, latents), Z)
    share = jnp.sum(share.astype(F32), axis=0).astype(BF)
    every = lax.all_gather(share, Z, axis=0, tiled=True)
    latent_part, weight_part = tail(query_both, latent_both, every, lax.axis_size("tensor"))

    latent_sum = jnp.sum(exchange(latent_part, ("core", "tensor")).astype(F32), axis=0)
    latent_grad = latent_sum.astype(BF).T[None]

    weight_parts = lax.all_gather(weight_part, ("core", "dp"))
    weight_grad = total(place, weight_parts, 1.0 / math.sqrt(latents * batches))
    return (whole(0), whole(half), latent_grad, weight_grad)


def solution(mesh):
    fine = Mesh(
        mesh.devices.reshape(4, 4, 2, *mesh.devices.shape[1:]), SEQ + tuple(mesh.axis_names[1:])
    )
    return jax.shard_map(
        local,
        mesh=fine,
        in_specs=(
            P("dp", SEQ, None),
            P(SEQ, "tensor"),
            P(SEQ, "tensor"),
            P(SEQ, "tensor"),
            P("dp", SEQ, "tensor"),
            P("dp", SEQ, "tensor"),
            P("dp", SEQ, "tensor"),
            P("dp", SEQ, "tensor"),
            P("dp", None, SEQ),
        ),
        out_specs=(
            P("dp", SEQ, "tensor"),
            P("dp", SEQ, "tensor"),
            P("dp", "tensor", SEQ),
            P(SEQ, "tensor"),
        ),
        check_vma=False,
    )
```

```python
import functools
import math

import jax
import jax.numpy as jnp
from jax import lax
from jax.experimental import pallas as pl
from jax.experimental.pallas import tpu as pltpu
from jax.sharding import Mesh, PartitionSpec as P

BF = jnp.bfloat16
F32 = jnp.float32
SEQ = ("zh", "zl", "core")
Z = ("zh", "zl")
SWAP = [(0, 1), (1, 0)]


def dot(a, b):
    return jnp.dot(a, b, preferred_element_type=F32)


def dot_nt(a, b):
    return lax.dot_general(a, b, (((1,), (1,)), ((), ())), preferred_element_type=F32)


def pack_kernel(place_ref, *refs):
    sources, block_ref, landing, arrived = refs[:6], refs[6], refs[7:13], refs[13]
    copies = [
        pltpu.make_async_copy(source, target, arrived.at[i])
        for i, (source, target) in enumerate(zip(sources, landing))
    ]
    for copy in copies:
        copy.start()
    for copy in copies:
        copy.wait()
    key_ref, value_ref, query_ref, grad_ref, out_ref, lse_ref = landing
    batch = place_ref[2]
    depth, columns = key_ref.shape
    rows = query_ref.shape[0]
    size = block_ref.shape[2]
    heads = columns // size
    half = columns // 2
    product = grad_ref[...].astype(F32) * out_ref[...].astype(F32)
    lane = lax.broadcasted_iota(jnp.int32, (rows, size), 1)
    delta = jnp.zeros((rows, size), F32)
    for head in range(heads):
        one = jnp.sum(product[:, head * size : (head + 1) * size], axis=1, keepdims=True)
        delta = jnp.where(lane == head, one, delta)
    lse, delta = lse_ref[...], delta.T[:heads]
    for core in range(2):
        column = pl.multiple_of(core * half + lax.rem(batch, 2) * size, size)
        mine = slice(core * heads // 2, (core + 1) * heads // 2)
        exact = jnp.concatenate([lse[mine], delta[mine]], axis=0)
        high = exact.astype(BF).astype(F32)
        stats = jnp.concatenate([high, exact - high], axis=0).astype(BF)

        @pl.when(batch < 2)
        def _():
            block_ref[core, :depth] = key_ref[:, pl.ds(column, size)]

        @pl.when(batch >= 2)
        def _():
            block_ref[core, :depth] = value_ref[:, pl.ds(column, size)]

        first = depth
        for ref in (query_ref, grad_ref):
            for lo in range(core * half, (core + 1) * half, size):
                block_ref[core, first : first + rows] = ref[:, lo : lo + size]
                first += rows
                if first == depth + rows:
                    block_ref[core, first : first + 16] = jnp.zeros((16, size), BF)
                    block_ref[core, first : first + 2 * heads, :rows] = stats
                    first += 16


def pack(place, key_weight, value_weight, query, grad, out, lse):
    depth, columns = key_weight.shape
    size = columns // lse.shape[0]
    sources = (key_weight, value_weight, query, grad, out, lse)
    return pl.pallas_call(
        pack_kernel,
        in_specs=[pl.BlockSpec(memory_space=pltpu.SMEM)]
        + [pl.BlockSpec(memory_space=pltpu.HBM)] * len(sources),
        out_specs=pl.BlockSpec(memory_space=pltpu.VMEM),
        out_shape=jax.ShapeDtypeStruct((2, depth + 16 + 4 * query.shape[0], size), BF),
        scratch_shapes=[pltpu.VMEM(x.shape, x.dtype) for x in sources]
        + [pltpu.SemaphoreType.DMA((len(sources),))],
        compiler_params=pltpu.CompilerParams(vmem_limit_bytes=60 * 2**20),
        cost_estimate=pl.CostEstimate(flops=0, bytes_accessed=2**19, transcendentals=0),
    )(place, *sources)


def attend_kernel(
    own_in, other_in, slab_ref, head_ref, stat_ref, rest_ref, own_ref, other_ref, part_ref,
    weight, kv, query, grad, qt, gt, pieces, stats, total,
    size, scaling, latent_factor, prefix_factor,
):
    step = pl.program_id(0)
    last = pl.num_programs(0) - 1
    half = pl.num_programs(0) // 2
    ranks = head_ref.shape[0]
    rows = query.shape[0] // ranks

    @pl.when(step == 0)
    def _():
        for slab in range(slab_ref.shape[0]):
            weight[:, slab * size : (slab + 1) * size] = slab_ref[slab]
        for rank in range(ranks):
            here = slice(rank * rows, (rank + 1) * rows)
            query[here, :size] = head_ref[rank]
            query[here, size:] = rest_ref[rank, :rows]
            grad[here, :size] = rest_ref[rank, rows : 2 * rows]
            grad[here, size:] = rest_ref[rank, 2 * rows :]
            pieces[:, here] = stat_ref[rank].astype(F32)[:8, :rows]
        stats[...] = pieces[:4] + pieces[4:]
        qt[...] = query[...].T
        gt[...] = grad[...].T
        total[...] = jnp.zeros_like(total)

    @pl.when(step < half)
    def _():
        kv[...] = dot(own_in[...], weight[...]).astype(BF)

    @pl.when(step >= half)
    def _():
        kv[...] = dot(other_in[...], weight[...]).astype(BF)

    key_out, value_out = [], []
    for head in range(2):
        cols = slice(head * size, (head + 1) * size)
        keys = kv[:, cols]
        values = kv[:, (2 + head) * size : (3 + head) * size]
        scores = dot(keys, qt[cols, :]) * scaling
        weights = jnp.exp(scores - stats[head : head + 1, :])
        probs = dot(values, gt[cols, :])
        score_grad = (weights * (probs - stats[2 + head : 3 + head, :])).astype(BF)
        value_out.append(dot(weights.astype(BF), grad[:, cols]) * latent_factor)
        key_out.append(dot(score_grad, query[:, cols]) * (scaling * latent_factor))
        total[cols, :] += dot(keys.T, score_grad)
    result = jnp.concatenate(key_out + value_out, axis=1).astype(BF)

    @pl.when(step < half)
    def _():
        own_ref[...] = result

    @pl.when(step >= half)
    def _():
        other_ref[...] = result

    @pl.when(step == last)
    def _():
        part_ref[...] = (total[...] * (scaling * prefix_factor)).astype(BF)


def attend(own, other, slabs, first_rows, last_rows, latents, prefix_count):
    tokens, width = own.shape
    count, _, size = slabs.shape
    columns = count * size
    ranks = first_rows.shape[0]
    rows = latents // ranks
    depth = first_rows.shape[1] - 16 - rows
    block = 256
    half = tokens // block
    kernel = functools.partial(
        attend_kernel,
        size=size,
        scaling=1.0 / math.sqrt(size),
        latent_factor=1.0 / math.sqrt(latents),
        prefix_factor=1.0 / math.sqrt(prefix_count),
    )
    return pl.pallas_call(
        kernel,
        grid=(2 * half,),
        in_specs=[
            pl.BlockSpec((block, width), lambda t: (jnp.minimum(t, half - 1), 0)),
            pl.BlockSpec((block, width), lambda t: (jnp.maximum(t - half, 0), 0)),
            pl.BlockSpec(slabs.shape, lambda t: (0, 0, 0)),
            pl.BlockSpec((ranks, rows, size), lambda t: (0, depth // rows, 0)),
            pl.BlockSpec((ranks, 16, size), lambda t: (0, (depth + rows) // 16, 0)),
            pl.BlockSpec(last_rows.shape, lambda t: (0, 0, 0)),
        ],
        out_specs=[
            pl.BlockSpec((block, columns), lambda t: (jnp.minimum(t, half - 1), 0)),
            pl.BlockSpec((block, columns), lambda t: (jnp.maximum(t - half, 0), 0)),
            pl.BlockSpec((2 * size, latents), lambda t: (0, 0)),
        ],
        out_shape=[
            jax.ShapeDtypeStruct((tokens, columns), BF),
            jax.ShapeDtypeStruct((tokens, columns), BF),
            jax.ShapeDtypeStruct((2 * size, latents), BF),
        ],
        scratch_shapes=[
            pltpu.VMEM((width, columns), BF),
            pltpu.VMEM((block, columns), BF),
            pltpu.VMEM((latents, 2 * size), BF),
            pltpu.VMEM((latents, 2 * size), BF),
            pltpu.VMEM((2 * size, latents), BF),
            pltpu.VMEM((2 * size, latents), BF),
            pltpu.VMEM((8, latents), F32),
            pltpu.VMEM((4, latents), F32),
            pltpu.VMEM((2 * size, latents), F32),
        ],
        compiler_params=pltpu.CompilerParams(vmem_limit_bytes=52 * 2**20),
        cost_estimate=pl.CostEstimate(
            flops=40 * tokens * latents * size,
            bytes_accessed=6 * 2**20,
            transcendentals=4 * tokens * latents,
        ),
    )(own, other, slabs, first_rows, first_rows, last_rows)


def tail_kernel(place_ref, query_ref, latent_ref, every_ref, latent_out, mine_out, theirs_out):
    core = place_ref[0]
    count, rows, width = latent_out.shape
    weight = dot_nt(latent_ref[...], every_ref[...]).astype(BF)
    for one, out in enumerate((mine_out, theirs_out)):

        @pl.when(core == 0)
        def _():
            out[...] = weight[one * rows : (one + 1) * rows]

        @pl.when(core == 1)
        def _():
            out[...] = weight[(1 - one) * rows : (2 - one) * rows]

    latent = dot(query_ref[...], every_ref[...]).astype(BF)
    for i in range(count):
        half, group = divmod(i, count // 2)
        latent_out[i] = latent[half * rows : (half + 1) * rows, group * width : (group + 1) * width]


def tail(place, query, latent, every, tensors):
    both, half = query.shape
    rows = both // 2
    latents = latent.shape[1]
    return pl.pallas_call(
        tail_kernel,
        in_specs=[pl.BlockSpec(memory_space=pltpu.SMEM)]
        + [pl.BlockSpec(memory_space=pltpu.VMEM)] * 3,
        out_specs=[pl.BlockSpec(memory_space=pltpu.VMEM)] * 3,
        out_shape=[
            jax.ShapeDtypeStruct((2 * tensors, rows, latents // tensors), BF),
            jax.ShapeDtypeStruct((rows, half), BF),
            jax.ShapeDtypeStruct((rows, half), BF),
        ],
        compiler_params=pltpu.CompilerParams(vmem_limit_bytes=32 * 2**20),
        cost_estimate=pl.CostEstimate(flops=0, bytes_accessed=2**20, transcendentals=0),
    )(place, query, latent, every)


def total_kernel(part_ref, out_ref, *, factor):
    parts = [part_ref[i].astype(F32) for i in range(part_ref.shape[0])]
    out_ref[...] = sum(parts[1:], parts[0]) * factor


def total(parts, factor):
    return pl.pallas_call(
        functools.partial(total_kernel, factor=factor),
        in_specs=[pl.BlockSpec(memory_space=pltpu.VMEM)],
        out_specs=pl.BlockSpec(memory_space=pltpu.VMEM),
        out_shape=jax.ShapeDtypeStruct(parts.shape[1:], F32),
        compiler_params=pltpu.CompilerParams(vmem_limit_bytes=32 * 2**20),
        cost_estimate=pl.CostEstimate(flops=0, bytes_accessed=2**10, transcendentals=0),
    )(parts)


def exchange(x, axes):
    return lax.all_to_all(x, axes, 0, 0, tiled=True)


def halves(x):
    return jnp.transpose(x.reshape(x.shape[0], 2, x.shape[1] // 2), (1, 0, 2))


def local(
    prefix, key_weight, value_weight, query_weight, queries, out_grad, attn_out, shifted_lse, latent_in
):
    core = lax.axis_index("core")
    batch = lax.axis_index("dp")
    first = core == 0
    ranks = lax.axis_size(SEQ)
    batches = lax.axis_size("dp")
    tokens_in = prefix[0]
    token_count = tokens_in.shape[0]
    rows, columns = queries.shape[1:]
    heads = shifted_lse.shape[2]
    size = columns // heads
    latents = rows * ranks

    other_tokens = lax.ppermute(tokens_in, "core", SWAP)
    latent_own = latent_in[0].T
    query_halves = halves(query_weight)
    query_mine = jnp.where(first, query_halves[0], query_halves[1])
    query_theirs = jnp.where(first, query_halves[1], query_halves[0])
    swapped = lax.ppermute(jnp.concatenate([latent_own, query_theirs], axis=1), "core", SWAP)
    latent_other, query_other = swapped[:, :latents], swapped[:, latents:]

    def in_order(own, other):
        return jnp.where(first, jnp.concatenate([own, other], 0), jnp.concatenate([other, own], 0))

    latent_both = in_order(latent_own, latent_other)
    query_both = in_order(query_mine, query_other)

    depth = key_weight.shape[0]
    place = jnp.stack([core, lax.axis_index("zl"), batch]).astype(jnp.int32)
    blocks = exchange(
        pack(place, key_weight, value_weight, queries[0], out_grad[0], attn_out[0], shifted_lse[0].T), "core"
    )
    cut = depth + 16 + rows
    first_rows = lax.all_gather(blocks[:, :cut], Z, axis=0, tiled=True)
    slab = first_rows[:, :depth].reshape(-1, size)
    slabs = jnp.broadcast_to(slab[None], (batches,) + slab.shape)
    slabs, rest = lax.optimization_barrier((slabs, blocks[:, cut:]))
    slabs = exchange(slabs, "dp")
    last_rows = lax.all_gather(rest, Z, axis=0, tiled=True)

    own_grads, other_grads, part = attend(
        tokens_in, other_tokens, slabs, first_rows, last_rows, latents, token_count * ranks
    )
    theirs = lax.ppermute(other_grads, "core", SWAP)
    half = columns // 2

    def whole(lo):
        mine, other = own_grads[:, lo : lo + half], theirs[:, lo : lo + half]
        return jnp.where(
            first, jnp.concatenate([mine, other], 1), jnp.concatenate([other, mine], 1)
        )[None]

    share = exchange(part.reshape(lax.axis_size(Z), -1, latents), Z)
    share = jnp.sum(share.astype(F32), axis=0).astype(BF)
    every = lax.all_gather(share, Z, axis=0, tiled=True)
    latent_part, weight_mine, weight_theirs = tail(
        place, query_both, latent_both, every, lax.axis_size("tensor")
    )

    latent_sum = jnp.sum(exchange(latent_part, ("core", "tensor")).astype(F32), axis=0)
    latent_grad = latent_sum.astype(BF).T[None]

    weight_other = lax.ppermute(weight_theirs, "core", SWAP)
    weight_rows = jnp.where(
        first,
        jnp.concatenate([weight_mine, weight_other], 1),
        jnp.concatenate([weight_other, weight_mine], 1),
    )
    weight_grad = total(
        lax.all_gather(weight_rows, "dp"), 1.0 / math.sqrt(latents * batches)
    )
    return (whole(0), whole(half), latent_grad, weight_grad)


def solution(mesh):
    fine = Mesh(
        mesh.devices.reshape(4, 4, 2, *mesh.devices.shape[1:]), SEQ + tuple(mesh.axis_names[1:])
    )
    return jax.shard_map(
        local,
        mesh=fine,
        in_specs=(
            P("dp", SEQ, None),
            P(SEQ, "tensor"),
            P(SEQ, "tensor"),
            P(SEQ, "tensor"),
            P("dp", SEQ, "tensor"),
            P("dp", SEQ, "tensor"),
            P("dp", SEQ, "tensor"),
            P("dp", SEQ, "tensor"),
            P("dp", None, SEQ),
        ),
        out_specs=(
            P("dp", SEQ, "tensor"),
            P("dp", SEQ, "tensor"),
            P("dp", "tensor", SEQ),
            P(SEQ, "tensor"),
        ),
        check_vma=False,
    )
```

```python
import functools
import math

import jax
import jax.numpy as jnp
from jax import lax
from jax.experimental import pallas as pl
from jax.experimental.pallas import tpu as pltpu
from jax.sharding import Mesh, PartitionSpec as P

BF = jnp.bfloat16
F32 = jnp.float32
SEQ = ("zh", "zl", "core")
Z = ("zh", "zl")
SWAP = [(0, 1), (1, 0)]


def dot(a, b):
    return jnp.dot(a, b, preferred_element_type=F32)


def dot_nt(a, b):
    return lax.dot_general(a, b, (((1,), (1,)), ((), ())), preferred_element_type=F32)


def pack_kernel(place_ref, *refs):
    sources, outs, landing, arrived = refs[:6], refs[6:8], refs[8:14], refs[14]
    copies = [
        pltpu.make_async_copy(source, target, arrived.at[i])
        for i, (source, target) in enumerate(zip(sources, landing))
    ]
    for copy in copies:
        copy.start()
    for copy in copies:
        copy.wait()
    key_ref, value_ref, query_ref, grad_ref, out_ref, lse_ref = landing
    batch = place_ref[1]
    depth, columns = key_ref.shape
    rows = query_ref.shape[0]
    size = outs[0].shape[1]
    heads = columns // size
    half = columns // 2
    product = grad_ref[...].astype(F32) * out_ref[...].astype(F32)
    lane = lax.broadcasted_iota(jnp.int32, (rows, size), 1)
    delta = jnp.zeros((rows, size), F32)
    for head in range(heads):
        one = jnp.sum(product[:, head * size : (head + 1) * size], axis=1, keepdims=True)
        delta = jnp.where(lane == head, one, delta)
    lse, delta = lse_ref[...], delta.T[:heads]
    exact = [
        jnp.concatenate([lse[lo : lo + heads // 2], delta[lo : lo + heads // 2]], axis=0)
        for lo in (0, heads // 2)
    ]
    for other, block_ref in enumerate(outs):
        core = lax.rem(place_ref[0] + other, 2)
        column = pl.multiple_of(core * half + lax.rem(batch, 2) * size, size)
        mine = jnp.where(core == 0, exact[0], exact[1])
        high = mine.astype(BF).astype(F32)
        stats = jnp.concatenate([high, mine - high], axis=0).astype(BF)

        @pl.when(batch < 2)
        def _():
            block_ref[:depth] = key_ref[:, pl.ds(column, size)]

        @pl.when(batch >= 2)
        def _():
            block_ref[:depth] = value_ref[:, pl.ds(column, size)]

        first = depth
        for ref in (query_ref, grad_ref):
            for lo in range(0, half, size):
                here = pl.ds(pl.multiple_of(core * half + lo, size), size)
                block_ref[first : first + rows] = ref[:, here]
                first += rows
                if first == depth + rows:
                    block_ref[first : first + 16] = jnp.zeros((16, size), BF)
                    block_ref[first : first + 2 * heads, :rows] = stats
                    first += 16


def pack(place, key_weight, value_weight, query, grad, out, lse):
    depth, columns = key_weight.shape
    size = columns // lse.shape[0]
    sources = (key_weight, value_weight, query, grad, out, lse)
    return pl.pallas_call(
        pack_kernel,
        in_specs=[pl.BlockSpec(memory_space=pltpu.SMEM)]
        + [pl.BlockSpec(memory_space=pltpu.HBM)] * len(sources),
        out_specs=[pl.BlockSpec(memory_space=pltpu.VMEM)] * 2,
        out_shape=[jax.ShapeDtypeStruct((depth + 16 + 4 * query.shape[0], size), BF)] * 2,
        scratch_shapes=[pltpu.VMEM(x.shape, x.dtype) for x in sources]
        + [pltpu.SemaphoreType.DMA((len(sources),))],
        compiler_params=pltpu.CompilerParams(vmem_limit_bytes=60 * 2**20),
        cost_estimate=pl.CostEstimate(flops=0, bytes_accessed=2**19, transcendentals=0),
    )(place, *sources)


def attend_kernel(
    place_ref, own_in, other_in, slab_ref, head_ref, stat_ref, rest_ref, own_ref, other_ref, part_ref,
    weight, kv, query, grad, qt, gt, pieces, stats, total,
    size, scaling, latent_factor, prefix_factor,
):
    step = pl.program_id(0)
    last = pl.num_programs(0) - 1
    half = pl.num_programs(0) // 2
    ranks = head_ref.shape[0]
    rows = query.shape[0] // ranks

    @pl.when(step == 0)
    def _():
        depth = weight.shape[0] // ranks
        for rank in range(ranks):
            at = rank - rank % 2 + lax.rem(rank + place_ref[0], 2)
            there = pl.ds(pl.multiple_of(at * depth, depth), depth)
            for slab in range(slab_ref.shape[0]):
                weight[rank * depth : (rank + 1) * depth, slab * size : (slab + 1) * size] = slab_ref[
                    slab, there
                ]
            here = slice(rank * rows, (rank + 1) * rows)
            query[here, :size] = head_ref[at]
            query[here, size:] = rest_ref[at, :rows]
            grad[here, :size] = rest_ref[at, rows : 2 * rows]
            grad[here, size:] = rest_ref[at, 2 * rows :]
            pieces[:, here] = stat_ref[at].astype(F32)[:8, :rows]
        stats[...] = pieces[:4] + pieces[4:]
        qt[...] = query[...].T
        gt[...] = grad[...].T
        total[...] = jnp.zeros_like(total)

    @pl.when(step < half)
    def _():
        kv[...] = dot(own_in[...], weight[...]).astype(BF)

    @pl.when(step >= half)
    def _():
        kv[...] = dot(other_in[...], weight[...]).astype(BF)

    key_out, value_out = [], []
    for head in range(2):
        cols = slice(head * size, (head + 1) * size)
        keys = kv[:, cols]
        values = kv[:, (2 + head) * size : (3 + head) * size]
        scores = dot(keys, qt[cols, :]) * scaling
        weights = jnp.exp(scores - stats[head : head + 1, :])
        probs = dot(values, gt[cols, :])
        score_grad = (weights * (probs - stats[2 + head : 3 + head, :])).astype(BF)
        value_out.append(dot(weights.astype(BF), grad[:, cols]) * latent_factor)
        key_out.append(dot(score_grad, query[:, cols]) * (scaling * latent_factor))
        total[cols, :] += dot(keys.T, score_grad)
    result = jnp.concatenate(key_out + value_out, axis=1).astype(BF)

    @pl.when(step < half)
    def _():
        own_ref[...] = result

    @pl.when(step >= half)
    def _():
        other_ref[...] = result

    @pl.when(step == last)
    def _():
        part_ref[...] = (total[...] * (scaling * prefix_factor)).astype(BF)


def attend(place, own, other, slabs, first_rows, last_rows, latents, prefix_count):
    tokens, width = own.shape
    count, _, size = slabs.shape
    columns = count * size
    ranks = first_rows.shape[0]
    rows = latents // ranks
    depth = first_rows.shape[1] - 16 - rows
    block = 256
    half = tokens // block
    kernel = functools.partial(
        attend_kernel,
        size=size,
        scaling=1.0 / math.sqrt(size),
        latent_factor=1.0 / math.sqrt(latents),
        prefix_factor=1.0 / math.sqrt(prefix_count),
    )
    return pl.pallas_call(
        kernel,
        grid=(2 * half,),
        in_specs=[
            pl.BlockSpec(memory_space=pltpu.SMEM),
            pl.BlockSpec((block, width), lambda t: (jnp.minimum(t, half - 1), 0)),
            pl.BlockSpec((block, width), lambda t: (jnp.maximum(t - half, 0), 0)),
            pl.BlockSpec(slabs.shape, lambda t: (0, 0, 0)),
            pl.BlockSpec((ranks, rows, size), lambda t: (0, depth // rows, 0)),
            pl.BlockSpec((ranks, 16, size), lambda t: (0, (depth + rows) // 16, 0)),
            pl.BlockSpec(last_rows.shape, lambda t: (0, 0, 0)),
        ],
        out_specs=[
            pl.BlockSpec((block, columns), lambda t: (jnp.minimum(t, half - 1), 0)),
            pl.BlockSpec((block, columns), lambda t: (jnp.maximum(t - half, 0), 0)),
            pl.BlockSpec((2 * size, latents), lambda t: (0, 0)),
        ],
        out_shape=[
            jax.ShapeDtypeStruct((tokens, columns), BF),
            jax.ShapeDtypeStruct((tokens, columns), BF),
            jax.ShapeDtypeStruct((2 * size, latents), BF),
        ],
        scratch_shapes=[
            pltpu.VMEM((width, columns), BF),
            pltpu.VMEM((block, columns), BF),
            pltpu.VMEM((latents, 2 * size), BF),
            pltpu.VMEM((latents, 2 * size), BF),
            pltpu.VMEM((2 * size, latents), BF),
            pltpu.VMEM((2 * size, latents), BF),
            pltpu.VMEM((8, latents), F32),
            pltpu.VMEM((4, latents), F32),
            pltpu.VMEM((2 * size, latents), F32),
        ],
        compiler_params=pltpu.CompilerParams(vmem_limit_bytes=52 * 2**20),
        cost_estimate=pl.CostEstimate(
            flops=40 * tokens * latents * size,
            bytes_accessed=6 * 2**20,
            transcendentals=4 * tokens * latents,
        ),
    )(place, own, other, slabs, first_rows, first_rows, last_rows)


def tail_kernel(place_ref, query_ref, latent_ref, every_ref, latent_out, mine_out, theirs_out):
    core = place_ref[0]
    count, rows, width = latent_out.shape
    weight = dot_nt(latent_ref[...], every_ref[...]).astype(BF)
    for one, out in enumerate((mine_out, theirs_out)):

        @pl.when(core == 0)
        def _():
            out[...] = weight[one * rows : (one + 1) * rows]

        @pl.when(core == 1)
        def _():
            out[...] = weight[(1 - one) * rows : (2 - one) * rows]

    latent = dot(query_ref[...], every_ref[...]).astype(BF)
    for i in range(count):
        half, group = divmod(i, count // 2)
        latent_out[i] = latent[half * rows : (half + 1) * rows, group * width : (group + 1) * width]


def tail(place, query, latent, every, tensors):
    both, half = query.shape
    rows = both // 2
    latents = latent.shape[1]
    return pl.pallas_call(
        tail_kernel,
        in_specs=[pl.BlockSpec(memory_space=pltpu.SMEM)]
        + [pl.BlockSpec(memory_space=pltpu.VMEM)] * 3,
        out_specs=[pl.BlockSpec(memory_space=pltpu.VMEM)] * 3,
        out_shape=[
            jax.ShapeDtypeStruct((2 * tensors, rows, latents // tensors), BF),
            jax.ShapeDtypeStruct((rows, half), BF),
            jax.ShapeDtypeStruct((rows, half), BF),
        ],
        compiler_params=pltpu.CompilerParams(vmem_limit_bytes=32 * 2**20),
        cost_estimate=pl.CostEstimate(flops=0, bytes_accessed=2**20, transcendentals=0),
    )(place, query, latent, every)


def total_kernel(part_ref, out_ref, *, factor):
    parts = [part_ref[i].astype(F32) for i in range(part_ref.shape[0])]
    out_ref[...] = sum(parts[1:], parts[0]) * factor


def total(parts, factor):
    return pl.pallas_call(
        functools.partial(total_kernel, factor=factor),
        in_specs=[pl.BlockSpec(memory_space=pltpu.VMEM)],
        out_specs=pl.BlockSpec(memory_space=pltpu.VMEM),
        out_shape=jax.ShapeDtypeStruct(parts.shape[1:], F32),
        compiler_params=pltpu.CompilerParams(vmem_limit_bytes=32 * 2**20),
        cost_estimate=pl.CostEstimate(flops=0, bytes_accessed=2**10, transcendentals=0),
    )(parts)


def exchange(x, axes):
    return lax.all_to_all(x, axes, 0, 0, tiled=True)


def halves(x):
    return jnp.transpose(x.reshape(x.shape[0], 2, x.shape[1] // 2), (1, 0, 2))


def local(
    prefix, key_weight, value_weight, query_weight, queries, out_grad, attn_out, shifted_lse, latent_in
):
    core = lax.axis_index("core")
    batch = lax.axis_index("dp")
    first = core == 0
    ranks = lax.axis_size(SEQ)
    batches = lax.axis_size("dp")
    tokens_in = prefix[0]
    token_count = tokens_in.shape[0]
    rows, columns = queries.shape[1:]
    heads = shifted_lse.shape[2]
    size = columns // heads
    latents = rows * ranks

    other_tokens = lax.ppermute(tokens_in, "core", SWAP)
    latent_own = latent_in[0].T
    query_halves = halves(query_weight)
    query_mine = jnp.where(first, query_halves[0], query_halves[1])
    query_theirs = jnp.where(first, query_halves[1], query_halves[0])
    swapped = lax.ppermute(jnp.concatenate([latent_own, query_theirs], axis=1), "core", SWAP)
    latent_other, query_other = swapped[:, :latents], swapped[:, latents:]

    def in_order(own, other):
        return jnp.where(first, jnp.concatenate([own, other], 0), jnp.concatenate([other, own], 0))

    latent_both = in_order(latent_own, latent_other)
    query_both = in_order(query_mine, query_other)

    depth = key_weight.shape[0]
    place = jnp.stack([core, batch]).astype(jnp.int32)
    mine, theirs = pack(
        place, key_weight, value_weight, queries[0], out_grad[0], attn_out[0], shifted_lse[0].T
    )
    blocks = jnp.stack([mine, lax.ppermute(theirs, "core", SWAP)])
    cut = depth + 16 + rows
    first_rows = lax.all_gather(blocks[:, :cut], Z, axis=0, tiled=True)
    slab = first_rows[:, :depth].reshape(-1, size)
    slabs = jnp.broadcast_to(slab[None], (batches,) + slab.shape)
    slabs, rest = lax.optimization_barrier((slabs, blocks[:, cut:]))
    slabs = exchange(slabs, "dp")
    last_rows = lax.all_gather(rest, Z, axis=0, tiled=True)

    own_grads, other_grads, part = attend(
        place, tokens_in, other_tokens, slabs, first_rows, last_rows, latents, token_count * ranks
    )
    theirs = lax.ppermute(other_grads, "core", SWAP)
    half = columns // 2

    def whole(lo):
        mine, other = own_grads[:, lo : lo + half], theirs[:, lo : lo + half]
        return jnp.where(
            first, jnp.concatenate([mine, other], 1), jnp.concatenate([other, mine], 1)
        )[None]

    share = exchange(part.reshape(lax.axis_size(Z), -1, latents), Z)
    share = jnp.sum(share.astype(F32), axis=0).astype(BF)
    share, key_grad, value_grad = lax.optimization_barrier((share, whole(0), whole(half)))
    every = exchange(jnp.broadcast_to(share, (lax.axis_size(Z),) + share.shape), Z).reshape(part.shape)
    latent_part, weight_mine, weight_theirs = tail(
        place, query_both, latent_both, every, lax.axis_size("tensor")
    )

    latent_sum = jnp.sum(exchange(latent_part, ("core", "tensor")).astype(F32), axis=0)
    latent_grad = latent_sum.astype(BF).T[None]

    weight_other = lax.ppermute(weight_theirs, "core", SWAP)
    weight_rows = jnp.where(
        first,
        jnp.concatenate([weight_mine, weight_other], 1),
        jnp.concatenate([weight_other, weight_mine], 1),
    )
    weight_grad = total(
        lax.all_gather(weight_rows, "dp"), 1.0 / math.sqrt(latents * batches)
    )
    return (key_grad, value_grad, latent_grad, weight_grad)


def solution(mesh):
    fine = Mesh(
        mesh.devices.reshape(4, 4, 2, *mesh.devices.shape[1:]), SEQ + tuple(mesh.axis_names[1:])
    )
    return jax.shard_map(
        local,
        mesh=fine,
        in_specs=(
            P("dp", SEQ, None),
            P(SEQ, "tensor"),
            P(SEQ, "tensor"),
            P(SEQ, "tensor"),
            P("dp", SEQ, "tensor"),
            P("dp", SEQ, "tensor"),
            P("dp", SEQ, "tensor"),
            P("dp", SEQ, "tensor"),
            P("dp", None, SEQ),
        ),
        out_specs=(
            P("dp", SEQ, "tensor"),
            P("dp", SEQ, "tensor"),
            P("dp", "tensor", SEQ),
            P(SEQ, "tensor"),
        ),
        check_vma=False,
    )
```

```python
import functools
import math

import jax
import jax.numpy as jnp
from jax import lax
from jax.experimental import pallas as pl
from jax.experimental.pallas import tpu as pltpu
from jax.sharding import Mesh, PartitionSpec as P

BF = jnp.bfloat16
F32 = jnp.float32
SEQ = ("zh", "zl", "core")
Z = ("zh", "zl")
SWAP = [(0, 1), (1, 0)]


def dot(a, b):
    return jnp.dot(a, b, preferred_element_type=F32)


def dot_nt(a, b):
    return lax.dot_general(a, b, (((1,), (1,)), ((), ())), preferred_element_type=F32)


def pack_kernel(place_ref, *refs):
    sources, outs, landing, tile, arrived = refs[:6], refs[6:8], refs[8:14], refs[14], refs[15]
    copies = [
        pltpu.make_async_copy(source, target, arrived.at[i])
        for i, (source, target) in enumerate(zip(sources, landing))
    ]
    for copy in copies:
        copy.start()
    for copy in copies:
        copy.wait()
    key_ref, value_ref, query_ref, grad_ref, out_ref, lse_ref = landing
    batch = place_ref[1]
    depth, columns = key_ref.shape
    rows = query_ref.shape[0]
    size = outs[0].shape[1]
    heads = columns // size
    half = columns // 2
    product = grad_ref[...].astype(F32) * out_ref[...].astype(F32)
    lane = lax.broadcasted_iota(jnp.int32, (rows, size), 1)
    delta = jnp.zeros((rows, size), F32)
    for head in range(heads):
        one = jnp.sum(product[:, head * size : (head + 1) * size], axis=1, keepdims=True)
        delta = jnp.where(lane == head, one, delta)
    lse, delta = lse_ref[...], delta.T[:heads]
    exact = [
        jnp.concatenate([lse[lo : lo + heads // 2], delta[lo : lo + heads // 2]], axis=0)
        for lo in (0, heads // 2)
    ]
    for other, block_ref in enumerate(outs):
        core = lax.rem(place_ref[0] + other, 2)
        column = pl.multiple_of(core * half + lax.rem(batch, 2) * size, size)
        mine = jnp.where(core == 0, exact[0], exact[1])
        high = mine.astype(BF).astype(F32)
        last = pl.ds(pl.multiple_of(core * half + half - size, size), size)
        tile[...] = grad_ref[rows - 16 :, last].astype(F32)
        for i in range(heads):
            tile[0:1, i * rows : (i + 1) * rows] = high[i : i + 1]
            tile[1:2, i * rows : (i + 1) * rows] = (mine - high)[i : i + 1]
        block_ref[depth : depth + 16] = tile[...].astype(BF)

        @pl.when(batch < 2)
        def _():
            block_ref[:depth] = key_ref[:, pl.ds(column, size)]

        @pl.when(batch >= 2)
        def _():
            block_ref[:depth] = value_ref[:, pl.ds(column, size)]

        first = depth + 16
        for ref in (query_ref, grad_ref):
            for lo in range(0, half, size):
                here = pl.ds(pl.multiple_of(core * half + lo, size), size)
                block_ref[first : first + rows] = ref[:, here]
                first += rows


def pack(place, key_weight, value_weight, query, grad, out, lse):
    depth, columns = key_weight.shape
    size = columns // lse.shape[0]
    sources = (key_weight, value_weight, query, grad, out, lse)
    return pl.pallas_call(
        pack_kernel,
        in_specs=[pl.BlockSpec(memory_space=pltpu.SMEM)]
        + [pl.BlockSpec(memory_space=pltpu.HBM)] * len(sources),
        out_specs=[pl.BlockSpec(memory_space=pltpu.VMEM)] * 2,
        out_shape=[jax.ShapeDtypeStruct((depth + 16 + 4 * query.shape[0], size), BF)] * 2,
        scratch_shapes=[pltpu.VMEM(x.shape, x.dtype) for x in sources]
        + [pltpu.VMEM((16, size), F32), pltpu.SemaphoreType.DMA((len(sources),))],
        compiler_params=pltpu.CompilerParams(vmem_limit_bytes=60 * 2**20),
        cost_estimate=pl.CostEstimate(flops=0, bytes_accessed=2**19, transcendentals=0),
    )(place, *sources)


def attend_kernel(
    place_ref, own_in, other_in, slab_ref, tile_ref, rest_ref, own_ref, other_ref, part_ref,
    weight, kv, query, grad, qt, gt, stats, total,
    size, scaling, latent_factor, prefix_factor,
):
    step = pl.program_id(0)
    last = pl.num_programs(0) - 1
    half = pl.num_programs(0) // 2
    ranks = tile_ref.shape[0]
    rows = query.shape[0] // ranks

    @pl.when(step == 0)
    def _():
        depth = weight.shape[0] // ranks
        for rank in range(ranks):
            at = rank - rank % 2 + lax.rem(rank + place_ref[0], 2)
            there = pl.ds(pl.multiple_of(at * depth, depth), depth)
            for slab in range(slab_ref.shape[0]):
                weight[rank * depth : (rank + 1) * depth, slab * size : (slab + 1) * size] = slab_ref[
                    slab, there
                ]
            here = slice(rank * rows, (rank + 1) * rows)
            query[here, :size] = rest_ref[at, :rows]
            query[here, size:] = rest_ref[at, rows : 2 * rows]
            grad[here, :size] = rest_ref[at, 2 * rows : 3 * rows]
            end = rank * rows + rows - 16
            grad[rank * rows : end, size:] = rest_ref[at, 3 * rows : 4 * rows - 16]
            grad[end : end + 16, size:] = tile_ref[at]
            grad[end : end + 2, size:] = rest_ref[at, 4 * rows - 16 :]
            tile = tile_ref[at].astype(F32)
            dense = tile[0:1] + tile[1:2]
            for i in range(4):
                stats[i : i + 1, here] = dense[:, i * rows : (i + 1) * rows]
        qt[...] = query[...].T
        gt[...] = grad[...].T
        total[...] = jnp.zeros_like(total)

    @pl.when(step < half)
    def _():
        kv[...] = dot(own_in[...], weight[...]).astype(BF)

    @pl.when(step >= half)
    def _():
        kv[...] = dot(other_in[...], weight[...]).astype(BF)

    key_out, value_out = [], []
    for head in range(2):
        cols = slice(head * size, (head + 1) * size)
        keys = kv[:, cols]
        values = kv[:, (2 + head) * size : (3 + head) * size]
        scores = dot(keys, qt[cols, :]) * scaling
        weights = jnp.exp(scores - stats[head : head + 1, :])
        probs = dot(values, gt[cols, :])
        score_grad = (weights * (probs - stats[2 + head : 3 + head, :])).astype(BF)
        value_out.append(dot(weights.astype(BF), grad[:, cols]) * latent_factor)
        key_out.append(dot(score_grad, query[:, cols]) * (scaling * latent_factor))
        total[cols, :] += dot(keys.T, score_grad)
    result = jnp.concatenate(key_out + value_out, axis=1).astype(BF)

    @pl.when(step < half)
    def _():
        own_ref[...] = result

    @pl.when(step >= half)
    def _():
        other_ref[...] = result

    @pl.when(step == last)
    def _():
        part_ref[...] = (total[...] * (scaling * prefix_factor)).astype(BF)


def attend(place, own, other, slabs, first_rows, last_rows, latents, prefix_count):
    tokens, width = own.shape
    count, _, size = slabs.shape
    columns = count * size
    ranks = first_rows.shape[0]
    rows = latents // ranks
    depth = first_rows.shape[1] - 16
    block = 256
    half = tokens // block
    kernel = functools.partial(
        attend_kernel,
        size=size,
        scaling=1.0 / math.sqrt(size),
        latent_factor=1.0 / math.sqrt(latents),
        prefix_factor=1.0 / math.sqrt(prefix_count),
    )
    return pl.pallas_call(
        kernel,
        grid=(2 * half,),
        in_specs=[
            pl.BlockSpec(memory_space=pltpu.SMEM),
            pl.BlockSpec((block, width), lambda t: (jnp.minimum(t, half - 1), 0)),
            pl.BlockSpec((block, width), lambda t: (jnp.maximum(t - half, 0), 0)),
            pl.BlockSpec(slabs.shape, lambda t: (0, 0, 0)),
            pl.BlockSpec((ranks, 16, size), lambda t: (0, depth // 16, 0)),
            pl.BlockSpec(last_rows.shape, lambda t: (0, 0, 0)),
        ],
        out_specs=[
            pl.BlockSpec((block, columns), lambda t: (jnp.minimum(t, half - 1), 0)),
            pl.BlockSpec((block, columns), lambda t: (jnp.maximum(t - half, 0), 0)),
            pl.BlockSpec((2 * size, latents), lambda t: (0, 0)),
        ],
        out_shape=[
            jax.ShapeDtypeStruct((tokens, columns), BF),
            jax.ShapeDtypeStruct((tokens, columns), BF),
            jax.ShapeDtypeStruct((2 * size, latents), BF),
        ],
        scratch_shapes=[
            pltpu.VMEM((width, columns), BF),
            pltpu.VMEM((block, columns), BF),
            pltpu.VMEM((latents, 2 * size), BF),
            pltpu.VMEM((latents, 2 * size), BF),
            pltpu.VMEM((2 * size, latents), BF),
            pltpu.VMEM((2 * size, latents), BF),
            pltpu.VMEM((4, latents), F32),
            pltpu.VMEM((2 * size, latents), F32),
        ],
        compiler_params=pltpu.CompilerParams(vmem_limit_bytes=52 * 2**20),
        cost_estimate=pl.CostEstimate(
            flops=40 * tokens * latents * size,
            bytes_accessed=6 * 2**20,
            transcendentals=4 * tokens * latents,
        ),
    )(place, own, other, slabs, first_rows, last_rows)


def tail_kernel(place_ref, query_ref, latent_ref, every_ref, latent_out, mine_out, theirs_out):
    core = place_ref[0]
    count, rows, width = latent_out.shape
    weight = dot_nt(latent_ref[...], every_ref[...]).astype(BF)
    for one, out in enumerate((mine_out, theirs_out)):

        @pl.when(core == 0)
        def _():
            out[...] = weight[one * rows : (one + 1) * rows]

        @pl.when(core == 1)
        def _():
            out[...] = weight[(1 - one) * rows : (2 - one) * rows]

    latent = dot(query_ref[...], every_ref[...]).astype(BF)
    for i in range(count):
        half, group = divmod(i, count // 2)
        latent_out[i] = latent[half * rows : (half + 1) * rows, group * width : (group + 1) * width]


def tail(place, query, latent, every, tensors):
    both, half = query.shape
    rows = both // 2
    latents = latent.shape[1]
    return pl.pallas_call(
        tail_kernel,
        in_specs=[pl.BlockSpec(memory_space=pltpu.SMEM)]
        + [pl.BlockSpec(memory_space=pltpu.VMEM)] * 3,
        out_specs=[pl.BlockSpec(memory_space=pltpu.VMEM)] * 3,
        out_shape=[
            jax.ShapeDtypeStruct((2 * tensors, rows, latents // tensors), BF),
            jax.ShapeDtypeStruct((rows, half), BF),
            jax.ShapeDtypeStruct((rows, half), BF),
        ],
        compiler_params=pltpu.CompilerParams(vmem_limit_bytes=32 * 2**20),
        cost_estimate=pl.CostEstimate(flops=0, bytes_accessed=2**20, transcendentals=0),
    )(place, query, latent, every)


def total_kernel(part_ref, out_ref, *, factor):
    parts = [part_ref[i].astype(F32) for i in range(part_ref.shape[0])]
    out_ref[...] = sum(parts[1:], parts[0]) * factor


def total(parts, factor):
    return pl.pallas_call(
        functools.partial(total_kernel, factor=factor),
        in_specs=[pl.BlockSpec(memory_space=pltpu.VMEM)],
        out_specs=pl.BlockSpec(memory_space=pltpu.VMEM),
        out_shape=jax.ShapeDtypeStruct(parts.shape[1:], F32),
        compiler_params=pltpu.CompilerParams(vmem_limit_bytes=32 * 2**20),
        cost_estimate=pl.CostEstimate(flops=0, bytes_accessed=2**10, transcendentals=0),
    )(parts)


def exchange(x, axes):
    return lax.all_to_all(x, axes, 0, 0, tiled=True)


def halves(x):
    return jnp.transpose(x.reshape(x.shape[0], 2, x.shape[1] // 2), (1, 0, 2))


def local(
    prefix, key_weight, value_weight, query_weight, queries, out_grad, attn_out, shifted_lse, latent_in
):
    core = lax.axis_index("core")
    batch = lax.axis_index("dp")
    first = core == 0
    ranks = lax.axis_size(SEQ)
    batches = lax.axis_size("dp")
    tokens_in = prefix[0]
    token_count = tokens_in.shape[0]
    rows, columns = queries.shape[1:]
    heads = shifted_lse.shape[2]
    size = columns // heads
    latents = rows * ranks

    other_tokens = lax.ppermute(tokens_in, "core", SWAP)
    latent_own = latent_in[0].T
    query_halves = halves(query_weight)
    query_mine = jnp.where(first, query_halves[0], query_halves[1])
    query_theirs = jnp.where(first, query_halves[1], query_halves[0])
    swapped = lax.ppermute(jnp.concatenate([latent_own, query_theirs], axis=1), "core", SWAP)
    latent_other, query_other = swapped[:, :latents], swapped[:, latents:]

    def in_order(own, other):
        return jnp.where(first, jnp.concatenate([own, other], 0), jnp.concatenate([other, own], 0))

    latent_both = in_order(latent_own, latent_other)
    query_both = in_order(query_mine, query_other)

    depth = key_weight.shape[0]
    place = jnp.stack([core, batch]).astype(jnp.int32)
    mine, theirs = pack(
        place, key_weight, value_weight, queries[0], out_grad[0], attn_out[0], shifted_lse[0].T
    )
    blocks = jnp.stack([mine, lax.ppermute(theirs, "core", SWAP)])
    cut = depth + 16
    ranks_z = lax.axis_size(Z)
    first_rows = exchange(jnp.broadcast_to(blocks[:, :cut], (ranks_z, 2, cut, size)), Z).reshape(ranks, cut, size)
    slab = first_rows[:, :depth].reshape(-1, size)
    slabs = jnp.broadcast_to(slab[None], (batches,) + slab.shape)
    slabs, rest = lax.optimization_barrier((slabs, blocks[:, cut : cut + 4 * rows - 14]))
    slabs = exchange(slabs, "dp")
    last_rows = lax.all_gather(rest, Z, axis=0, tiled=True)

    own_grads, other_grads, part = attend(
        place, tokens_in, other_tokens, slabs, first_rows, last_rows, latents, token_count * ranks
    )
    theirs = lax.ppermute(other_grads, "core", SWAP)
    half = columns // 2

    def whole(lo):
        mine, other = own_grads[:, lo : lo + half], theirs[:, lo : lo + half]
        return jnp.where(
            first, jnp.concatenate([mine, other], 1), jnp.concatenate([other, mine], 1)
        )[None]

    share = exchange(part.reshape(lax.axis_size(Z), -1, latents), Z)
    share = jnp.sum(share.astype(F32), axis=0).astype(BF)
    share, key_grad, value_grad = lax.optimization_barrier((share, whole(0), whole(half)))
    every = exchange(jnp.broadcast_to(share, (ranks_z,) + share.shape), Z).reshape(part.shape)
    latent_part, weight_mine, weight_theirs = tail(
        place, query_both, latent_both, every, lax.axis_size("tensor")
    )

    latent_sum = jnp.sum(exchange(latent_part, ("core", "tensor")).astype(F32), axis=0)
    latent_grad = latent_sum.astype(BF).T[None]

    weight_other = lax.ppermute(weight_theirs, "core", SWAP)
    weight_rows = jnp.where(
        first,
        jnp.concatenate([weight_mine, weight_other], 1),
        jnp.concatenate([weight_other, weight_mine], 1),
    )
    weight_grad = total(
        lax.all_gather(weight_rows, "dp"), 1.0 / math.sqrt(latents * batches)
    )
    return (key_grad, value_grad, latent_grad, weight_grad)


def solution(mesh):
    fine = Mesh(
        mesh.devices.reshape(4, 4, 2, *mesh.devices.shape[1:]), SEQ + tuple(mesh.axis_names[1:])
    )
    return jax.shard_map(
        local,
        mesh=fine,
        in_specs=(
            P("dp", SEQ, None),
            P(SEQ, "tensor"),
            P(SEQ, "tensor"),
            P(SEQ, "tensor"),
            P("dp", SEQ, "tensor"),
            P("dp", SEQ, "tensor"),
            P("dp", SEQ, "tensor"),
            P("dp", SEQ, "tensor"),
            P("dp", None, SEQ),
        ),
        out_specs=(
            P("dp", SEQ, "tensor"),
            P("dp", SEQ, "tensor"),
            P("dp", "tensor", SEQ),
            P(SEQ, "tensor"),
        ),
        check_vma=False,
    )
```

```python
import functools
import math

import jax
import jax.numpy as jnp
from jax import lax
from jax.experimental import pallas as pl
from jax.experimental.pallas import tpu as pltpu
from jax.sharding import Mesh, PartitionSpec as P

BF = jnp.bfloat16
F16 = jnp.float16
F32 = jnp.float32
SEQ = ("zh", "zl", "core")
Z = ("zh", "zl")
SWAP = [(0, 1), (1, 0)]


def dot(a, b):
    return jnp.dot(a, b, preferred_element_type=F32)


def dot_nt(a, b):
    return lax.dot_general(a, b, (((1,), (1,)), ((), ())), preferred_element_type=F32)


def power(*arrays):
    most = jnp.full((1, 1), 1e-38, F32)
    for x in arrays:
        peak = jnp.max(jnp.abs(x.astype(F32)), axis=0, keepdims=True)
        most = jnp.maximum(most, jnp.max(peak, axis=1, keepdims=True))
    return jnp.clip(13.0 - jnp.floor(jnp.log(most) * (1.0 / math.log(2.0))), -126.0, 126.0)


def scaled(x, exponent):
    return (x.astype(F32) * jnp.exp2(exponent)).astype(BF)


def pack_kernel(place_ref, *refs):
    sources, outs, landing, tile, arrived = refs[:6], refs[6:8], refs[8:14], refs[14], refs[15]
    copies = [
        pltpu.make_async_copy(source, target, arrived.at[i])
        for i, (source, target) in enumerate(zip(sources, landing))
    ]
    for copy in copies:
        copy.start()
    for copy in copies:
        copy.wait()
    key_ref, value_ref, query_ref, grad_ref, out_ref, lse_ref = landing
    batch = place_ref[1]
    depth, columns = key_ref.shape
    rows = query_ref.shape[0]
    size = outs[0].shape[1]
    heads = columns // size
    half = columns // 2
    product = grad_ref[...].astype(F32) * out_ref[...].astype(F32)
    lane = lax.broadcasted_iota(jnp.int32, (rows, size), 1)
    delta = jnp.zeros((rows, size), F32)
    for head in range(heads):
        one = jnp.sum(product[:, head * size : (head + 1) * size], axis=1, keepdims=True)
        delta = jnp.where(lane == head, one, delta)
    lse, delta = lse_ref[...], delta.T[:heads]
    weight_power = power(key_ref[...], value_ref[...])
    query_power = power(query_ref[...])
    grad_power = power(grad_ref[...])
    delta_power = power(delta)
    delta = delta * jnp.exp2(delta_power)
    exact = [
        jnp.concatenate([lse[lo : lo + heads // 2], delta[lo : lo + heads // 2]], axis=0)
        for lo in (0, heads // 2)
    ]
    for other, block_ref in enumerate(outs):
        core = lax.rem(place_ref[0] + other, 2)
        column = pl.multiple_of(core * half + lax.rem(batch, 2) * size, size)
        mine = jnp.where(core == 0, exact[0], exact[1])
        high = mine.astype(BF).astype(F32)
        tile[...] = jnp.zeros_like(tile)
        tile[:heads, :rows] = high
        tile[heads : 2 * heads, :rows] = mine - high
        for i, exponent in enumerate((weight_power, query_power, grad_power, delta_power)):
            tile[2 * heads : 2 * heads + 1, i * rows : (i + 1) * rows] = jnp.broadcast_to(exponent, (1, rows))
        block_ref[depth + 4 * rows :] = tile[...].astype(BF)

        @pl.when(batch < 2)
        def _():
            block_ref[:depth] = scaled(key_ref[:, pl.ds(column, size)], weight_power)

        @pl.when(batch >= 2)
        def _():
            block_ref[:depth] = scaled(value_ref[:, pl.ds(column, size)], weight_power)

        first = depth
        for ref, exponent in ((query_ref, query_power), (grad_ref, grad_power)):
            for lo in range(0, half, size):
                here = pl.ds(pl.multiple_of(core * half + lo, size), size)
                block_ref[first : first + rows] = scaled(ref[:, here], exponent)
                first += rows


def pack(place, key_weight, value_weight, query, grad, out, lse):
    depth, columns = key_weight.shape
    size = columns // lse.shape[0]
    sources = (key_weight, value_weight, query, grad, out, lse)
    return pl.pallas_call(
        pack_kernel,
        in_specs=[pl.BlockSpec(memory_space=pltpu.SMEM)]
        + [pl.BlockSpec(memory_space=pltpu.HBM)] * len(sources),
        out_specs=[pl.BlockSpec(memory_space=pltpu.VMEM)] * 2,
        out_shape=[jax.ShapeDtypeStruct((depth + 16 + 4 * query.shape[0], size), BF)] * 2,
        scratch_shapes=[pltpu.VMEM(x.shape, x.dtype) for x in sources]
        + [pltpu.VMEM((16, size), F32), pltpu.SemaphoreType.DMA((len(sources),))],
        compiler_params=pltpu.CompilerParams(vmem_limit_bytes=60 * 2**20),
        cost_estimate=pl.CostEstimate(flops=0, bytes_accessed=2**19, transcendentals=0),
    )(place, *sources)


def attend_kernel(
    place_ref, own_in, other_in, slab_ref, rows_ref, tile_ref, own_ref, other_ref, part_ref,
    weight, kv, query, grad, qt, gt, pieces, exponents, stats, total,
    size, scaling, latent_factor, prefix_factor,
):
    step = pl.program_id(0)
    last = pl.num_programs(0) - 1
    half = pl.num_programs(0) // 2
    ranks = tile_ref.shape[0]
    rows = query.shape[0] // ranks

    @pl.when(step == 0)
    def _():
        depth = weight.shape[0] // ranks
        for rank in range(ranks):
            at = rank - rank % 2 + lax.rem(rank + place_ref[0], 2)
            there = pl.ds(pl.multiple_of(at * depth, depth), depth)
            for slab in range(slab_ref.shape[0]):
                weight[rank * depth : (rank + 1) * depth, slab * size : (slab + 1) * size] = slab_ref[
                    slab, there
                ]
            here = slice(rank * rows, (rank + 1) * rows)
            for i, to in enumerate((query, query, grad, grad)):
                to[here, i % 2 * size : (i % 2 + 1) * size] = rows_ref[at, i * rows : (i + 1) * rows]
            pieces[:, here] = tile_ref[at, :8, :rows]
            exponents[:, here] = tile_ref[at, 8:, 3 * rows : 4 * rows]
        stats[...] = pieces[:4] + pieces[4:]
        stats[2:] = stats[2:] * jnp.exp2(-exponents[:1])
        qt[...] = query[...].T
        gt[...] = grad[...].T
        total[...] = jnp.zeros_like(total)

    @pl.when(step < half)
    def _():
        kv[...] = dot(own_in[...], weight[...]).astype(BF)

    @pl.when(step >= half)
    def _():
        kv[...] = dot(other_in[...], weight[...]).astype(BF)

    key_out, value_out = [], []
    for head in range(2):
        cols = slice(head * size, (head + 1) * size)
        keys = kv[:, cols]
        values = kv[:, (2 + head) * size : (3 + head) * size]
        scores = dot(keys, qt[cols, :]) * scaling
        weights = jnp.exp(scores - stats[head : head + 1, :])
        probs = dot(values, gt[cols, :])
        score_grad = (weights * (probs - stats[2 + head : 3 + head, :])).astype(BF)
        value_out.append(dot(weights.astype(BF), grad[:, cols]) * latent_factor)
        key_out.append(dot(score_grad, query[:, cols]) * (scaling * latent_factor))
        total[cols, :] += dot(keys.T, score_grad)
    result = jnp.concatenate(key_out + value_out, axis=1).astype(BF)

    @pl.when(step < half)
    def _():
        own_ref[...] = result

    @pl.when(step >= half)
    def _():
        other_ref[...] = result

    @pl.when(step == last)
    def _():
        part_ref[...] = (total[...] * (scaling * prefix_factor)).astype(BF)


def attend(place, own, other, slabs, rows_all, tiles, latents, prefix_count):
    tokens, width = own.shape
    count, _, size = slabs.shape
    columns = count * size
    block = 256
    half = tokens // block
    kernel = functools.partial(
        attend_kernel,
        size=size,
        scaling=1.0 / math.sqrt(size),
        latent_factor=1.0 / math.sqrt(latents),
        prefix_factor=1.0 / math.sqrt(prefix_count),
    )
    return pl.pallas_call(
        kernel,
        grid=(2 * half,),
        in_specs=[
            pl.BlockSpec(memory_space=pltpu.SMEM),
            pl.BlockSpec((block, width), lambda t: (jnp.minimum(t, half - 1), 0)),
            pl.BlockSpec((block, width), lambda t: (jnp.maximum(t - half, 0), 0)),
            pl.BlockSpec(slabs.shape, lambda t: (0, 0, 0)),
            pl.BlockSpec(rows_all.shape, lambda t: (0, 0, 0)),
            pl.BlockSpec(tiles.shape, lambda t: (0, 0, 0)),
        ],
        out_specs=[
            pl.BlockSpec((block, columns), lambda t: (jnp.minimum(t, half - 1), 0)),
            pl.BlockSpec((block, columns), lambda t: (jnp.maximum(t - half, 0), 0)),
            pl.BlockSpec((2 * size, latents), lambda t: (0, 0)),
        ],
        out_shape=[
            jax.ShapeDtypeStruct((tokens, columns), BF),
            jax.ShapeDtypeStruct((tokens, columns), BF),
            jax.ShapeDtypeStruct((2 * size, latents), BF),
        ],
        scratch_shapes=[
            pltpu.VMEM((width, columns), BF),
            pltpu.VMEM((block, columns), BF),
            pltpu.VMEM((latents, 2 * size), BF),
            pltpu.VMEM((latents, 2 * size), BF),
            pltpu.VMEM((2 * size, latents), BF),
            pltpu.VMEM((2 * size, latents), BF),
            pltpu.VMEM((8, latents), F32),
            pltpu.VMEM((8, latents), F32),
            pltpu.VMEM((4, latents), F32),
            pltpu.VMEM((2 * size, latents), F32),
        ],
        compiler_params=pltpu.CompilerParams(vmem_limit_bytes=52 * 2**20),
        cost_estimate=pl.CostEstimate(
            flops=40 * tokens * latents * size,
            bytes_accessed=6 * 2**20,
            transcendentals=4 * tokens * latents,
        ),
    )(place, own, other, slabs, rows_all, tiles)


def tail_kernel(place_ref, query_ref, latent_ref, every_ref, latent_out, mine_out, theirs_out):
    core = place_ref[0]
    count, rows, width = latent_out.shape
    weight = dot_nt(latent_ref[...], every_ref[...]).astype(BF)
    for one, out in enumerate((mine_out, theirs_out)):

        @pl.when(core == 0)
        def _():
            out[...] = weight[one * rows : (one + 1) * rows]

        @pl.when(core == 1)
        def _():
            out[...] = weight[(1 - one) * rows : (2 - one) * rows]

    latent = dot(query_ref[...], every_ref[...]).astype(BF)
    for i in range(count):
        half, group = divmod(i, count // 2)
        latent_out[i] = latent[half * rows : (half + 1) * rows, group * width : (group + 1) * width]


def tail(place, query, latent, every, tensors):
    both, half = query.shape
    rows = both // 2
    latents = latent.shape[1]
    return pl.pallas_call(
        tail_kernel,
        in_specs=[pl.BlockSpec(memory_space=pltpu.SMEM)]
        + [pl.BlockSpec(memory_space=pltpu.VMEM)] * 3,
        out_specs=[pl.BlockSpec(memory_space=pltpu.VMEM)] * 3,
        out_shape=[
            jax.ShapeDtypeStruct((2 * tensors, rows, latents // tensors), BF),
            jax.ShapeDtypeStruct((rows, half), BF),
            jax.ShapeDtypeStruct((rows, half), BF),
        ],
        compiler_params=pltpu.CompilerParams(vmem_limit_bytes=32 * 2**20),
        cost_estimate=pl.CostEstimate(flops=0, bytes_accessed=2**20, transcendentals=0),
    )(place, query, latent, every)


def total_kernel(part_ref, out_ref, *, factor):
    parts = [part_ref[i].astype(F32) for i in range(part_ref.shape[0])]
    out_ref[...] = sum(parts[1:], parts[0]) * factor


def total(parts, factor):
    return pl.pallas_call(
        functools.partial(total_kernel, factor=factor),
        in_specs=[pl.BlockSpec(memory_space=pltpu.VMEM)],
        out_specs=pl.BlockSpec(memory_space=pltpu.VMEM),
        out_shape=jax.ShapeDtypeStruct(parts.shape[1:], F32),
        compiler_params=pltpu.CompilerParams(vmem_limit_bytes=32 * 2**20),
        cost_estimate=pl.CostEstimate(flops=0, bytes_accessed=2**10, transcendentals=0),
    )(parts)


def exchange(x, axes):
    return lax.all_to_all(x, axes, 0, 0, tiled=True)


def halves(x):
    return jnp.transpose(x.reshape(x.shape[0], 2, x.shape[1] // 2), (1, 0, 2))


def local(
    prefix, key_weight, value_weight, query_weight, queries, out_grad, attn_out, shifted_lse, latent_in
):
    core = lax.axis_index("core")
    batch = lax.axis_index("dp")
    first = core == 0
    ranks = lax.axis_size(SEQ)
    batches = lax.axis_size("dp")
    tokens_in = prefix[0]
    token_count = tokens_in.shape[0]
    rows, columns = queries.shape[1:]
    heads = shifted_lse.shape[2]
    size = columns // heads
    latents = rows * ranks

    other_tokens = lax.ppermute(tokens_in, "core", SWAP)
    latent_own = latent_in[0].T
    query_halves = halves(query_weight)
    query_mine = jnp.where(first, query_halves[0], query_halves[1])
    query_theirs = jnp.where(first, query_halves[1], query_halves[0])
    swapped = lax.ppermute(jnp.concatenate([latent_own, query_theirs], axis=1), "core", SWAP)
    latent_other, query_other = swapped[:, :latents], swapped[:, latents:]

    def in_order(own, other):
        return jnp.where(first, jnp.concatenate([own, other], 0), jnp.concatenate([other, own], 0))

    latent_both = in_order(latent_own, latent_other)
    query_both = in_order(query_mine, query_other)

    depth = key_weight.shape[0]
    place = jnp.stack([core, batch]).astype(jnp.int32)
    mine, theirs = pack(
        place, key_weight, value_weight, queries[0], out_grad[0], attn_out[0], shifted_lse[0].T
    )
    blocks = jnp.stack([mine, lax.ppermute(theirs, "core", SWAP)])
    gathered = lax.all_gather(blocks.astype(F16), Z, axis=0, tiled=True)
    slabs = lax.all_gather(gathered[:, :depth], "dp")
    tiles = gathered[:, -16:].astype(F32)
    back = jnp.exp2(-tiles[:, 8, :])
    slabs = (slabs.astype(F32) * back[None, :, :1, None]).astype(BF).reshape(batches, -1, size)
    rows_back = jnp.repeat(back[:, rows : 3 * rows : rows], 2 * rows, axis=1)
    rows_all = (gathered[:, depth:-16].astype(F32) * rows_back[:, :, None]).astype(BF)

    own_grads, other_grads, part = attend(
        place, tokens_in, other_tokens, slabs, rows_all, tiles, latents, token_count * ranks
    )
    theirs = lax.ppermute(other_grads, "core", SWAP)
    half = columns // 2

    def whole(lo):
        mine, other = own_grads[:, lo : lo + half], theirs[:, lo : lo + half]
        return jnp.where(
            first, jnp.concatenate([mine, other], 1), jnp.concatenate([other, mine], 1)
        )[None]

    share = exchange(part.reshape(lax.axis_size(Z), -1, latents), Z)
    share = jnp.sum(share.astype(F32), axis=0).astype(BF)
    share, key_grad, value_grad = lax.optimization_barrier((share, whole(0), whole(half)))
    every = exchange(jnp.broadcast_to(share, (lax.axis_size(Z),) + share.shape), Z).reshape(part.shape)
    latent_part, weight_mine, weight_theirs = tail(
        place, query_both, latent_both, every, lax.axis_size("tensor")
    )

    latent_sum = jnp.sum(exchange(latent_part, ("core", "tensor")).astype(F32), axis=0)
    latent_grad = latent_sum.astype(BF).T[None]

    weight_other = lax.ppermute(weight_theirs, "core", SWAP)
    weight_rows = jnp.where(
        first,
        jnp.concatenate([weight_mine, weight_other], 1),
        jnp.concatenate([weight_other, weight_mine], 1),
    )
    weight_grad = total(
        lax.all_gather(weight_rows, "dp"), 1.0 / math.sqrt(latents * batches)
    )
    return (key_grad, value_grad, latent_grad, weight_grad)


def solution(mesh):
    fine = Mesh(
        mesh.devices.reshape(4, 4, 2, *mesh.devices.shape[1:]), SEQ + tuple(mesh.axis_names[1:])
    )
    return jax.shard_map(
        local,
        mesh=fine,
        in_specs=(
            P("dp", SEQ, None),
            P(SEQ, "tensor"),
            P(SEQ, "tensor"),
            P(SEQ, "tensor"),
            P("dp", SEQ, "tensor"),
            P("dp", SEQ, "tensor"),
            P("dp", SEQ, "tensor"),
            P("dp", SEQ, "tensor"),
            P("dp", None, SEQ),
        ),
        out_specs=(
            P("dp", SEQ, "tensor"),
            P("dp", SEQ, "tensor"),
            P("dp", "tensor", SEQ),
            P(SEQ, "tensor"),
        ),
        check_vma=False,
    )
```

```python
import functools
import math

import jax
import jax.numpy as jnp
from jax import lax
from jax.experimental import pallas as pl
from jax.experimental.pallas import tpu as pltpu
from jax.sharding import Mesh, PartitionSpec as P

BF = jnp.bfloat16
F16 = jnp.float16
F32 = jnp.float32
SEQ = ("zh", "zl", "core")
Z = ("zh", "zl")
SWAP = [(0, 1), (1, 0)]


def dot(a, b):
    return jnp.dot(a, b, preferred_element_type=F32)


def dot_nt(a, b):
    return lax.dot_general(a, b, (((1,), (1,)), ((), ())), preferred_element_type=F32)


def power(*arrays):
    most = jnp.full((1, 1), 1e-38, F32)
    for x in arrays:
        peak = jnp.max(jnp.abs(x.astype(F32)), axis=0, keepdims=True)
        most = jnp.maximum(most, jnp.max(peak, axis=1, keepdims=True))
    return jnp.clip(13.0 - jnp.floor(jnp.log(most) * (1.0 / math.log(2.0))), -126.0, 126.0)


def scaled(x, exponent):
    return (x.astype(F32) * jnp.exp2(exponent)).astype(BF)


def pack_kernel(place_ref, *refs):
    sources, outs, landing, tile, arrived = refs[:6], refs[6:8], refs[8:14], refs[14], refs[15]
    copies = [
        pltpu.make_async_copy(source, target, arrived.at[i])
        for i, (source, target) in enumerate(zip(sources, landing))
    ]
    for copy in copies:
        copy.start()
    for copy in copies:
        copy.wait()
    key_ref, value_ref, query_ref, grad_ref, out_ref, lse_ref = landing
    batch = lax.div(place_ref[0], 2)
    depth, columns = key_ref.shape
    rows = query_ref.shape[0]
    size = outs[0].shape[1]
    heads = columns // size
    half = columns // 2
    product = grad_ref[...].astype(F32) * out_ref[...].astype(F32)
    lane = lax.broadcasted_iota(jnp.int32, (rows, size), 1)
    delta = jnp.zeros((rows, size), F32)
    for head in range(heads):
        one = jnp.sum(product[:, head * size : (head + 1) * size], axis=1, keepdims=True)
        delta = jnp.where(lane == head, one, delta)
    lse, delta = lse_ref[...], delta.T[:heads]
    weight_power = power(key_ref[...], value_ref[...])
    query_power = power(query_ref[...])
    grad_power = power(grad_ref[...])
    delta_power = power(delta)
    delta = delta * jnp.exp2(delta_power)
    exact = [
        jnp.concatenate([lse[lo : lo + heads // 2], delta[lo : lo + heads // 2]], axis=0)
        for lo in (0, heads // 2)
    ]
    for other, block_ref in enumerate(outs):
        core = lax.rem(lax.rem(place_ref[0], 2) + other, 2)
        column = pl.multiple_of(core * half + lax.rem(batch, 2) * size, size)
        mine = jnp.where(core == 0, exact[0], exact[1])
        high = mine.astype(BF).astype(F32)
        tile[...] = jnp.zeros_like(tile)
        tile[:heads, :rows] = high
        tile[heads : 2 * heads, :rows] = mine - high
        for i, exponent in enumerate((weight_power, query_power, grad_power, delta_power)):
            tile[2 * heads : 2 * heads + 1, i * rows : (i + 1) * rows] = jnp.broadcast_to(exponent, (1, rows))
        block_ref[depth + 4 * rows :] = tile[...].astype(BF)

        @pl.when(batch < 2)
        def _():
            block_ref[:depth] = scaled(key_ref[:, pl.ds(column, size)], weight_power)

        @pl.when(batch >= 2)
        def _():
            block_ref[:depth] = scaled(value_ref[:, pl.ds(column, size)], weight_power)

        first = depth
        for ref, exponent in ((query_ref, query_power), (grad_ref, grad_power)):
            for lo in range(0, half, size):
                here = pl.ds(pl.multiple_of(core * half + lo, size), size)
                block_ref[first : first + rows] = scaled(ref[:, here], exponent)
                first += rows


def pack(place, key_weight, value_weight, query, grad, out, lse):
    depth, columns = key_weight.shape
    size = columns // lse.shape[0]
    sources = (key_weight, value_weight, query, grad, out, lse)
    return pl.pallas_call(
        pack_kernel,
        in_specs=[pl.BlockSpec(memory_space=pltpu.SMEM)]
        + [pl.BlockSpec(memory_space=pltpu.HBM)] * len(sources),
        out_specs=[pl.BlockSpec(memory_space=pltpu.VMEM)] * 2,
        out_shape=[jax.ShapeDtypeStruct((depth + 16 + 4 * query.shape[0], size), BF)] * 2,
        scratch_shapes=[pltpu.VMEM(x.shape, x.dtype) for x in sources]
        + [pltpu.VMEM((16, size), F32), pltpu.SemaphoreType.DMA((len(sources),))],
        compiler_params=pltpu.CompilerParams(vmem_limit_bytes=60 * 2**20),
        cost_estimate=pl.CostEstimate(flops=0, bytes_accessed=2**19, transcendentals=0),
    )(place, *sources)


def attend_kernel(
    place_ref, own_in, other_in, slab_ref, rows_ref, tile_ref, own_ref, other_ref, part_ref,
    weight, kv, query, grad, qt, gt, pieces, exponents, stats, total,
    size, scaling, latent_factor, prefix_factor,
):
    step = pl.program_id(0)
    last = pl.num_programs(0) - 1
    half = pl.num_programs(0) // 2
    ranks = tile_ref.shape[0]
    rows = query.shape[0] // ranks

    @pl.when(step == 0)
    def _():
        depth = weight.shape[0] // ranks
        for rank in range(ranks):
            at = rank - rank % 2 + lax.rem(rank + lax.rem(place_ref[0], 2), 2)
            there = pl.ds(pl.multiple_of(at * depth, depth), depth)
            for slab in range(slab_ref.shape[0]):
                weight[rank * depth : (rank + 1) * depth, slab * size : (slab + 1) * size] = slab_ref[
                    slab, there
                ]
            here = slice(rank * rows, (rank + 1) * rows)
            for i, to in enumerate((query, query, grad, grad)):
                to[here, i % 2 * size : (i % 2 + 1) * size] = rows_ref[at, i * rows : (i + 1) * rows]
            pieces[:, here] = tile_ref[at, :8, :rows]
            exponents[:, here] = tile_ref[at, 8:, 3 * rows : 4 * rows]
        stats[...] = pieces[:4] + pieces[4:]
        stats[2:] = stats[2:] * jnp.exp2(-exponents[:1])
        qt[...] = query[...].T
        gt[...] = grad[...].T
        total[...] = jnp.zeros_like(total)

    @pl.when(step < half)
    def _():
        kv[...] = dot(own_in[...], weight[...]).astype(BF)

    @pl.when(step >= half)
    def _():
        kv[...] = dot(other_in[...], weight[...]).astype(BF)

    key_out, value_out = [], []
    for head in range(2):
        cols = slice(head * size, (head + 1) * size)
        keys = kv[:, cols]
        values = kv[:, (2 + head) * size : (3 + head) * size]
        scores = dot(keys, qt[cols, :]) * scaling
        weights = jnp.exp(scores - stats[head : head + 1, :])
        probs = dot(values, gt[cols, :])
        score_grad = (weights * (probs - stats[2 + head : 3 + head, :])).astype(BF)
        value_out.append(dot(weights.astype(BF), grad[:, cols]) * latent_factor)
        key_out.append(dot(score_grad, query[:, cols]) * (scaling * latent_factor))
        total[cols, :] += dot(keys.T, score_grad)
    result = jnp.concatenate(key_out + value_out, axis=1).astype(BF)

    @pl.when(step < half)
    def _():
        own_ref[...] = result

    @pl.when(step >= half)
    def _():
        other_ref[...] = result

    @pl.when(step == last)
    def _():
        part_ref[...] = (total[...] * (scaling * prefix_factor)).astype(BF)


def attend(place, own, other, slabs, rows_all, tiles, latents, prefix_count):
    tokens, width = own.shape
    count, _, size = slabs.shape
    columns = count * size
    block = 256
    half = tokens // block
    kernel = functools.partial(
        attend_kernel,
        size=size,
        scaling=1.0 / math.sqrt(size),
        latent_factor=1.0 / math.sqrt(latents),
        prefix_factor=1.0 / math.sqrt(prefix_count),
    )
    return pl.pallas_call(
        kernel,
        grid=(2 * half,),
        in_specs=[
            pl.BlockSpec(memory_space=pltpu.SMEM),
            pl.BlockSpec((block, width), lambda t: (jnp.minimum(t, half - 1), 0)),
            pl.BlockSpec((block, width), lambda t: (jnp.maximum(t - half, 0), 0)),
            pl.BlockSpec(slabs.shape, lambda t: (0, 0, 0)),
            pl.BlockSpec(rows_all.shape, lambda t: (0, 0, 0)),
            pl.BlockSpec(tiles.shape, lambda t: (0, 0, 0)),
        ],
        out_specs=[
            pl.BlockSpec((block, columns), lambda t: (jnp.minimum(t, half - 1), 0)),
            pl.BlockSpec((block, columns), lambda t: (jnp.maximum(t - half, 0), 0)),
            pl.BlockSpec((2 * size, latents), lambda t: (0, 0)),
        ],
        out_shape=[
            jax.ShapeDtypeStruct((tokens, columns), BF),
            jax.ShapeDtypeStruct((tokens, columns), BF),
            jax.ShapeDtypeStruct((2 * size, latents), BF),
        ],
        scratch_shapes=[
            pltpu.VMEM((width, columns), BF),
            pltpu.VMEM((block, columns), BF),
            pltpu.VMEM((latents, 2 * size), BF),
            pltpu.VMEM((latents, 2 * size), BF),
            pltpu.VMEM((2 * size, latents), BF),
            pltpu.VMEM((2 * size, latents), BF),
            pltpu.VMEM((8, latents), F32),
            pltpu.VMEM((8, latents), F32),
            pltpu.VMEM((4, latents), F32),
            pltpu.VMEM((2 * size, latents), F32),
        ],
        compiler_params=pltpu.CompilerParams(vmem_limit_bytes=49 * 2**20),
        cost_estimate=pl.CostEstimate(
            flops=40 * tokens * latents * size,
            bytes_accessed=6 * 2**20,
            transcendentals=4 * tokens * latents,
        ),
    )(place, own, other, slabs, rows_all, tiles)


def tail_kernel(place_ref, query_ref, latent_ref, every_ref, latent_out, mine_out, theirs_out):
    core = lax.rem(place_ref[0], 2)
    count, rows, width = latent_out.shape
    weight = dot_nt(latent_ref[...], every_ref[...]).astype(BF)
    for one, out in enumerate((mine_out, theirs_out)):

        @pl.when(core == 0)
        def _():
            out[...] = weight[one * rows : (one + 1) * rows]

        @pl.when(core == 1)
        def _():
            out[...] = weight[(1 - one) * rows : (2 - one) * rows]

    latent = dot(query_ref[...], every_ref[...]).astype(BF)
    for i in range(count):
        half, group = divmod(i, count // 2)
        latent_out[i] = latent[half * rows : (half + 1) * rows, group * width : (group + 1) * width]


def tail(place, query, latent, every, tensors):
    both, half = query.shape
    rows = both // 2
    latents = latent.shape[1]
    return pl.pallas_call(
        tail_kernel,
        in_specs=[pl.BlockSpec(memory_space=pltpu.SMEM)]
        + [pl.BlockSpec(memory_space=pltpu.VMEM)] * 3,
        out_specs=[pl.BlockSpec(memory_space=pltpu.VMEM)] * 3,
        out_shape=[
            jax.ShapeDtypeStruct((2 * tensors, rows, latents // tensors), BF),
            jax.ShapeDtypeStruct((rows, half), BF),
            jax.ShapeDtypeStruct((rows, half), BF),
        ],
        compiler_params=pltpu.CompilerParams(vmem_limit_bytes=32 * 2**20),
        cost_estimate=pl.CostEstimate(flops=0, bytes_accessed=2**20, transcendentals=0),
    )(place, query, latent, every)


def total_kernel(part_ref, out_ref, *, factor):
    parts = [part_ref[i].astype(F32) for i in range(part_ref.shape[0])]
    out_ref[...] = sum(parts[1:], parts[0]) * factor


def total(parts, factor):
    return pl.pallas_call(
        functools.partial(total_kernel, factor=factor),
        in_specs=[pl.BlockSpec(memory_space=pltpu.VMEM)],
        out_specs=pl.BlockSpec(memory_space=pltpu.VMEM),
        out_shape=jax.ShapeDtypeStruct(parts.shape[1:], F32),
        compiler_params=pltpu.CompilerParams(vmem_limit_bytes=32 * 2**20),
        cost_estimate=pl.CostEstimate(flops=0, bytes_accessed=2**10, transcendentals=0),
    )(parts)


def exchange(x, axes):
    return lax.all_to_all(x, axes, 0, 0, tiled=True)


def halves(x):
    return jnp.transpose(x.reshape(x.shape[0], 2, x.shape[1] // 2), (1, 0, 2))


def local(
    prefix, key_weight, value_weight, query_weight, queries, out_grad, attn_out, shifted_lse, latent_in
):
    core = lax.axis_index("core")
    batch = lax.axis_index("dp")
    first = core == 0
    ranks = lax.axis_size(SEQ)
    batches = lax.axis_size("dp")
    tokens_in = prefix[0]
    token_count = tokens_in.shape[0]
    rows, columns = queries.shape[1:]
    heads = shifted_lse.shape[2]
    size = columns // heads
    latents = rows * ranks

    other_tokens = lax.ppermute(tokens_in, "core", SWAP)
    latent_own = latent_in[0].T
    query_halves = halves(query_weight)
    query_mine = jnp.where(first, query_halves[0], query_halves[1])
    query_theirs = jnp.where(first, query_halves[1], query_halves[0])
    swapped = lax.ppermute(jnp.concatenate([latent_own, query_theirs], axis=1), "core", SWAP)
    latent_other, query_other = swapped[:, :latents], swapped[:, latents:]

    def in_order(own, other):
        return jnp.where(first, jnp.concatenate([own, other], 0), jnp.concatenate([other, own], 0))

    latent_both = in_order(latent_own, latent_other)
    query_both = in_order(query_mine, query_other)

    depth = key_weight.shape[0]
    place = jnp.reshape(core + 2 * batch, (1,)).astype(jnp.int32)
    mine, theirs = pack(
        place, key_weight, value_weight, queries[0], out_grad[0], attn_out[0], shifted_lse[0].T
    )
    blocks = jnp.stack([mine, lax.ppermute(theirs, "core", SWAP)])
    gathered = lax.all_gather(blocks.astype(F16), Z, axis=0, tiled=True)
    slabs = lax.all_gather(gathered[:, :depth], "dp")
    tiles = gathered[:, -16:].astype(F32)
    back = jnp.exp2(-tiles[:, 8, :])
    slabs = (slabs.astype(F32) * back[None, :, :1, None]).astype(BF).reshape(batches, -1, size)
    rows_back = jnp.repeat(back[:, rows : 3 * rows : rows], 2 * rows, axis=1)
    rows_all = (gathered[:, depth:-16].astype(F32) * rows_back[:, :, None]).astype(BF)

    own_grads, other_grads, part = attend(
        place, tokens_in, other_tokens, slabs, rows_all, tiles, latents, token_count * ranks
    )
    theirs = lax.ppermute(other_grads, "core", SWAP)
    half = columns // 2

    def whole(lo):
        mine, other = own_grads[:, lo : lo + half], theirs[:, lo : lo + half]
        return jnp.where(
            first, jnp.concatenate([mine, other], 1), jnp.concatenate([other, mine], 1)
        )[None]

    share = exchange(part.reshape(lax.axis_size(Z), -1, latents), Z)
    share = jnp.sum(share.astype(F32), axis=0).astype(BF)
    share, key_grad, value_grad, latent_both, query_both = lax.optimization_barrier(
        (share, whole(0), whole(half), latent_both, query_both)
    )
    every = exchange(jnp.broadcast_to(share, (lax.axis_size(Z),) + share.shape), Z).reshape(part.shape)
    latent_part, weight_mine, weight_theirs = tail(
        place, query_both, latent_both, every, lax.axis_size("tensor")
    )

    latent_sum = jnp.sum(exchange(latent_part, ("core", "tensor")).astype(F32), axis=0)
    latent_grad = latent_sum.astype(BF).T[None]

    weight_other = lax.ppermute(weight_theirs, "core", SWAP)
    weight_rows = jnp.where(
        first,
        jnp.concatenate([weight_mine, weight_other], 1),
        jnp.concatenate([weight_other, weight_mine], 1),
    )
    weight_grad = total(
        lax.all_gather(weight_rows, "dp"), 1.0 / math.sqrt(latents * batches)
    )
    return (key_grad, value_grad, latent_grad, weight_grad)


def solution(mesh):
    fine = Mesh(
        mesh.devices.reshape(4, 4, 2, *mesh.devices.shape[1:]), SEQ + tuple(mesh.axis_names[1:])
    )
    return jax.shard_map(
        local,
        mesh=fine,
        in_specs=(
            P("dp", SEQ, None),
            P(SEQ, "tensor"),
            P(SEQ, "tensor"),
            P(SEQ, "tensor"),
            P("dp", SEQ, "tensor"),
            P("dp", SEQ, "tensor"),
            P("dp", SEQ, "tensor"),
            P("dp", SEQ, "tensor"),
            P("dp", None, SEQ),
        ),
        out_specs=(
            P("dp", SEQ, "tensor"),
            P("dp", SEQ, "tensor"),
            P("dp", "tensor", SEQ),
            P(SEQ, "tensor"),
        ),
        check_vma=False,
    )
```

```python
import functools
import math

import jax
import jax.numpy as jnp
from jax import lax
from jax.experimental import pallas as pl
from jax.experimental.pallas import tpu as pltpu
from jax.sharding import Mesh, PartitionSpec as P

BF = jnp.bfloat16
F16 = jnp.float16
F32 = jnp.float32
SEQ = ("zh", "zl", "core")
Z = ("zh", "zl")
SWAP = [(0, 1), (1, 0)]


def dot(a, b):
    return jnp.dot(a, b, preferred_element_type=F32)


def dot_nt(a, b):
    return lax.dot_general(a, b, (((1,), (1,)), ((), ())), preferred_element_type=F32)


def power(*arrays):
    most = jnp.full((1, 1), 1e-38, F32)
    for x in arrays:
        peak = jnp.max(jnp.abs(x.astype(F32)), axis=0, keepdims=True)
        most = jnp.maximum(most, jnp.max(peak, axis=1, keepdims=True))
    return jnp.clip(13.0 - jnp.floor(jnp.log(most) * (1.0 / math.log(2.0))), -126.0, 126.0)


def scaled(x, exponent):
    return (x.astype(F32) * jnp.exp2(exponent)).astype(BF)


def pack_kernel(place_ref, *refs):
    sources, outs, landing, tile, arrived = refs[:6], refs[6:8], refs[8:14], refs[14], refs[15]
    copies = [
        pltpu.make_async_copy(source, target, arrived.at[i])
        for i, (source, target) in enumerate(zip(sources, landing))
    ]
    for copy in copies:
        copy.start()
    for copy in copies:
        copy.wait()
    key_ref, value_ref, query_ref, grad_ref, out_ref, lse_ref = landing
    batch = lax.div(place_ref[0], 2)
    depth, columns = key_ref.shape
    rows = query_ref.shape[0]
    size = outs[0].shape[1]
    heads = columns // size
    half = columns // 2
    product = grad_ref[...].astype(F32) * out_ref[...].astype(F32)
    lane = lax.broadcasted_iota(jnp.int32, (rows, size), 1)
    delta = jnp.zeros((rows, size), F32)
    for head in range(heads):
        one = jnp.sum(product[:, head * size : (head + 1) * size], axis=1, keepdims=True)
        delta = jnp.where(lane == head, one, delta)
    lse, delta = lse_ref[...], delta.T[:heads]
    weight_power = power(key_ref[...], value_ref[...])
    query_power = power(query_ref[...])
    grad_power = power(grad_ref[...])
    delta_power = power(delta)
    delta = delta * jnp.exp2(delta_power)
    exact = [
        jnp.concatenate([lse[lo : lo + heads // 2], delta[lo : lo + heads // 2]], axis=0)
        for lo in (0, heads // 2)
    ]
    for other, block_ref in enumerate(outs):
        core = lax.rem(lax.rem(place_ref[0], 2) + other, 2)
        column = pl.multiple_of(core * half + lax.rem(batch, 2) * size, size)
        mine = jnp.where(core == 0, exact[0], exact[1])
        high = mine.astype(BF).astype(F32)
        tile[...] = jnp.zeros_like(tile)
        tile[:heads, :rows] = high
        tile[heads : 2 * heads, :rows] = mine - high
        for i, exponent in enumerate((weight_power, query_power, grad_power, delta_power)):
            tile[2 * heads : 2 * heads + 1, i * rows : (i + 1) * rows] = jnp.broadcast_to(exponent, (1, rows))
        block_ref[depth + 4 * rows :] = tile[...].astype(BF)

        @pl.when(batch < 2)
        def _():
            block_ref[:depth] = scaled(key_ref[:, pl.ds(column, size)], weight_power)

        @pl.when(batch >= 2)
        def _():
            block_ref[:depth] = scaled(value_ref[:, pl.ds(column, size)], weight_power)

        first = depth
        for ref, exponent in ((query_ref, query_power), (grad_ref, grad_power)):
            for lo in range(0, half, size):
                here = pl.ds(pl.multiple_of(core * half + lo, size), size)
                block_ref[first : first + rows] = scaled(ref[:, here], exponent)
                first += rows


def pack(place, key_weight, value_weight, query, grad, out, lse):
    depth, columns = key_weight.shape
    size = columns // lse.shape[0]
    sources = (key_weight, value_weight, query, grad, out, lse)
    return pl.pallas_call(
        pack_kernel,
        in_specs=[pl.BlockSpec(memory_space=pltpu.SMEM)]
        + [pl.BlockSpec(memory_space=pltpu.HBM)] * len(sources),
        out_specs=[pl.BlockSpec(memory_space=pltpu.VMEM)] * 2,
        out_shape=[jax.ShapeDtypeStruct((depth + 16 + 4 * query.shape[0], size), BF)] * 2,
        scratch_shapes=[pltpu.VMEM(x.shape, x.dtype) for x in sources]
        + [pltpu.VMEM((16, size), F32), pltpu.SemaphoreType.DMA((len(sources),))],
        compiler_params=pltpu.CompilerParams(vmem_limit_bytes=60 * 2**20),
        cost_estimate=pl.CostEstimate(flops=0, bytes_accessed=2**19, transcendentals=0),
    )(place, *sources)


def attend_kernel(
    place_ref, own_in, other_in, slab_ref, rows_ref, tile_ref, own_ref, other_ref, part_ref,
    weight, kv, query, grad, qt, gt, pieces, exponents, stats, total,
    size, scaling, latent_factor, prefix_factor,
):
    step = pl.program_id(0)
    last = pl.num_programs(0) - 1
    half = pl.num_programs(0) // 2
    ranks = tile_ref.shape[0]
    rows = query.shape[0] // ranks

    @pl.when(step == 0)
    def _():
        depth = weight.shape[0] // ranks
        for rank in range(ranks):
            at = rank - rank % 2 + lax.rem(rank + lax.rem(place_ref[0], 2), 2)
            there = pl.ds(pl.multiple_of(at * depth, depth), depth)
            for slab in range(slab_ref.shape[0]):
                weight[rank * depth : (rank + 1) * depth, slab * size : (slab + 1) * size] = slab_ref[
                    slab, there
                ]
            here = slice(rank * rows, (rank + 1) * rows)
            for i, to in enumerate((query, query, grad, grad)):
                to[here, i % 2 * size : (i % 2 + 1) * size] = rows_ref[at, i * rows : (i + 1) * rows]
            pieces[:, here] = tile_ref[at, :8, :rows]
            exponents[:, here] = tile_ref[at, 8:, 3 * rows : 4 * rows]
        stats[...] = pieces[:4] + pieces[4:]
        stats[2:] = stats[2:] * jnp.exp2(-exponents[:1])
        qt[...] = query[...].T
        gt[...] = grad[...].T
        total[...] = jnp.zeros_like(total)

    @pl.when(step < half)
    def _():
        kv[...] = dot(own_in[...], weight[...]).astype(BF)

    @pl.when(step >= half)
    def _():
        kv[...] = dot(other_in[...], weight[...]).astype(BF)

    key_out, value_out = [], []
    for head in range(2):
        cols = slice(head * size, (head + 1) * size)
        keys = kv[:, cols]
        values = kv[:, (2 + head) * size : (3 + head) * size]
        scores = dot(keys, qt[cols, :]) * scaling
        weights = jnp.exp(scores - stats[head : head + 1, :])
        probs = dot(values, gt[cols, :])
        score_grad = (weights * (probs - stats[2 + head : 3 + head, :])).astype(BF)
        value_out.append(dot(weights.astype(BF), grad[:, cols]) * latent_factor)
        key_out.append(dot(score_grad, query[:, cols]) * (scaling * latent_factor))
        total[cols, :] += dot(keys.T, score_grad)
    result = jnp.concatenate(key_out + value_out, axis=1).astype(BF)

    @pl.when(step < half)
    def _():
        own_ref[...] = result

    @pl.when(step >= half)
    def _():
        other_ref[...] = result

    @pl.when(step == last)
    def _():
        part_ref[...] = (total[...] * (scaling * prefix_factor)).astype(BF)


def attend(place, own, other, slabs, rows_all, tiles, latents, prefix_count):
    tokens, width = own.shape
    count, _, size = slabs.shape
    columns = count * size
    block = 512
    half = tokens // block
    kernel = functools.partial(
        attend_kernel,
        size=size,
        scaling=1.0 / math.sqrt(size),
        latent_factor=1.0 / math.sqrt(latents),
        prefix_factor=1.0 / math.sqrt(prefix_count),
    )
    return pl.pallas_call(
        kernel,
        grid=(2 * half,),
        in_specs=[
            pl.BlockSpec(memory_space=pltpu.SMEM),
            pl.BlockSpec((block, width), lambda t: (jnp.minimum(t, half - 1), 0)),
            pl.BlockSpec((block, width), lambda t: (jnp.maximum(t - half, 0), 0)),
            pl.BlockSpec(slabs.shape, lambda t: (0, 0, 0)),
            pl.BlockSpec(rows_all.shape, lambda t: (0, 0, 0)),
            pl.BlockSpec(tiles.shape, lambda t: (0, 0, 0)),
        ],
        out_specs=[
            pl.BlockSpec((block, columns), lambda t: (jnp.minimum(t, half - 1), 0)),
            pl.BlockSpec((block, columns), lambda t: (jnp.maximum(t - half, 0), 0)),
            pl.BlockSpec((2 * size, latents), lambda t: (0, 0)),
        ],
        out_shape=[
            jax.ShapeDtypeStruct((tokens, columns), BF),
            jax.ShapeDtypeStruct((tokens, columns), BF),
            jax.ShapeDtypeStruct((2 * size, latents), BF),
        ],
        scratch_shapes=[
            pltpu.VMEM((width, columns), BF),
            pltpu.VMEM((block, columns), BF),
            pltpu.VMEM((latents, 2 * size), BF),
            pltpu.VMEM((latents, 2 * size), BF),
            pltpu.VMEM((2 * size, latents), BF),
            pltpu.VMEM((2 * size, latents), BF),
            pltpu.VMEM((8, latents), F32),
            pltpu.VMEM((8, latents), F32),
            pltpu.VMEM((4, latents), F32),
            pltpu.VMEM((2 * size, latents), F32),
        ],
        compiler_params=pltpu.CompilerParams(vmem_limit_bytes=49 * 2**20),
        cost_estimate=pl.CostEstimate(
            flops=40 * tokens * latents * size,
            bytes_accessed=6 * 2**20,
            transcendentals=4 * tokens * latents,
        ),
    )(place, own, other, slabs, rows_all, tiles)


def tail_kernel(place_ref, query_ref, latent_ref, every_ref, latent_out, mine_out, theirs_out):
    core = lax.rem(place_ref[0], 2)
    count, rows, width = latent_out.shape
    weight = dot_nt(latent_ref[...], every_ref[...]).astype(BF)
    for one, out in enumerate((mine_out, theirs_out)):

        @pl.when(core == 0)
        def _():
            out[...] = weight[one * rows : (one + 1) * rows]

        @pl.when(core == 1)
        def _():
            out[...] = weight[(1 - one) * rows : (2 - one) * rows]

    latent = dot(query_ref[...], every_ref[...]).astype(BF)
    for i in range(count):
        half, group = divmod(i, count // 2)
        latent_out[i] = latent[half * rows : (half + 1) * rows, group * width : (group + 1) * width]


def tail(place, query, latent, every, tensors):
    both, half = query.shape
    rows = both // 2
    latents = latent.shape[1]
    return pl.pallas_call(
        tail_kernel,
        in_specs=[pl.BlockSpec(memory_space=pltpu.SMEM)]
        + [pl.BlockSpec(memory_space=pltpu.VMEM)] * 3,
        out_specs=[pl.BlockSpec(memory_space=pltpu.VMEM)] * 3,
        out_shape=[
            jax.ShapeDtypeStruct((2 * tensors, rows, latents // tensors), BF),
            jax.ShapeDtypeStruct((rows, half), BF),
            jax.ShapeDtypeStruct((rows, half), BF),
        ],
        compiler_params=pltpu.CompilerParams(vmem_limit_bytes=32 * 2**20),
        cost_estimate=pl.CostEstimate(flops=0, bytes_accessed=2**20, transcendentals=0),
    )(place, query, latent, every)


def total_kernel(part_ref, out_ref, *, factor):
    parts = [part_ref[i].astype(F32) for i in range(part_ref.shape[0])]
    out_ref[...] = sum(parts[1:], parts[0]) * factor


def total(parts, factor):
    return pl.pallas_call(
        functools.partial(total_kernel, factor=factor),
        in_specs=[pl.BlockSpec(memory_space=pltpu.VMEM)],
        out_specs=pl.BlockSpec(memory_space=pltpu.VMEM),
        out_shape=jax.ShapeDtypeStruct(parts.shape[1:], F32),
        compiler_params=pltpu.CompilerParams(vmem_limit_bytes=32 * 2**20),
        cost_estimate=pl.CostEstimate(flops=0, bytes_accessed=2**10, transcendentals=0),
    )(parts)


def exchange(x, axes):
    return lax.all_to_all(x, axes, 0, 0, tiled=True)


def halves(x):
    return jnp.transpose(x.reshape(x.shape[0], 2, x.shape[1] // 2), (1, 0, 2))


def local(
    prefix, key_weight, value_weight, query_weight, queries, out_grad, attn_out, shifted_lse, latent_in
):
    core = lax.axis_index("core")
    batch = lax.axis_index("dp")
    first = core == 0
    ranks = lax.axis_size(SEQ)
    batches = lax.axis_size("dp")
    tokens_in = prefix[0]
    token_count = tokens_in.shape[0]
    rows, columns = queries.shape[1:]
    heads = shifted_lse.shape[2]
    size = columns // heads
    latents = rows * ranks

    other_tokens = lax.ppermute(tokens_in, "core", SWAP)
    latent_own = latent_in[0].T
    query_halves = halves(query_weight)
    query_mine = jnp.where(first, query_halves[0], query_halves[1])
    query_theirs = jnp.where(first, query_halves[1], query_halves[0])
    swapped = lax.ppermute(jnp.concatenate([latent_own, query_theirs], axis=1), "core", SWAP)
    latent_other, query_other = swapped[:, :latents], swapped[:, latents:]

    def in_order(own, other):
        return jnp.where(first, jnp.concatenate([own, other], 0), jnp.concatenate([other, own], 0))

    latent_both = in_order(latent_own, latent_other)
    query_both = in_order(query_mine, query_other)

    depth = key_weight.shape[0]
    place = jnp.reshape(core + 2 * batch, (1,)).astype(jnp.int32)
    mine, theirs = pack(
        place, key_weight, value_weight, queries[0], out_grad[0], attn_out[0], shifted_lse[0].T
    )
    blocks = jnp.stack([mine, lax.ppermute(theirs, "core", SWAP)])
    gathered = lax.all_gather(blocks.astype(F16), Z, axis=0, tiled=True)
    slabs = lax.all_gather(gathered[:, :depth], "dp")
    tiles = gathered[:, -16:].astype(F32)
    back = jnp.exp2(-tiles[:, 8, :])
    slabs = (slabs.astype(F32) * back[None, :, :1, None]).astype(BF).reshape(batches, -1, size)
    rows_back = jnp.repeat(back[:, rows : 3 * rows : rows], 2 * rows, axis=1)
    rows_all = (gathered[:, depth:-16].astype(F32) * rows_back[:, :, None]).astype(BF)

    own_grads, other_grads, part = attend(
        place, tokens_in, other_tokens, slabs, rows_all, tiles, latents, token_count * ranks
    )
    theirs = lax.ppermute(other_grads, "core", SWAP)
    half = columns // 2

    def whole(lo):
        mine, other = own_grads[:, lo : lo + half], theirs[:, lo : lo + half]
        return jnp.where(
            first, jnp.concatenate([mine, other], 1), jnp.concatenate([other, mine], 1)
        )[None]

    share = exchange(part.reshape(lax.axis_size(Z), -1, latents), Z)
    share = jnp.sum(share.astype(F32), axis=0).astype(BF)
    share, key_grad, value_grad, latent_both, query_both = lax.optimization_barrier(
        (share, whole(0), whole(half), latent_both, query_both)
    )
    every = exchange(jnp.broadcast_to(share, (lax.axis_size(Z),) + share.shape), Z).reshape(part.shape)
    latent_part, weight_mine, weight_theirs = tail(
        place, query_both, latent_both, every, lax.axis_size("tensor")
    )

    latent_sum = jnp.sum(exchange(latent_part, ("core", "tensor")).astype(F32), axis=0)
    latent_grad = latent_sum.astype(BF).T[None]

    weight_other = lax.ppermute(weight_theirs, "core", SWAP)
    weight_rows = jnp.where(
        first,
        jnp.concatenate([weight_mine, weight_other], 1),
        jnp.concatenate([weight_other, weight_mine], 1),
    )
    weight_grad = total(
        lax.all_gather(weight_rows, "dp"), 1.0 / math.sqrt(latents * batches)
    )
    return (key_grad, value_grad, latent_grad, weight_grad)


def solution(mesh):
    fine = Mesh(
        mesh.devices.reshape(4, 4, 2, *mesh.devices.shape[1:]), SEQ + tuple(mesh.axis_names[1:])
    )
    return jax.shard_map(
        local,
        mesh=fine,
        in_specs=(
            P("dp", SEQ, None),
            P(SEQ, "tensor"),
            P(SEQ, "tensor"),
            P(SEQ, "tensor"),
            P("dp", SEQ, "tensor"),
            P("dp", SEQ, "tensor"),
            P("dp", SEQ, "tensor"),
            P("dp", SEQ, "tensor"),
            P("dp", None, SEQ),
        ),
        out_specs=(
            P("dp", SEQ, "tensor"),
            P("dp", SEQ, "tensor"),
            P("dp", "tensor", SEQ),
            P(SEQ, "tensor"),
        ),
        check_vma=False,
    )
```

```python
import functools
import math

import jax
import jax.numpy as jnp
from jax import lax
from jax.experimental import pallas as pl
from jax.experimental.pallas import tpu as pltpu
from jax.sharding import Mesh, PartitionSpec as P

BF = jnp.bfloat16
F16 = jnp.float16
F32 = jnp.float32
SEQ = ("zh", "zl", "core")
Z = ("zh", "zl")
SWAP = [(0, 1), (1, 0)]
LOG2E = 1.0 / math.log(2.0)


def dot(a, b):
    return jnp.dot(a, b, preferred_element_type=F32)


def dot_nt(a, b):
    return lax.dot_general(a, b, (((1,), (1,)), ((), ())), preferred_element_type=F32)


def power(*arrays):
    most = jnp.full((1, 1), 1e-38, F32)
    for x in arrays:
        peak = jnp.max(jnp.abs(x.astype(F32)), axis=0, keepdims=True)
        most = jnp.maximum(most, jnp.max(peak, axis=1, keepdims=True))
    return jnp.clip(13.0 - jnp.floor(jnp.log(most) * (1.0 / math.log(2.0))), -126.0, 126.0)


def scaled(x, exponent):
    return (x.astype(F32) * jnp.exp2(exponent)).astype(BF)


def pack_kernel(place_ref, *refs):
    sources, outs, landing, tile, arrived = refs[:6], refs[6:8], refs[8:14], refs[14], refs[15]
    copies = [
        pltpu.make_async_copy(source, target, arrived.at[i])
        for i, (source, target) in enumerate(zip(sources, landing))
    ]
    for copy in copies:
        copy.start()
    for copy in copies:
        copy.wait()
    key_ref, value_ref, query_ref, grad_ref, out_ref, lse_ref = landing
    batch = lax.div(place_ref[0], 2)
    depth, columns = key_ref.shape
    rows = query_ref.shape[0]
    size = outs[0].shape[1]
    heads = columns // size
    half = columns // 2
    product = grad_ref[...].astype(F32) * out_ref[...].astype(F32)
    lane = lax.broadcasted_iota(jnp.int32, (rows, size), 1)
    delta = jnp.zeros((rows, size), F32)
    for head in range(heads):
        one = jnp.sum(product[:, head * size : (head + 1) * size], axis=1, keepdims=True)
        delta = jnp.where(lane == head, one, delta)
    lse, delta = lse_ref[...], delta.T[:heads]
    weight_power = power(key_ref[...], value_ref[...])
    query_power = power(query_ref[...])
    grad_power = power(grad_ref[...])
    delta_power = power(delta)
    delta = delta * jnp.exp2(delta_power)
    exact = [
        jnp.concatenate([lse[lo : lo + heads // 2], delta[lo : lo + heads // 2]], axis=0)
        for lo in (0, heads // 2)
    ]
    for other, block_ref in enumerate(outs):
        core = lax.rem(lax.rem(place_ref[0], 2) + other, 2)
        column = pl.multiple_of(core * half + lax.rem(batch, 2) * size, size)
        mine = jnp.where(core == 0, exact[0], exact[1])
        high = mine.astype(BF).astype(F32)
        tile[...] = jnp.zeros_like(tile)
        tile[:heads, :rows] = high
        tile[heads : 2 * heads, :rows] = mine - high
        for i, exponent in enumerate((weight_power, query_power, grad_power, delta_power)):
            tile[2 * heads : 2 * heads + 1, i * rows : (i + 1) * rows] = jnp.broadcast_to(exponent, (1, rows))
        block_ref[depth + 4 * rows :] = tile[...].astype(BF)

        @pl.when(batch < 2)
        def _():
            block_ref[:depth] = scaled(key_ref[:, pl.ds(column, size)], weight_power)

        @pl.when(batch >= 2)
        def _():
            block_ref[:depth] = scaled(value_ref[:, pl.ds(column, size)], weight_power)

        first = depth
        for ref, exponent in ((query_ref, query_power), (grad_ref, grad_power)):
            for lo in range(0, half, size):
                here = pl.ds(pl.multiple_of(core * half + lo, size), size)
                block_ref[first : first + rows] = scaled(ref[:, here], exponent)
                first += rows


def pack(place, key_weight, value_weight, query, grad, out, lse):
    depth, columns = key_weight.shape
    size = columns // lse.shape[0]
    sources = (key_weight, value_weight, query, grad, out, lse)
    return pl.pallas_call(
        pack_kernel,
        in_specs=[pl.BlockSpec(memory_space=pltpu.SMEM)]
        + [pl.BlockSpec(memory_space=pltpu.HBM)] * len(sources),
        out_specs=[pl.BlockSpec(memory_space=pltpu.VMEM)] * 2,
        out_shape=[jax.ShapeDtypeStruct((depth + 16 + 4 * query.shape[0], size), BF)] * 2,
        scratch_shapes=[pltpu.VMEM(x.shape, x.dtype) for x in sources]
        + [pltpu.VMEM((16, size), F32), pltpu.SemaphoreType.DMA((len(sources),))],
        compiler_params=pltpu.CompilerParams(vmem_limit_bytes=60 * 2**20),
        cost_estimate=pl.CostEstimate(flops=0, bytes_accessed=2**19, transcendentals=0),
    )(place, *sources)


def attend_kernel(
    place_ref, own_in, other_in, slab_ref, rows_ref, tile_ref, own_ref, other_ref, part_ref,
    weight, kv, query, grad, qt, gt, pieces, exponents, stats, total,
    size, scaling, latent_factor, prefix_factor,
):
    step = pl.program_id(0)
    last = pl.num_programs(0) - 1
    half = pl.num_programs(0) // 2
    ranks = tile_ref.shape[0]
    rows = query.shape[0] // ranks

    @pl.when(step == 0)
    def _():
        depth = weight.shape[0] // ranks
        for rank in range(ranks):
            at = rank - rank % 2 + lax.rem(rank + lax.rem(place_ref[0], 2), 2)
            there = pl.ds(pl.multiple_of(at * depth, depth), depth)
            for slab in range(slab_ref.shape[0]):
                weight[rank * depth : (rank + 1) * depth, slab * size : (slab + 1) * size] = slab_ref[
                    slab, there
                ]
            here = slice(rank * rows, (rank + 1) * rows)
            for i, to in enumerate((query, query, grad, grad)):
                to[here, i % 2 * size : (i % 2 + 1) * size] = rows_ref[at, i * rows : (i + 1) * rows]
            pieces[:, here] = tile_ref[at, :8, :rows]
            exponents[:, here] = tile_ref[at, 8:, 3 * rows : 4 * rows]
        stats[...] = pieces[:4] + pieces[4:]
        stats[2:] = stats[2:] * jnp.exp2(-exponents[:1])
        stats[:2] = stats[:2] * LOG2E
        qt[...] = query[...].T
        gt[...] = grad[...].T
        total[...] = jnp.zeros_like(total)

    @pl.when(step < half)
    def _():
        kv[...] = dot(own_in[...], weight[...]).astype(BF)

    @pl.when(step >= half)
    def _():
        kv[...] = dot(other_in[...], weight[...]).astype(BF)

    key_out, value_out = [], []
    for head in range(2):
        cols = slice(head * size, (head + 1) * size)
        keys = kv[:, cols]
        values = kv[:, (2 + head) * size : (3 + head) * size]
        scores = dot(keys, qt[cols, :]) * (scaling * LOG2E)
        weights = jnp.exp2(scores - stats[head : head + 1, :])
        probs = dot(values, gt[cols, :])
        score_grad = (weights * (probs - stats[2 + head : 3 + head, :])).astype(BF)
        value_out.append(dot(weights.astype(BF), grad[:, cols]) * latent_factor)
        key_out.append(dot(score_grad, query[:, cols]) * (scaling * latent_factor))
        total[cols, :] += dot(keys.T, score_grad)
    result = jnp.concatenate(key_out + value_out, axis=1).astype(BF)

    @pl.when(step < half)
    def _():
        own_ref[...] = result

    @pl.when(step >= half)
    def _():
        other_ref[...] = result

    @pl.when(step == last)
    def _():
        part_ref[...] = (total[...] * (scaling * prefix_factor)).astype(BF)


def attend(place, own, other, slabs, rows_all, tiles, latents, prefix_count):
    tokens, width = own.shape
    count, _, size = slabs.shape
    columns = count * size
    block = 512
    half = tokens // block
    kernel = functools.partial(
        attend_kernel,
        size=size,
        scaling=1.0 / math.sqrt(size),
        latent_factor=1.0 / math.sqrt(latents),
        prefix_factor=1.0 / math.sqrt(prefix_count),
    )
    return pl.pallas_call(
        kernel,
        grid=(2 * half,),
        in_specs=[
            pl.BlockSpec(memory_space=pltpu.SMEM),
            pl.BlockSpec((block, width), lambda t: (jnp.minimum(t, half - 1), 0)),
            pl.BlockSpec((block, width), lambda t: (jnp.maximum(t - half, 0), 0)),
            pl.BlockSpec(slabs.shape, lambda t: (0, 0, 0)),
            pl.BlockSpec(rows_all.shape, lambda t: (0, 0, 0)),
            pl.BlockSpec(tiles.shape, lambda t: (0, 0, 0)),
        ],
        out_specs=[
            pl.BlockSpec((block, columns), lambda t: (jnp.minimum(t, half - 1), 0)),
            pl.BlockSpec((block, columns), lambda t: (jnp.maximum(t - half, 0), 0)),
            pl.BlockSpec((2 * size, latents), lambda t: (0, 0)),
        ],
        out_shape=[
            jax.ShapeDtypeStruct((tokens, columns), BF),
            jax.ShapeDtypeStruct((tokens, columns), BF),
            jax.ShapeDtypeStruct((2 * size, latents), BF),
        ],
        scratch_shapes=[
            pltpu.VMEM((width, columns), BF),
            pltpu.VMEM((block, columns), BF),
            pltpu.VMEM((latents, 2 * size), BF),
            pltpu.VMEM((latents, 2 * size), BF),
            pltpu.VMEM((2 * size, latents), BF),
            pltpu.VMEM((2 * size, latents), BF),
            pltpu.VMEM((8, latents), F32),
            pltpu.VMEM((8, latents), F32),
            pltpu.VMEM((4, latents), F32),
            pltpu.VMEM((2 * size, latents), F32),
        ],
        compiler_params=pltpu.CompilerParams(vmem_limit_bytes=49 * 2**20),
        cost_estimate=pl.CostEstimate(
            flops=40 * tokens * latents * size,
            bytes_accessed=6 * 2**20,
            transcendentals=4 * tokens * latents,
        ),
    )(place, own, other, slabs, rows_all, tiles)


def tail_kernel(place_ref, query_ref, latent_ref, every_ref, latent_out, mine_out, theirs_out):
    core = lax.rem(place_ref[0], 2)
    count, rows, width = latent_out.shape
    weight = dot_nt(latent_ref[...], every_ref[...]).astype(BF)
    for one, out in enumerate((mine_out, theirs_out)):

        @pl.when(core == 0)
        def _():
            out[...] = weight[one * rows : (one + 1) * rows]

        @pl.when(core == 1)
        def _():
            out[...] = weight[(1 - one) * rows : (2 - one) * rows]

    latent = dot(query_ref[...], every_ref[...]).astype(BF)
    for i in range(count):
        half, group = divmod(i, count // 2)
        latent_out[i] = latent[half * rows : (half + 1) * rows, group * width : (group + 1) * width]


def tail(place, query, latent, every, tensors):
    both, half = query.shape
    rows = both // 2
    latents = latent.shape[1]
    return pl.pallas_call(
        tail_kernel,
        in_specs=[pl.BlockSpec(memory_space=pltpu.SMEM)]
        + [pl.BlockSpec(memory_space=pltpu.VMEM)] * 3,
        out_specs=[pl.BlockSpec(memory_space=pltpu.VMEM)] * 3,
        out_shape=[
            jax.ShapeDtypeStruct((2 * tensors, rows, latents // tensors), BF),
            jax.ShapeDtypeStruct((rows, half), BF),
            jax.ShapeDtypeStruct((rows, half), BF),
        ],
        compiler_params=pltpu.CompilerParams(vmem_limit_bytes=32 * 2**20),
        cost_estimate=pl.CostEstimate(flops=0, bytes_accessed=2**20, transcendentals=0),
    )(place, query, latent, every)


def total_kernel(part_ref, out_ref, *, factor):
    parts = [part_ref[i].astype(F32) for i in range(part_ref.shape[0])]
    out_ref[...] = sum(parts[1:], parts[0]) * factor


def total(parts, factor):
    return pl.pallas_call(
        functools.partial(total_kernel, factor=factor),
        in_specs=[pl.BlockSpec(memory_space=pltpu.VMEM)],
        out_specs=pl.BlockSpec(memory_space=pltpu.VMEM),
        out_shape=jax.ShapeDtypeStruct(parts.shape[1:], F32),
        compiler_params=pltpu.CompilerParams(vmem_limit_bytes=32 * 2**20),
        cost_estimate=pl.CostEstimate(flops=0, bytes_accessed=2**10, transcendentals=0),
    )(parts)


def exchange(x, axes):
    return lax.all_to_all(x, axes, 0, 0, tiled=True)


def halves(x):
    return jnp.transpose(x.reshape(x.shape[0], 2, x.shape[1] // 2), (1, 0, 2))


def local(
    prefix, key_weight, value_weight, query_weight, queries, out_grad, attn_out, shifted_lse, latent_in
):
    core = lax.axis_index("core")
    batch = lax.axis_index("dp")
    first = core == 0
    ranks = lax.axis_size(SEQ)
    batches = lax.axis_size("dp")
    tokens_in = prefix[0]
    token_count = tokens_in.shape[0]
    rows, columns = queries.shape[1:]
    heads = shifted_lse.shape[2]
    size = columns // heads
    latents = rows * ranks

    other_tokens = lax.ppermute(tokens_in, "core", SWAP)
    latent_own = latent_in[0].T
    query_halves = halves(query_weight)
    query_mine = jnp.where(first, query_halves[0], query_halves[1])
    query_theirs = jnp.where(first, query_halves[1], query_halves[0])
    swapped = lax.ppermute(jnp.concatenate([latent_own, query_theirs], axis=1), "core", SWAP)
    latent_other, query_other = swapped[:, :latents], swapped[:, latents:]

    def in_order(own, other):
        return jnp.where(first, jnp.concatenate([own, other], 0), jnp.concatenate([other, own], 0))

    latent_both = in_order(latent_own, latent_other)
    query_both = in_order(query_mine, query_other)

    depth = key_weight.shape[0]
    place = jnp.reshape(core + 2 * batch, (1,)).astype(jnp.int32)
    mine, theirs = pack(
        place, key_weight, value_weight, queries[0], out_grad[0], attn_out[0], shifted_lse[0].T
    )
    blocks = jnp.stack([mine, lax.ppermute(theirs, "core", SWAP)])
    gathered = lax.all_gather(blocks.astype(F16), Z, axis=0, tiled=True)
    slabs = lax.all_gather(gathered[:, :depth], "dp")
    tiles = gathered[:, -16:].astype(F32)
    back = jnp.exp2(-tiles[:, 8, :])
    slabs = (slabs.astype(F32) * back[None, :, :1, None]).astype(BF).reshape(batches, -1, size)
    rows_back = jnp.repeat(back[:, rows : 3 * rows : rows], 2 * rows, axis=1)
    rows_all = (gathered[:, depth:-16].astype(F32) * rows_back[:, :, None]).astype(BF)

    own_grads, other_grads, part = attend(
        place, tokens_in, other_tokens, slabs, rows_all, tiles, latents, token_count * ranks
    )
    theirs = lax.ppermute(other_grads, "core", SWAP)
    half = columns // 2

    def whole(lo):
        mine, other = own_grads[:, lo : lo + half], theirs[:, lo : lo + half]
        return jnp.where(
            first, jnp.concatenate([mine, other], 1), jnp.concatenate([other, mine], 1)
        )[None]

    share = exchange(part.reshape(lax.axis_size(Z), -1, latents), Z)
    share = jnp.sum(share.astype(F32), axis=0).astype(BF)
    share, key_grad, value_grad, latent_both, query_both = lax.optimization_barrier(
        (share, whole(0), whole(half), latent_both, query_both)
    )
    every = exchange(jnp.broadcast_to(share, (lax.axis_size(Z),) + share.shape), Z).reshape(part.shape)
    latent_part, weight_mine, weight_theirs = tail(
        place, query_both, latent_both, every, lax.axis_size("tensor")
    )

    latent_sum = jnp.sum(exchange(latent_part, ("core", "tensor")).astype(F32), axis=0)
    latent_grad = latent_sum.astype(BF).T[None]

    weight_other = lax.ppermute(weight_theirs, "core", SWAP)
    weight_rows = jnp.where(
        first,
        jnp.concatenate([weight_mine, weight_other], 1),
        jnp.concatenate([weight_other, weight_mine], 1),
    )
    weight_grad = total(
        lax.all_gather(weight_rows, "dp"), 1.0 / math.sqrt(latents * batches)
    )
    return (key_grad, value_grad, latent_grad, weight_grad)


def solution(mesh):
    fine = Mesh(
        mesh.devices.reshape(4, 4, 2, *mesh.devices.shape[1:]), SEQ + tuple(mesh.axis_names[1:])
    )
    return jax.shard_map(
        local,
        mesh=fine,
        in_specs=(
            P("dp", SEQ, None),
            P(SEQ, "tensor"),
            P(SEQ, "tensor"),
            P(SEQ, "tensor"),
            P("dp", SEQ, "tensor"),
            P("dp", SEQ, "tensor"),
            P("dp", SEQ, "tensor"),
            P("dp", SEQ, "tensor"),
            P("dp", None, SEQ),
        ),
        out_specs=(
            P("dp", SEQ, "tensor"),
            P("dp", SEQ, "tensor"),
            P("dp", "tensor", SEQ),
            P(SEQ, "tensor"),
        ),
        check_vma=False,
    )
```
